32 devices in a mesh: dp: 16 (over z, y, core), mp: 2 (over x).
Axes of the slice: x: 2, y: 2, z: 4, core: 2. Of those that a mesh axis runs over, the one named last changes fastest.
Arguments:
- frames: bfloat16 [32, 320, 768], P('dp', None, 'mp'), may hold values from -16 to 16
- segment_ids: int32 [32, 320], P('dp'), may hold values from 0 to 4, as said below
- live: int32 [32, 320], P('dp'), may hold values from 0 to 1, as said below
- conv_weight: bfloat16 [6144, 768], P('dp', 'mp'), may hold values from -0.078125 to 0.078125
- qkv_weight: bfloat16 [768, 3, 768], P('dp', None, 'mp'), may hold values from -0.3125 to 0.3125
- out_weight: bfloat16 [768, 768], P('mp', 'dp'), may hold values from -0.875 to 0.875
- up_weight: bfloat16 [768, 3072], P('dp', 'mp'), may hold values from -0.21875 to 0.21875
- down_weight: bfloat16 [3072, 768], P('mp', 'dp'), may hold values from -0.109375 to 0.109375
- up_bias: float32 [3072], P('mp'), may hold values from -3 to 3
- gains: float32 [3, 768], P(None, 'mp'), may hold values from 0.1 to 1.9
- biases: float32 [8, 768], P(None, 'mp'), may hold values from -3 to 3
- out_grad: bfloat16 [32, 320, 768], P('dp', None, 'mp'), may hold values from -6 to 6
Outputs:
- mixed: bfloat16 [32, 320, 768], P('dp', None, 'mp')
- grad_frames: float32 [32, 320, 768], P('dp', None, 'mp')
- grad_conv: float32 [6144, 768], P('dp', 'mp')
- grad_qkv: float32 [768, 3, 768], P('dp', None, 'mp')
- grad_out: float32 [768, 768], P('mp', 'dp')
- grad_up: float32 [768, 3072], P('dp', 'mp')
- grad_down: float32 [3072, 768], P('mp', 'dp')
- grad_up_bias: float32 [3072], P('mp')
- grad_gains: float32 [3, 768], P(None, 'mp')
- grad_biases: float32 [8, 768], P(None, 'mp')
The draws below stay inside these ranges and needn't reach their ends.
Inputs may be any that keep to these rules, and one draw needn't show every extreme that they name: `segment_ids`: along each row the ids start at 0 and never fall; a row holds 2 to 4 clips, each with its own id; padding frames, at the row's end, take the id after the last clip's. `live`: 1 exactly on the frames of clips, 0 on the padding at a row's end.
All inputs are finite; a program needn't handle non-finite values.
Results may differ from the reference program's by a relative error of at most 0.02.
Values may be sent and summed in bfloat16 or wider, within the bound.
A program may use at most 192 MiB of HBM per device.

```python
import jax
import jax.numpy as jnp
from jax import lax

D = 768
HEADS = 12
HEAD_DIM = 64
FF = 3072
KERNEL = 128
GROUPS = 16
FRAMES = 320
ROWS = 32
KC = 6144


def clip_layout(key):
    base_key = jax.random.fold_in(key, 11)
    key_count, key_length, key_shift = jax.random.split(base_key, 3)
    counts = jax.random.randint(key_count, (ROWS,), 2, 5)
    lengths = jax.random.randint(key_length, (ROWS,), FRAMES // 2, FRAMES + 1)
    first_row = jnp.arange(ROWS) == 0
    counts = jnp.where(first_row, 4, counts)
    lengths = jnp.where(first_row, jnp.minimum(lengths, FRAMES - 1), lengths)
    jitter_span = lengths // (4 * counts)
    raw_bits = jax.random.randint(key_shift, (ROWS, 3), 0, 1 << 20)
    offsets = raw_bits % (2 * jitter_span[:, None] + 1) - jitter_span[:, None]
    cut_order = jnp.arange(1, 4)
    cut_points = cut_order[None, :] * lengths[:, None] // counts[:, None] + offsets
    cut_points = jnp.where(cut_order[None, :] < counts[:, None], cut_points, FRAMES + 1)
    positions = jnp.arange(FRAMES)
    clip_ids = jnp.sum((positions[None, :, None] >= cut_points[:, None, :]).astype(jnp.int32), axis=-1)
    clip_ids = clip_ids + (positions[None, :] >= lengths[:, None]).astype(jnp.int32)
    alive_mask = (positions[None, :] < lengths[:, None]).astype(jnp.int32)
    return (clip_ids.astype(jnp.int32), alive_mask)


def draw_segment_ids(key, part):
    return clip_layout(key)[0]


def draw_live(key, part):
    return clip_layout(key)[1]


def draw_frames(key, part):
    key_base, key_channel = jax.random.split(jax.random.fold_in(key, 5), 2)
    rising = jnp.exp(jnp.linspace(jnp.log(0.5), jnp.log(1.5), D))
    channel_scale = rising * jnp.exp(jax.random.uniform(key_channel, (D,), jnp.float32, -0.35, 0.35))
    values = jnp.clip(jax.random.normal(key_base, (ROWS, FRAMES, D), jnp.float32), -4.0, 4.0) * channel_scale
    return values.astype(jnp.bfloat16)


def level_of(stream_key, dims, cuts, low, top_value):
    def one(axis_at, shards_of):
        steps = jax.random.uniform(jax.random.fold_in(jax.random.fold_in(stream_key, 6), axis_at), (shards_of,), jnp.float32, low / len(cuts), top_value / len(cuts))
        return jnp.repeat(jnp.exp(steps), dims[axis_at] // shards_of).reshape((-1,) + (1,) * (len(dims) - axis_at - 1))

    gain = one(*cuts[0])
    for cut in cuts[1:]:
        gain = gain * one(*cut)
    return gain


def scatter_about(stream_key, dims, width, reach, shards=(), held_as=jnp.bfloat16):
    values = width * jax.random.normal(stream_key, dims, jnp.float32)
    if shards:
        values = values * level_of(stream_key, dims, shards, -0.22, 0.18)
    return jnp.clip(values, -reach, reach).astype(held_as)


def setup_inputs(seed: int = 0) -> dict:
    splits = jax.random.split(jax.random.key(seed), 13)
    return {
        "frames": draw_frames(jax.random.fold_in(splits[12], 71), 0),
        "segment_ids": draw_segment_ids(jax.random.fold_in(splits[12], 71), 0),
        "live": draw_live(jax.random.fold_in(splits[12], 71), 0),
        "conv_weight": scatter_about(splits[3], (KC, D), KC ** -0.5, 0.078125, ((0, 16), (1, 2))),
        "qkv_weight": scatter_about(splits[4], (D, 3, D), (D // 2) ** -0.5, 0.3125, ((0, 16), (2, 2))),
        "out_weight": scatter_about(splits[5], (D, D), (D // 16) ** -0.5, 0.875, ((0, 2), (1, 16))),
        "up_weight": scatter_about(splits[6], (D, FF), D ** -0.5, 0.21875, ((0, 16), (1, 2))),
        "down_weight": scatter_about(splits[7], (FF, D), FF ** -0.5, 0.109375, ((0, 2), (1, 16))),
        "up_bias": scatter_about(splits[8], (FF,), 0.5, 3.0, ((0, 2),), jnp.float32),
        "gains": jnp.clip(1.0 + 0.18 * jax.random.normal(splits[9], (3, D), jnp.float32), 0.1, 1.9),
        "biases": scatter_about(splits[10], (8, D), 0.5, 3.0, ((1, 2),), jnp.float32),
        "out_grad": scatter_about(splits[11], (ROWS, FRAMES, D), 1.0, 6.0, ((0, 16), (2, 2))),
    }


HIGHEST_PRECISION = lax.Precision.HIGHEST
EPSILON = 1e-05
MASKED = -1e+30

@jax.custom_vjp
def low(v):
    return lax.optimization_barrier(v.astype(jnp.bfloat16)).astype(jnp.float32)

@jax.custom_vjp
def low_back(v):
    return v

def low_keep(v):
    return (low(v), None)

def low_pass(kept, grad):
    return (grad,)

def back_keep(v):
    return (v, None)

def back_low(kept, grad):
    return (low(grad),)
low.defvjp(low_keep, low_pass)
low_back.defvjp(back_keep, back_low)

def both_ways(features):
    return low(low_back(features))

def norm(features, gain_vec, shift_vec):
    mean_value = lax.optimization_barrier(jnp.mean(features, axis=-1, keepdims=True))
    center = features - mean_value
    variance = lax.optimization_barrier(jnp.mean(center * center, axis=-1, keepdims=True))
    return center * lax.rsqrt(variance + EPSILON) * gain_vec + shift_vec

def gelu_exact(features):
    return jax.nn.gelu(features, approximate=False)

def layer(row_frames, clip_ids, alive_mask, conv_weight, qkv_weight, out_weight, up_weight, down_weight, up_bias, gains, biases):
    group_width = D // GROUPS
    masked_input = row_frames * alive_mask[:, None]
    kernel = conv_weight.reshape(KERNEL, group_width, D)
    conv_out = lax.conv_general_dilated(masked_input[None], kernel, (1,), [(KERNEL // 2, KERNEL // 2 - 1)], dimension_numbers=('NWC', 'WIO', 'NWC'), feature_group_count=GROUPS, precision=HIGHEST_PRECISION)[0]
    conv_out = low_back(conv_out + biases[0])
    first_norm = norm(row_frames + gelu_exact(conv_out), gains[0], biases[1])
    first_low = low(first_norm)
    projected = jnp.einsum('sd,dcn->scn', first_low, qkv_weight, precision=HIGHEST_PRECISION)
    queries = both_ways(projected[:, 0] + biases[2]).reshape(FRAMES, HEADS, HEAD_DIM)
    keys_low = both_ways(projected[:, 1]).reshape(FRAMES, HEADS, HEAD_DIM)
    values = both_ways(projected[:, 2] + biases[3]).reshape(FRAMES, HEADS, HEAD_DIM)
    scores = low_back(jnp.einsum('qhe,khe->hqk', queries, keys_low, precision=HIGHEST_PRECISION) * HEAD_DIM ** (-0.5))
    same_clip = clip_ids[:, None] == clip_ids[None, :]
    scores = jnp.where(same_clip[None], scores, MASKED)
    probabilities = low(jax.nn.softmax(scores, axis=-1))
    context = both_ways(jnp.einsum('hqk,khe->qhe', probabilities, values, precision=HIGHEST_PRECISION).reshape(FRAMES, D))
    attended = low_back(jnp.dot(context, out_weight, precision=HIGHEST_PRECISION))
    second_norm = norm(first_norm + attended + biases[4], gains[1], biases[5])
    second_low = low(second_norm)
    up_proj = low_back(jnp.dot(second_low, up_weight, precision=HIGHEST_PRECISION) + up_bias)
    hidden = low(gelu_exact(up_proj))
    down_proj = low_back(jnp.dot(hidden, down_weight, precision=HIGHEST_PRECISION))
    return norm(second_norm + down_proj + biases[6], gains[2], biases[7])

def reference(frames, segment_ids, live, conv_weight, qkv_weight, out_weight, up_weight, down_weight, up_bias, gains, biases, out_grad):
    weight_list = tuple((piece.astype(jnp.float32) for piece in (conv_weight, qkv_weight, out_weight, up_weight, down_weight, up_bias, gains, biases)))

    def one_row(totals, item_pack):
        row_frames, clip_ids, alive_mask, row_grad = item_pack

        def apply_layer(features, *weight_args):
            return layer(features, clip_ids, alive_mask.astype(jnp.float32), *weight_args)
        mixed_out, pull_back = jax.vjp(apply_layer, row_frames.astype(jnp.float32), *weight_list)
        gradients = pull_back(row_grad.astype(jnp.float32))
        totals = tuple((running + addend for running, addend in zip(totals, gradients[1:])))
        return (totals, (mixed_out.astype(jnp.bfloat16), gradients[0]))
    zero_sums = tuple((jnp.zeros(piece.shape, jnp.float32) for piece in weight_list))
    totals, outputs = lax.scan(one_row, zero_sums, (frames, segment_ids, live, out_grad))
    return (outputs[0], outputs[1], totals[0], totals[1], totals[2], totals[3], totals[4], totals[5], totals[6], totals[7])
```

```python
from functools import partial

import jax
import jax.numpy as jnp
from jax import lax
from jax.experimental import pallas as pl
from jax.experimental.pallas import tpu as pltpu
from jax.sharding import PartitionSpec as P

D = 768
HEAD_DIM = 64
KERNEL = 128
GROUPS = 16


EPSILON = 1e-05
MASKED = -1e30


def spread_features(features):
    return lax.all_gather(features.astype(jnp.bfloat16), "mp", axis=2, tiled=True)


def spread_grads(features):
    return lax.all_gather(features.astype(jnp.bfloat16), "mp", axis=2, tiled=True)


def fold_partials(features):
    return lax.psum_scatter(
        features.astype(jnp.bfloat16), "mp", scatter_dimension=2, tiled=True
    ).astype(jnp.float32)


def fold_grads(features):
    return lax.psum_scatter(
        features.astype(jnp.bfloat16), "mp", scatter_dimension=2, tiled=True
    ).astype(jnp.float32)


def norm_forward(features, gain_vec, shift_vec):
    row_total = lax.psum(jnp.sum(features, axis=-1), "mp")
    center = features - (row_total / D)[..., None]
    spread = lax.psum(jnp.sum(center * center, axis=-1), "mp")
    variance = spread / D
    inv_scale = lax.rsqrt(variance + EPSILON)[..., None]
    normed = center * inv_scale
    return (normed * gain_vec + shift_vec, normed, inv_scale)


def norm_backward(incoming, normed, inv_scale, gain_vec):
    scaled = incoming * gain_vec
    first_sum, second_sum = lax.psum(
        (jnp.sum(scaled, axis=-1), jnp.sum(scaled * normed, axis=-1)), "mp"
    )
    result = inv_scale * (
        scaled - (first_sum / D)[..., None] - normed * (second_sum / D)[..., None]
    )
    return (result, jnp.sum(incoming * normed, axis=(0, 1)), jnp.sum(incoming, axis=(0, 1)))


def conv_fwd_kernel(x_ref, live_ref, w_ref, bias_ref, conv_ref, xt, ot, x16):
    g = pl.program_id(0)
    R, T, C = x_ref.shape
    L = xt.shape[2]
    nb, gw, na = 8, 48, 16
    @pl.when(g == 0)
    def _():
        for r in range(R):
            m = x_ref[r].astype(jnp.float32) * live_ref[r].astype(jnp.float32)
            m = jnp.concatenate([m, jnp.zeros((L - T, C), jnp.float32)], axis=0)
            xt[r] = m.T
    rows = pl.ds(pl.multiple_of(g * gw, 16), gw)
    for r in range(R):
        xg = xt[r, rows, :]
        for a in range(na):
            sh = (64 - 8 * a) % L
            v = pltpu.roll(xg, sh, axis=1) if sh else xg
            x16[a * gw:(a + 1) * gw, r * L:(r + 1) * L] = v.astype(jnp.bfloat16)
    w = w_ref[...].reshape(na * gw, nb * gw)
    y = lax.dot_general(w, x16[...], (((0,), (0,)), ((), ())), preferred_element_type=jnp.float32)
    for r in range(R):
        acc = y[0:gw, r * L:(r + 1) * L]
        for b in range(1, nb):
            acc = acc + pltpu.roll(y[b * gw:(b + 1) * gw, r * L:(r + 1) * L], L - b, axis=1)
        ot[r, rows, :] = acc
    @pl.when(g == pl.num_programs(0) - 1)
    def _():
        for r in range(R):
            conv_ref[r] = ot[r].T[:T] + bias_ref[...]

def conv_fwd(x, live, w, bias):
    R, T, C = x.shape
    L = 384
    return pl.pallas_call(
        conv_fwd_kernel,
        grid=(8,),
        in_specs=[pl.BlockSpec((R, T, C), lambda g: (0, 0, 0)),
                  pl.BlockSpec((R, T, 1), lambda g: (0, 0, 0)),
                  pl.BlockSpec((16, 1, 48, 384), lambda g: (0, g, 0, 0)),
                  pl.BlockSpec((1, C), lambda g: (0, 0))],
        out_specs=pl.BlockSpec((R, T, C), lambda g: (0, 0, 0)),
        out_shape=jax.ShapeDtypeStruct((R, T, C), jnp.float32),
        scratch_shapes=[pltpu.VMEM((R, C, L), jnp.float32), pltpu.VMEM((R, C, L), jnp.float32), pltpu.VMEM((768, R * L), jnp.bfloat16)],
        compiler_params=pltpu.CompilerParams(vmem_limit_bytes=48 << 20),
        name="conv_fwd",
    )(x, live, w, bias)

def conv_bwd_kernel(x_ref, live_ref, w_ref, gl_ref, gw_ref, gi_ref, xt, gt, ot, x16, g8):
    g = pl.program_id(0)
    R, T, C = x_ref.shape
    L = xt.shape[2]
    nb, gw, na = 8, 48, 16
    @pl.when(g == 0)
    def _():
        for r in range(R):
            m = x_ref[r].astype(jnp.float32) * live_ref[r].astype(jnp.float32)
            z = jnp.zeros((L - T, C), jnp.float32)
            xt[r] = jnp.concatenate([m, z], axis=0).T
            gt[r] = jnp.concatenate([gl_ref[r].astype(jnp.float32), z], axis=0).T
    rows = pl.ds(pl.multiple_of(g * gw, 16), gw)
    for r in range(R):
        xg = xt[r, rows, :]
        for a in range(na):
            sh = (64 - 8 * a) % L
            v = pltpu.roll(xg, sh, axis=1) if sh else xg
            x16[a * gw:(a + 1) * gw, r * L:(r + 1) * L] = v.astype(jnp.bfloat16)
        gg = gt[r, rows, :]
        for b in range(nb):
            v = pltpu.roll(gg, b, axis=1) if b else gg
            g8[b * gw:(b + 1) * gw, r * L:(r + 1) * L] = v.astype(jnp.bfloat16)
    grad = lax.dot_general(x16[...], g8[...], (((1,), (1,)), ((), ())), preferred_element_type=jnp.float32)
    gw_ref[...] = grad.reshape(na, 1, gw, nb * gw).astype(gw_ref.dtype)
    w = w_ref[...].reshape(na * gw, nb * gw)
    z = jnp.dot(w, g8[...], preferred_element_type=jnp.float32)
    for r in range(R):
        acc = None
        for a in range(na):
            sh = (8 * a - 64) % L
            v = z[a * gw:(a + 1) * gw, r * L:(r + 1) * L]
            v = pltpu.roll(v, sh, axis=1) if sh else v
            acc = v if acc is None else acc + v
        ot[r, rows, :] = acc
    @pl.when(g == pl.num_programs(0) - 1)
    def _():
        for r in range(R):
            gi_ref[r] = ot[r].T[:T] * live_ref[r].astype(jnp.float32)

def conv_bwd(x, live, w, gl, gdtype=jnp.float32):
    R, T, C = x.shape
    L = 384
    full = lambda g: (0, 0, 0)
    return pl.pallas_call(
        conv_bwd_kernel,
        grid=(8,),
        in_specs=[pl.BlockSpec((R, T, C), full), pl.BlockSpec((R, T, 1), full),
                  pl.BlockSpec((16, 1, 48, 384), lambda g: (0, g, 0, 0)),
                  pl.BlockSpec((R, T, C), full)],
        out_specs=[pl.BlockSpec((16, 1, 48, 384), lambda g: (0, g, 0, 0)), pl.BlockSpec((R, T, C), full)],
        out_shape=[jax.ShapeDtypeStruct((16, 8, 48, 384), gdtype), jax.ShapeDtypeStruct((R, T, C), jnp.float32)],
        scratch_shapes=[pltpu.VMEM((R, C, L), jnp.float32)] * 3 + [pltpu.VMEM((768, R * L), jnp.bfloat16), pltpu.VMEM((384, R * L), jnp.bfloat16)],
        compiler_params=pltpu.CompilerParams(vmem_limit_bytes=48 << 20),
        name="conv_bwd",
    )(x, live, w, gl)

def taps_in(weight):
    blocks = weight.reshape(-1, 8, 48, 8, 48)
    return blocks.transpose(0, 3, 2, 1, 4).reshape(-1, 8, 48, 384)


def taps_out(grad):
    blocks = grad.reshape(-1, 8, 48, 8, 48)
    return blocks.transpose(0, 3, 2, 1, 4).reshape(-1, 384)


def heads_first(features):
    row_count, frame_count, width = features.shape
    return (
        features.reshape(row_count, frame_count, width // HEAD_DIM, HEAD_DIM)
        .transpose(0, 2, 1, 3)
        .reshape(-1, frame_count, HEAD_DIM)
    )


def heads_last(items, row_count):
    item_count, frame_count, head_width = items.shape
    return (
        items.reshape(row_count, item_count // row_count, frame_count, head_width)
        .transpose(0, 2, 1, 3)
        .reshape(row_count, frame_count, -1)
    )


def masked_scores(queries, keys_low, clip_ids):
    scale_factor = queries.shape[-1] ** (-0.5)
    scores = (
        jnp.einsum("qe,ke->qk", queries, keys_low, preferred_element_type=jnp.float32)
        * scale_factor
    )
    same_clip = clip_ids[:, None] == clip_ids[None, :]
    return jnp.where(same_clip, scores, MASKED)


def attend_one(item_pack):
    queries, keys_low, values, clip_ids = item_pack
    scores = masked_scores(queries, keys_low, clip_ids)
    row_max = jnp.max(scores, axis=-1, keepdims=True)
    weights = jnp.exp(scores - row_max)
    row_total = jnp.sum(weights, axis=-1, keepdims=True)
    probabilities = (weights / row_total).astype(jnp.bfloat16)
    context = jnp.dot(probabilities, values, preferred_element_type=jnp.float32).astype(
        jnp.bfloat16
    )
    return (context, (row_max + jnp.log(row_total))[:, 0])


def attend_back(item_pack):
    queries, keys_low, values, clip_ids, log_total, grad_context = item_pack
    scale_factor = queries.shape[-1] ** (-0.5)
    scores = masked_scores(queries, keys_low, clip_ids)
    probabilities = jnp.exp(scores - log_total[:, None])
    grad_probs = jnp.einsum("qe,ke->qk", grad_context, values, preferred_element_type=jnp.float32)
    row_dot = jnp.sum(grad_probs * probabilities, axis=-1, keepdims=True)
    grad_scores = (probabilities * (grad_probs - row_dot)).astype(jnp.bfloat16)
    grad_queries = (
        jnp.dot(grad_scores, keys_low, preferred_element_type=jnp.float32) * scale_factor
    ).astype(jnp.bfloat16)
    grad_keys = (
        jnp.einsum("qk,qe->ke", grad_scores, queries, preferred_element_type=jnp.float32)
        * scale_factor
    ).astype(jnp.bfloat16)
    grad_values = jnp.einsum(
        "qk,qe->ke",
        probabilities.astype(jnp.bfloat16),
        grad_context,
        preferred_element_type=jnp.float32,
    ).astype(jnp.bfloat16)
    return (grad_queries, grad_keys, grad_values)


def body(
    frames,
    segment_ids,
    live,
    conv_weight,
    qkv_weight,
    out_weight,
    up_weight,
    down_weight,
    up_bias,
    gains,
    biases,
    out_grad,
):
    row_count = frames.shape[0]
    width = frames.shape[2]
    head_count = width // HEAD_DIM
    hid = up_weight.shape[1]
    gelu_exact = partial(jax.nn.gelu, approximate=False)
    whole_blocks = conv_weight.shape[0] % (8 * 48) == 0
    if whole_blocks:
        conv_full = lax.all_gather(taps_in(conv_weight), "dp", axis=0, tiled=True)
    else:
        conv_full = taps_in(lax.all_gather(conv_weight, "dp", axis=0, tiled=True))
    wall = jnp.concatenate(
        [qkv_weight.reshape(-1, 3 * width), out_weight.T, up_weight, down_weight.T], axis=1
    )
    wall = lax.all_gather(wall, "dp", axis=0, tiled=True)
    cuts = (3 * width, 4 * width, 4 * width + hid)
    qkv_full, out_t, up_full, down_t = jnp.split(wall, cuts, axis=1)
    alive = live[..., None]
    conv_out = conv_fwd(frames, alive, conv_full, biases[0:1])
    positioned = frames.astype(jnp.float32) + gelu_exact(conv_out)
    first_norm, normed_zero, scale_zero = norm_forward(positioned, gains[0], biases[1])
    first_full = spread_features(first_norm)
    projected = jnp.einsum("rsd,dn->rsn", first_full, qkv_full, preferred_element_type=jnp.float32)
    query_items = heads_first((projected[:, :, :width] + biases[2]).astype(jnp.bfloat16))
    key_items = heads_first(projected[:, :, width : 2 * width].astype(jnp.bfloat16))
    value_items = heads_first((projected[:, :, 2 * width :] + biases[3]).astype(jnp.bfloat16))
    item_ids = jnp.repeat(segment_ids, head_count, axis=0)
    context_items, log_total = jax.vmap(lambda *p: attend_one(p))(
        query_items, key_items, value_items, item_ids
    )
    context = heads_last(context_items, row_count)
    attended = fold_partials(
        jnp.einsum("rsh,dh->rsd", context, out_t, preferred_element_type=jnp.float32)
    )
    second_norm, normed_one, scale_one = norm_forward(
        first_norm + attended + biases[4], gains[1], biases[5]
    )
    second_full = spread_features(second_norm)
    up_proj = (
        jnp.einsum("rsd,df->rsf", second_full, up_full, preferred_element_type=jnp.float32)
        + up_bias
    )
    hidden = gelu_exact(up_proj).astype(jnp.bfloat16)
    down_proj = fold_partials(
        jnp.einsum("rsf,df->rsd", hidden, down_t, preferred_element_type=jnp.float32)
    )
    mixed_out, normed_two, scale_two = norm_forward(
        second_norm + down_proj + biases[6], gains[2], biases[7]
    )
    incoming = out_grad.astype(jnp.float32)
    grad_second, gain_two, shift_two = norm_backward(incoming, normed_two, scale_two, gains[2])
    grad_down_full = spread_grads(grad_second)
    grad_down = jnp.einsum(
        "rsf,rsd->df", hidden, grad_down_full, preferred_element_type=jnp.float32
    )
    grad_hidden = jnp.einsum(
        "rsd,df->rsf", grad_down_full, down_t, preferred_element_type=jnp.float32
    )
    up_pull = jax.vjp(gelu_exact, up_proj)[1]
    grad_up_low = up_pull(grad_hidden)[0].astype(jnp.bfloat16)
    grad_up = jnp.einsum("rsd,rsf->df", second_full, grad_up_low, preferred_element_type=jnp.float32)
    grad_up_bias = jnp.sum(grad_up_low, axis=(0, 1), dtype=jnp.float32)
    grad_h_one = grad_second + fold_grads(
        jnp.einsum("rsf,df->rsd", grad_up_low, up_full, preferred_element_type=jnp.float32)
    )
    grad_first, gain_one, shift_one = norm_backward(grad_h_one, normed_one, scale_one, gains[1])
    grad_att_full = spread_grads(grad_first)
    grad_out = jnp.einsum(
        "rsh,rsd->dh", context, grad_att_full, preferred_element_type=jnp.float32
    )
    grad_context = jnp.einsum(
        "rsd,dh->rsh", grad_att_full, out_t, preferred_element_type=jnp.float32
    ).astype(jnp.bfloat16)
    grad_query_items, grad_key_items, grad_value_items = jax.vmap(lambda *p: attend_back(p))(
        query_items, key_items, value_items, item_ids, log_total, heads_first(grad_context)
    )
    grad_queries = heads_last(grad_query_items, row_count)
    grad_values = heads_last(grad_value_items, row_count)
    grad_stack = jnp.concatenate(
        [grad_queries, heads_last(grad_key_items, row_count), grad_values], axis=2
    )
    grad_qkv = jnp.einsum(
        "rsd,rsn->dn", first_full, grad_stack, preferred_element_type=jnp.float32
    )
    grad_h_zero = grad_first + fold_grads(
        jnp.einsum("rsn,dn->rsd", grad_stack, qkv_full, preferred_element_type=jnp.float32)
    )
    grad_pos, gain_zero, shift_zero = norm_backward(grad_h_zero, normed_zero, scale_zero, gains[0])
    conv_pull = jax.vjp(gelu_exact, conv_out)[1]
    grad_conv_low = conv_pull(grad_pos)[0].astype(jnp.bfloat16)
    grad_conv, grad_in = conv_bwd(frames, alive, conv_full, grad_conv_low, jnp.bfloat16)
    grad_wall = jnp.concatenate([grad_qkv, grad_out, grad_up, grad_down], axis=1)
    grad_wall = lax.psum_scatter(
        grad_wall.astype(jnp.bfloat16), "dp", scatter_dimension=0, tiled=True
    ).astype(jnp.float32)
    qkv_part, out_part, up_part, down_part = jnp.split(grad_wall, cuts, axis=1)
    if whole_blocks:
        conv_part = taps_out(
            lax.psum_scatter(grad_conv, "dp", scatter_dimension=0, tiled=True).astype(jnp.float32)
        )
    else:
        conv_part = lax.psum_scatter(
            taps_out(grad_conv), "dp", scatter_dimension=0, tiled=True
        ).astype(jnp.float32)
    gain_terms = jnp.stack([gain_zero, gain_one, gain_two])
    bias_terms = jnp.stack(
        [
            jnp.sum(grad_conv_low, axis=(0, 1), dtype=jnp.float32),
            shift_zero,
            jnp.sum(grad_queries, axis=(0, 1), dtype=jnp.float32),
            jnp.sum(grad_values, axis=(0, 1), dtype=jnp.float32),
            jnp.sum(grad_first, axis=(0, 1)),
            shift_one,
            jnp.sum(grad_second, axis=(0, 1)),
            shift_two,
        ]
    )
    gain_total, bias_total, up_bias_total = lax.psum((gain_terms, bias_terms, grad_up_bias), "dp")
    return (
        mixed_out.astype(jnp.bfloat16),
        grad_pos + grad_in,
        conv_part,
        qkv_part.reshape(-1, 3, width),
        out_part.T,
        up_part,
        down_part.T,
        up_bias_total,
        gain_total,
        bias_total,
    )


def solution(mesh):
    placed = (
        P("dp", None, "mp"),
        P("dp", None),
        P("dp", None),
        P("dp", "mp"),
        P("dp", None, "mp"),
        P("mp", "dp"),
        P("dp", "mp"),
        P("mp", "dp"),
        P("mp"),
        P(None, "mp"),
        P(None, "mp"),
        P("dp", None, "mp"),
    )
    return jax.shard_map(
        body,
        mesh=mesh,
        in_specs=placed,
        out_specs=(
            P("dp", None, "mp"),
            P("dp", None, "mp"),
            P("dp", "mp"),
            P("dp", None, "mp"),
            P("mp", "dp"),
            P("dp", "mp"),
            P("mp", "dp"),
            P("mp"),
            P(None, "mp"),
            P(None, "mp"),
        ),
        check_vma=False,
    )
```

```python
import functools

import jax
import jax.numpy as jnp
from jax import lax
from jax.experimental import pallas as pl
from jax.experimental.pallas import tpu as pltpu
from jax.sharding import PartitionSpec as P

MESH = pl.DeviceIdType.MESH
F32, BF16 = jnp.float32, jnp.bfloat16
D, H, FF, HD = 768, 384, 1536, 64
R, T, L = 2, 320, 384
NB, GW, NA = 8, 48, 16
TM = 64
EPS = 1e-5
QKV, OUT, UP, DOWN = 0, 1152, 1536, 3072
NN = (((1,), (0,)), ((), ()))
NT = (((1,), (1,)), ((), ()))
TN = (((0,), (0,)), ((), ()))

def mm(a, b, dims=NN):
    return lax.dot_general(a, b, dims, preferred_element_type=F32)

def gelu_both(v):
    p = 0.5 + 0.5 * lax.erf(v * 0.7071067811865476)
    return v * p, p + v * (0.3989422804014327 * jnp.exp(-0.5 * v * v))

def tiles(body, count=T // TM, init=0):
    return lax.fori_loop(0, count, body, init)

def at(i, size=TM):
    return pl.ds(pl.multiple_of(i * size, size), size)

class Mid:
    def shift_inputs(self, g):
        rows = at(g, GW)
        for r in range(R):
            xg = self.xt[r, rows, :]
            for a in range(NA):
                sh = (64 - 8 * a) % L
                v = pltpu.roll(xg, sh, axis=1) if sh else xg
                self.x16[a * GW:(a + 1) * GW, r * L:(r + 1) * L] = v.astype(BF16)

    def turn_in(self, dst, r, rows):
        dst[r] = jnp.concatenate([rows, jnp.zeros((L - T, H), F32)], axis=0).T

    def conv_forward(self):
        for r in range(R):
            self.turn_in(self.xt, r, self.act[0, r, :, self.own].astype(F32) * self.live[r].astype(F32))

        def group(g, c):
            self.shift_inputs(g)
            w = self.convw[:, at(g, GW), :].reshape(NA * GW, NB * GW)
            y = mm(w, self.x16[...], TN)
            for r in range(R):
                acc = y[0:GW, r * L:(r + 1) * L]
                for b in range(1, NB):
                    acc = acc + pltpu.roll(y[b * GW:(b + 1) * GW, r * L:(r + 1) * L], L - b, axis=1)
                self.ot[r, at(g, GW), :] = acc
            return c
        tiles(group, 8)

    def conv_finish(self, r):
        v = self.ot[r].T[:T] + self.par[3:4, self.own]
        gel, dg = gelu_both(v)
        self.dconv[r] = dg
        self.gc[r, :, self.own] = gel.astype(BF16)

    def norm_first(self, r):
        def tile(i, c):
            v = self.act[0, r, at(i), :].astype(F32) + self.gc[r, at(i), :].astype(F32)
            cen = v - jnp.sum(v, axis=1, keepdims=True) * (1.0 / D)
            inv = lax.rsqrt(jnp.sum(cen * cen, axis=1, keepdims=True) * (1.0 / D) + EPS)
            xh = cen * inv
            n = xh * self.par[0:1, :] + self.par[4:5, :]
            self.xh0[r, at(i), :] = xh
            self.inv0[r, at(i), :] = inv
            self.fn[r, at(i), :] = n
            self.flow[r, at(i), :] = n.astype(BF16)
            return c
        tiles(tile)

    def wall_cols(self, start, size):
        return self.wall[:, :, pl.ds(start, size)].reshape(D, size)

    def wall_rows(self, n, start, size):
        return self.wall[pl.ds(n * 8, 8), :, start:start + size].reshape(H, size)

    def project(self, r):
        for c in range(3):
            v = mm(self.flow[r], self.wall_cols(QKV + c * H, H))
            if c != 1:
                v = v + self.par[5 + c // 2:6 + c // 2, self.own]
            self.qkv[r, :, c * H:(c + 1) * H] = v.astype(BF16)

    def lane_masks(self):
        lane = lax.broadcasted_iota(jnp.int32, (1, 128), 1)
        return [(lane < HD).astype(F32).astype(BF16), (lane >= HD).astype(F32).astype(BF16)]

    def pair(self, ref, r, p, c=0):
        return ref[r, :, pl.ds(pl.multiple_of(p * 128 + c * H, 128), 128)]

    def attend(self, r):
        masks = self.lane_masks()
        same = self.segq[r] == self.segk[r]

        def step(p, c):
            q, k, v = (self.pair(self.qkv, r, p, i) for i in range(3))
            acc = None
            for h in range(2):
                s = mm(q * masks[h], k, NT) * 0.125
                s = jnp.where(same, s, -1e30)
                w = jnp.exp(s - jnp.max(s, axis=1, keepdims=True))
                pr = (w * (1.0 / jnp.sum(w, axis=1, keepdims=True))).astype(BF16)
                self.prob[r * 6 + p * 2 + h] = pr
                o = mm(pr, v * masks[h])
                acc = o if acc is None else acc + o
            self.ctx[r, :, pl.ds(pl.multiple_of(p * 128, 128), 128)] = acc.astype(BF16)
            return c
        tiles(step, 3)
        for n in range(2):
            self.a_own[r, :, n * H:(n + 1) * H] = mm(self.ctx[r], self.wall_rows(n, OUT, H), NT).astype(BF16)

    def norm_second(self, r):
        def tile(i, c):
            v = self.fn[r, at(i), :] + (self.a_own[r, at(i), :].astype(F32) + self.a_peer[r, at(i), :].astype(F32)) + self.par[7:8, :]
            cen = v - jnp.sum(v, axis=1, keepdims=True) * (1.0 / D)
            inv = lax.rsqrt(jnp.sum(cen * cen, axis=1, keepdims=True) * (1.0 / D) + EPS)
            xh = cen * inv
            n = xh * self.par[1:2, :] + self.par[8:9, :]
            self.xh1[r, at(i), :] = xh
            self.inv1[r, at(i), :] = inv
            self.sn[r, at(i), :] = n
            self.slow[r, at(i), :] = n.astype(BF16)
            return c
        tiles(tile)

    def feed_forward(self, r):
        for n in range(4):
            u = mm(self.slow[r], self.wall_cols(UP + n * H, H)) + self.upb[:, n * H:(n + 1) * H]
            gel, dg = gelu_both(u)
            self.hid[r, :, n * H:(n + 1) * H] = gel.astype(BF16)
            self.dg[r, :, n * H:(n + 1) * H] = dg.astype(BF16)
        for n in range(2):
            self.b_own[r, :, n * H:(n + 1) * H] = mm(self.hid[r], self.wall_rows(n, DOWN, FF), NT).astype(BF16)

    def add_sums(self, row, value):
        self.psum[row:row + 1, :] += value

    def norm_third(self, r):
        def tile(i, c):
            v = self.sn[r, at(i), :] + (self.b_own[r, at(i), :].astype(F32) + self.b_peer[r, at(i), :].astype(F32)) + self.par[9:10, :]
            cen = v - jnp.sum(v, axis=1, keepdims=True) * (1.0 / D)
            inv = lax.rsqrt(jnp.sum(cen * cen, axis=1, keepdims=True) * (1.0 / D) + EPS)
            xh = cen * inv
            self.mixf[at(i), :] = (xh * self.par[2:3, :] + self.par[10:11, :]).astype(BF16)
            e = self.act[1, r, at(i), :].astype(F32)
            sc = e * self.par[2:3, :]
            ex = e * xh
            m1 = jnp.sum(sc, axis=1, keepdims=True) * (1.0 / D)
            m2 = jnp.sum(sc * xh, axis=1, keepdims=True) * (1.0 / D)
            g = inv * (sc - m1 - xh * m2)
            self.sn[r, at(i), :] = g
            self.gdl[r, at(i), :] = g.astype(BF16)
            sums = [jnp.sum(w, axis=0, keepdims=True) for w in (ex, e, g)]
            return tuple(x + y for x, y in zip(c, sums))
        z = jnp.zeros((1, D), F32)
        s = tiles(tile, init=(z, z, z))
        for row, val in zip((2, 10, 9), s):
            self.add_sums(row, val)
        self.mixed[r] = self.mixf[:, self.own]

    def feed_backward(self, r):
        for n in range(4):
            gh = mm(self.gdl[r], self.wall_cols(DOWN + n * H, H))
            g = (gh * self.dg[r, :, n * H:(n + 1) * H].astype(F32)).astype(BF16)
            self.dg[r, :, n * H:(n + 1) * H] = g
            self.pout[12 + n:13 + n, :] += jnp.sum(g.astype(F32), axis=0, keepdims=True)
        for n in range(2):
            self.a_own[r, :, n * H:(n + 1) * H] = mm(self.dg[r], self.wall_rows(n, UP, FF), NT).astype(BF16)

    def weight_grad(self, src, other, count, start):
        for n in range(count):
            o = other[:, :, n * H:(n + 1) * H].reshape(R * T, H)
            g = mm(src[...].reshape(R * T, D), o, TN)
            self.wall[:, :, start + n * H:start + (n + 1) * H] = g.reshape(16, 48, H).astype(BF16)

    def norm_second_back(self, r):
        def tile(i, c):
            e = self.sn[r, at(i), :] + (self.a_own[r, at(i), :].astype(F32) + self.a_peer[r, at(i), :].astype(F32))
            xh = self.xh1[r, at(i), :]
            sc = e * self.par[1:2, :]
            m1 = jnp.sum(sc, axis=1, keepdims=True) * (1.0 / D)
            m2 = jnp.sum(sc * xh, axis=1, keepdims=True) * (1.0 / D)
            g = self.inv1[r, at(i), :] * (sc - m1 - xh * m2)
            self.sn[r, at(i), :] = g
            self.gal[r, at(i), :] = g.astype(BF16)
            sums = [jnp.sum(w, axis=0, keepdims=True) for w in (e * xh, e, g)]
            return tuple(x + y for x, y in zip(c, sums))
        z = jnp.zeros((1, D), F32)
        s = tiles(tile, init=(z, z, z))
        for row, val in zip((1, 8, 7), s):
            self.add_sums(row, val)

    def attend_back(self, r):
        self.gctx[r] = mm(self.gal[r], self.wall_cols(OUT, H)).astype(BF16)
        masks = self.lane_masks()

        def step(p, c):
            q, k, v = (self.pair(self.qkv, r, p, i) for i in range(3))
            go = self.pair(self.gctx, r, p)
            gq = gk = gv = None
            for h in range(2):
                gom = go * masks[h]
                gp = mm(gom, v, NT)
                pr = self.prob[r * 6 + p * 2 + h]
                pf = pr.astype(F32)
                gs = (pf * (gp - jnp.sum(gp * pf, axis=1, keepdims=True))).astype(BF16)
                a, b, d = mm(gs, k * masks[h]), mm(gs, q * masks[h], TN), mm(pr, gom, TN)
                gq, gk, gv = (a, b, d) if gq is None else (gq + a, gk + b, gv + d)
            for i, w in enumerate((gq * 0.125, gk * 0.125, gv)):
                self.gst[r, :, pl.ds(pl.multiple_of(p * 128 + i * H, 128), 128)] = w.astype(BF16)
            return c
        tiles(step, 3)
        for row, c in ((5, 0), (6, 2)):
            self.psum[row:row + 1, self.own] += jnp.sum(self.gst[r, :, c * H:(c + 1) * H].astype(F32), axis=0, keepdims=True)

    def project_back(self, r):
        po = mm(self.gst[r], self.wall_rows(1 - self.mp, QKV, 1152), NT)
        pw = mm(self.gst[r], self.wall_rows(self.mp, QKV, 1152), NT)
        self.b_own[r, :, 0:H] = po.astype(BF16)
        self.pown[r] = pw
        so = po * self.par[0:1, self.oth]
        sw = pw * self.par[0:1, self.own]
        s1 = jnp.sum(so + sw, axis=1, keepdims=True)
        s2 = jnp.sum(so * self.xh0[r, :, self.oth] + sw * self.xh0[r, :, self.own], axis=1, keepdims=True)
        lane = lax.broadcasted_iota(jnp.int32, (T, 128), 1)
        st = jnp.where(lane == 0, s1, jnp.where(lane == 1, s2, 0.0))
        self.st[r] = st
        st = jnp.concatenate([st, jnp.zeros((L - T, 128), F32)], axis=0).T
        self.st_own[r] = st[0:8, :]

    def norm_first_back(self, r):
        stp = jnp.concatenate([self.st_peer[r], jnp.zeros((120, L), F32)], axis=0).T[:T]
        self.st[r] += stp
        gain = self.par[0:1, :]

        def tile(i, c):
            g1 = self.sn[r, at(i), :]
            sc1 = g1 * gain
            st = self.st[r, at(i), :]
            m1 = (jnp.sum(sc1, axis=1, keepdims=True) + st[:, 0:1]) * (1.0 / D)
            m2 = (jnp.sum(sc1 * self.xh0[r, at(i), :], axis=1, keepdims=True) + st[:, 1:2]) * (1.0 / D)
            xh = self.xh0[r, at(i), self.own]
            e = self.sn[r, at(i), self.own] + self.pown[r, at(i), :] + self.b_peer[r, at(i), 0:H].astype(F32)
            g = self.inv0[r, at(i), :] * (e * self.par[0:1, self.own] - m1 - xh * m2)
            self.gf[r, at(i), :] = g
            low = (g * self.dconv[r, at(i), :]).astype(BF16)
            lf = low.astype(F32)
            self.dconv[r, at(i), :] = lf
            sums = [jnp.sum(w, axis=0, keepdims=True) for w in (e * xh, e, lf)]
            return tuple(x + y for x, y in zip(c, sums))
        z = jnp.zeros((1, H), F32)
        s = tiles(tile, init=(z, z, z))
        for row, val in zip((0, 4, 3), s):
            self.psum[row:row + 1, self.own] += val
        self.turn_in(self.gt, r, self.dconv[r])

    def conv_backward(self):
        def group(g, c):
            self.shift_inputs(g)
            for r in range(R):
                gg = self.gt[r, at(g, GW), :]
                for b in range(NB):
                    v = pltpu.roll(gg, b, axis=1) if b else gg
                    self.g8[b * GW:(b + 1) * GW, r * L:(r + 1) * L] = v.astype(BF16)
            w = self.convw[:, at(g, GW), :].reshape(NA * GW, NB * GW)
            z = mm(w, self.g8[...])
            for r in range(R):
                acc = None
                for a in range(NA):
                    sh = (8 * a - 64) % L
                    v = z[a * GW:(a + 1) * GW, r * L:(r + 1) * L]
                    v = pltpu.roll(v, sh, axis=1) if sh else v
                    acc = v if acc is None else acc + v
                self.ot[r, at(g, GW), :] = acc
            gr = mm(self.x16[...], self.g8[...], NT)
            self.convw[:, at(g, GW), :] = gr.reshape(NA, GW, NB * GW).astype(BF16)
            return c
        tiles(group, 8)
        for r in range(R):
            self.gf[r] += self.ot[r].T[:T] * self.live[r].astype(F32)

SCRATCH = dict(
    convw=((16, H, H), BF16), wall=((16, 48, 4608), BF16),
    xt=((R, H, L), F32), ot=((R, H, L), F32), gt=((R, H, L), F32), x16=((768, R * L), BF16), g8=((H, R * L), BF16),
    gc=((R, T, D), BF16), dconv=((R, T, H), F32), xh0=((R, T, D), F32), inv0=((R, T, 1), F32), fn=((R, T, D), F32), flow=((R, T, D), BF16),
    qkv=((R, T, 1152), BF16), prob=((R * 6, T, T), BF16), ctx=((R, T, H), BF16),
    a_own=((R, T, D), BF16), a_peer=((R, T, D), BF16), b_own=((R, T, D), BF16), b_peer=((R, T, D), BF16),
    xh1=((R, T, D), F32), inv1=((R, T, 1), F32), sn=((R, T, D), F32), slow=((R, T, D), BF16),
    hid=((R, T, FF), BF16), dg=((R, T, FF), BF16), mixf=((T, D), BF16), gdl=((R, T, D), BF16), gal=((R, T, D), BF16),
    gctx=((R, T, H), BF16), gst=((R, T, 1152), BF16), pown=((R, T, H), F32), st=((R, T, 128), F32),
    st_own=((R, 8, L), F32), st_peer=((R, 8, L), F32), psum=((16, D), F32),
)
INS = ("convw_hbm", "wa_hbm", "wb_hbm", "act", "par", "upb", "segq", "segk", "live")
OUTS = ("mixed", "gf", "gconv_hbm", "ga_hbm", "gb_hbm", "pout")

def mid_kernel(*refs):
    m = Mid()
    names = INS + OUTS + tuple(SCRATCH)
    for name, ref in zip(names, refs):
        setattr(m, name, ref)
    loc, snd, rcv = refs[len(names):]
    mp = lax.axis_index("mp")
    m.mp = mp
    m.own = pl.ds(pl.multiple_of(mp * H, 128), H)
    m.oth = pl.ds(pl.multiple_of((1 - mp) * H, 128), H)
    loads = [pltpu.make_async_copy(m.convw_hbm, m.convw, loc.at[0]), pltpu.make_async_copy(m.wa_hbm, m.wall.at[:, :, 0:UP], loc.at[1]), pltpu.make_async_copy(m.wb_hbm, m.wall.at[:, :, UP:4608], loc.at[2])]
    for c in loads:
        c.start()
    peer = {"mp": 1 - mp}
    bar = pltpu.get_barrier_semaphore()
    pl.semaphore_signal(bar, inc=1, device_id=peer, device_id_type=MESH)
    m.psum[...] = jnp.zeros((16, D), F32)
    m.pout[...] = jnp.zeros((16, H), F32)
    pl.semaphore_wait(bar, 1)

    def swap(i, r, src, dst, land):
        c = pltpu.make_async_remote_copy(src, dst, snd.at[i, r], rcv.at[i, r], device_id=peer, device_id_type=MESH)
        c.start()
        return c, pltpu.make_async_remote_copy(land, land, snd.at[i, r], rcv.at[i, r], device_id=peer, device_id_type=MESH)

    loads[0].wait()
    m.conv_forward()
    pend = {}
    for r in range(R):
        m.conv_finish(r)
        pend[0, r] = swap(0, r, m.gc.at[r, :, m.own], m.gc.at[r, :, m.own], m.gc.at[r, :, m.oth])
    loads[1].wait()
    loads[2].wait()
    for r in range(R):
        pend[0, r][1].wait_recv()
        m.norm_first(r)
        m.project(r)
        m.attend(r)
        pend[1, r] = swap(1, r, m.a_own.at[r], m.a_peer.at[r], m.a_peer.at[r])
    for r in range(R):
        pend[1, r][1].wait_recv()
        m.norm_second(r)
        m.feed_forward(r)
        pend[2, r] = swap(2, r, m.b_own.at[r], m.b_peer.at[r], m.b_peer.at[r])
    for r in range(R):
        pend[2, r][1].wait_recv()
        m.norm_third(r)
        pend[1, r][0].wait_send()
        m.feed_backward(r)
        pend[3, r] = swap(3, r, m.a_own.at[r], m.a_peer.at[r], m.a_peer.at[r])
    m.weight_grad(m.gdl, m.hid, 4, DOWN)
    m.weight_grad(m.slow, m.dg, 4, UP)
    gb = pltpu.make_async_copy(m.wall.at[:, :, UP:4608], m.gb_hbm, loc.at[2])
    gb.start()
    for r in range(R):
        pend[3, r][1].wait_recv()
        m.norm_second_back(r)
        m.attend_back(r)
        pend[2, r][0].wait_send()
        m.project_back(r)
        pend[4, r] = swap(4, r, m.b_own.at[r, :, 0:H], m.b_peer.at[r, :, 0:H], m.b_peer.at[r, :, 0:H])
        pend[5, r] = swap(5, r, m.st_own.at[r], m.st_peer.at[r], m.st_peer.at[r])
    m.weight_grad(m.gal, m.ctx, 1, OUT)
    m.weight_grad(m.flow, m.gst, 3, QKV)
    ga = pltpu.make_async_copy(m.wall.at[:, :, 0:UP], m.ga_hbm, loc.at[1])
    ga.start()
    for r in range(R):
        pend[5, r][1].wait_recv()
        pend[4, r][1].wait_recv()
        m.norm_first_back(r)
    m.conv_backward()
    gc = pltpu.make_async_copy(m.convw, m.gconv_hbm, loc.at[0])
    gc.start()
    m.pout[0:11, :] = m.psum[0:11, m.own]
    for i, r in ((0, 0), (0, 1), (3, 0), (3, 1), (4, 0), (4, 1), (5, 0), (5, 1)):
        pend[i, r][0].wait_send()
    ga.wait()
    gb.wait()
    gc.wait()

def mid(convw, wa, wb, act, par, upb, segq, segk, live):
    vm, hb = pl.BlockSpec(memory_space=pltpu.VMEM), pl.BlockSpec(memory_space=pl.ANY)
    return pl.pallas_call(
        mid_kernel,
        out_shape=[jax.ShapeDtypeStruct((R, T, H), BF16), jax.ShapeDtypeStruct((R, T, H), F32), jax.ShapeDtypeStruct((16, H, H), BF16),
                   jax.ShapeDtypeStruct((16, 48, UP), BF16), jax.ShapeDtypeStruct((16, 48, 4608 - UP), BF16), jax.ShapeDtypeStruct((16, H), F32)],
        in_specs=[hb] * 3 + [vm] * 6,
        out_specs=[vm, vm, hb, hb, hb, vm],
        scratch_shapes=[pltpu.VMEM(s, d) for s, d in SCRATCH.values()] + [pltpu.SemaphoreType.DMA((3,)), pltpu.SemaphoreType.DMA((6, R)), pltpu.SemaphoreType.DMA((6, R))],
        compiler_params=pltpu.CompilerParams(collective_id=1, has_side_effects=True, vmem_limit_bytes=60 << 20),
        name="layer",
    )(convw, wa, wb, act, par, upb, segq, segk, live)


def ring_place(n):
    me = lax.axis_index("dp")
    core = lax.rem(me, 2)
    chip = me // 2
    odd = lax.rem(chip, 2)
    half = chip // 2
    pos = (1 - odd) * half + odd * (n - 1 - half)
    step = 1 - 2 * core
    def dev_at(p, c):
        p = lax.rem(p + 8 * n, n)
        q = p // (n // 2)
        return 2 * ((1 - q) * 2 * p + q * (2 * (n - 1 - p) + 1)) + c
    return me, core, pos, step, dev_at

def ag_kernel(n, ns, *refs):
    shards, (act, par), fulls, (act_full, par_full), sems = refs[:ns], refs[ns:ns+2], refs[ns+2:2*ns+2], refs[2*ns+2:2*ns+4], refs[2*ns+4:]
    ring_s, ring_r, sib_s, sib_r, loc, mp_s, mp_r = sems
    me, core, pos, step, dev_at = ring_place(n)
    mp = lax.axis_index("mp")
    nxt, prv, sib = dev_at(pos + step, core), dev_at(pos - step, core), me + 1 - 2 * core
    bar = pltpu.get_barrier_semaphore()
    for d in ({"dp": nxt}, {"dp": prv}, {"dp": sib}, {"mp": 1 - mp}):
        pl.semaphore_signal(bar, inc=1, device_id=d, device_id_type=MESH)
    pl.semaphore_wait(bar, 4)
    W = act.shape[-1]
    cols = pl.ds(pl.multiple_of(mp * W, 128), W)
    mps = [pltpu.make_async_remote_copy(act, act_full.at[:, :, :, cols], mp_s.at[0], mp_r.at[0], device_id={"mp": 1 - mp}, device_id_type=MESH),
           pltpu.make_async_remote_copy(par, par_full.at[:, cols], mp_s.at[1], mp_r.at[1], device_id={"mp": 1 - mp}, device_id_type=MESH)]
    for c in mps: c.start()
    locs = [pltpu.make_async_copy(act, act_full.at[:, :, :, cols], loc.at[ns]), pltpu.make_async_copy(par, par_full.at[:, cols], loc.at[ns + 1])]
    for i in range(ns):
        locs.append(pltpu.make_async_copy(shards[i], fulls[i].at[me], loc.at[i]))
    for c in locs: c.start()
    started = []
    for s in range(n):
        mine = dev_at(pos - step * s, core)
        for i in range(ns):
            slot = fulls[i].at[mine]
            src = shards[i] if s == 0 else slot
            if s > 0:
                pltpu.make_async_remote_copy(slot, slot, ring_s.at[i, s - 1], ring_r.at[i, s - 1], device_id={"dp": nxt}, device_id_type=MESH).wait_recv()
            if s < n - 1:
                c = pltpu.make_async_remote_copy(src, slot, ring_s.at[i, s], ring_r.at[i, s], device_id={"dp": nxt}, device_id_type=MESH)
                c.start(); started.append(c)
            c = pltpu.make_async_remote_copy(src, slot, sib_s.at[i, s], sib_r.at[i, s], device_id={"dp": sib}, device_id_type=MESH)
            c.start(); started.append(c)
    for c in started: c.wait_send()
    for s in range(n):
        theirs = dev_at(pos + step * s, 1 - core)
        for i in range(ns):
            slot = fulls[i].at[theirs]
            pltpu.make_async_remote_copy(slot, slot, sib_s.at[i, s], sib_r.at[i, s], device_id={"dp": sib}, device_id_type=MESH).wait_recv()
    for c in locs: c.wait()
    ocols = pl.ds(pl.multiple_of((1 - mp) * W, 128), W)
    for c in mps: c.wait_send()
    for i, d in enumerate((act_full.at[:, :, :, ocols], par_full.at[:, ocols])):
        pltpu.make_async_remote_copy(d, d, mp_s.at[i], mp_r.at[i], device_id={"mp": 1 - mp}, device_id_type=MESH).wait_recv()

def ag(shards, act, par, ndp):
    n = ndp // 2
    ns = len(shards)
    hb = pl.BlockSpec(memory_space=pl.ANY)
    outs = [jax.ShapeDtypeStruct((ndp,) + s.shape, s.dtype) for s in shards]
    outs += [jax.ShapeDtypeStruct(act.shape[:-1] + (2 * act.shape[-1],), act.dtype), jax.ShapeDtypeStruct((par.shape[0], 2 * par.shape[1]), par.dtype)]
    return pl.pallas_call(functools.partial(ag_kernel, n, ns), out_shape=outs, in_specs=[hb] * (ns + 2), out_specs=[hb] * (ns + 2),
        scratch_shapes=[pltpu.SemaphoreType.DMA((ns, n)), pltpu.SemaphoreType.DMA((ns, n)), pltpu.SemaphoreType.DMA((ns, n)), pltpu.SemaphoreType.DMA((ns, n)),
                        pltpu.SemaphoreType.DMA((ns + 2,)), pltpu.SemaphoreType.DMA((2,)), pltpu.SemaphoreType.DMA((2,))],
        compiler_params=pltpu.CompilerParams(collective_id=0, has_side_effects=True), name="gather")(*shards, act, par)


def rs_kernel(n, ns, *refs):
    gins, par, outs, par_out = refs[:ns], refs[ns], refs[ns + 1:2 * ns + 1], refs[2 * ns + 1]
    k = 2 * ns + 2
    owns, sibs, rrs = refs[k:k + ns], refs[k + ns:k + 2 * ns], refs[k + 2 * ns:k + 3 * ns]
    pall, ring_s, ring_r, sib_s, sib_r, loc = refs[k + 3 * ns:]
    me, core, pos, step, dev_at = ring_place(n)
    nxt, prv, sib = dev_at(pos + step, core), dev_at(pos - step, core), me + 1 - 2 * core
    bar = pltpu.get_barrier_semaphore()
    for d in (nxt, prv, sib):
        pl.semaphore_signal(bar, inc=1, device_id={"dp": d}, device_id_type=MESH)
    def rc(src, dst, s, r, d):
        return pltpu.make_async_remote_copy(src, dst, s, r, device_id={"dp": d}, device_id_type=MESH)
    loads = {}
    for j in range(n):
        for i in range(ns):
            c = pltpu.make_async_copy(gins[i].at[dev_at(pos - step * (1 + j), core)], owns[i].at[j], loc.at[i, j])
            c.start(); loads[i, j] = c
    pall[pl.ds(me, 1)] = par[...][None]
    pl.semaphore_wait(bar, 3)
    sends = []
    for j in range(n):
        for i in range(ns):
            c = rc(gins[i].at[dev_at(pos + step * (1 + j), 1 - core)], sibs[i].at[j], sib_s.at[i, j], sib_r.at[i, j], sib)
            c.start(); sends.append(c)
    for j in range(n):
        mine = dev_at(pos - step * j, core)
        slot = pall.at[pl.ds(mine, 1)]
        if j > 0:
            rc(slot, slot, ring_s.at[ns, j - 1], ring_r.at[ns, j - 1], nxt).wait_recv()
        if j < n - 1:
            c = rc(slot, slot, ring_s.at[ns, j], ring_r.at[ns, j], nxt)
            c.start(); sends.append(c)
        c = rc(slot, slot, sib_s.at[ns, j], sib_r.at[ns, j], sib)
        c.start(); sends.append(c)
        for i in range(ns):
            loads[i, j].wait()
            sb = sibs[i].at[j]
            rc(sb, sb, sib_s.at[i, j], sib_r.at[i, j], sib).wait_recv()
            if j > 0:
                rb = rrs[i].at[j - 1]
                rc(rb, rb, ring_s.at[i, j - 1], ring_r.at[i, j - 1], nxt).wait_recv()
            rows, cols = owns[i].shape[1:]
            tm = 16
            def tile(t, c, i=i, j=j):
                at = pl.ds(pl.multiple_of(t * tm, tm), tm)
                v = owns[i][j, at, :].astype(F32) + sibs[i][j, at, :].astype(F32)
                if j > 0:
                    v = v + rrs[i][j - 1, at, :].astype(F32)
                if j < n - 1:
                    sibs[i][j, at, :] = v.astype(BF16)
                else:
                    outs[i][at, :] = v
                return c
            lax.fori_loop(0, rows // tm, tile, 0)
            if j < n - 1:
                c = rc(sibs[i].at[j], rrs[i].at[j], ring_s.at[i, j], ring_r.at[i, j], nxt)
                c.start(); sends.append(c)
    for j in range(n):
        slot = pall.at[pl.ds(dev_at(pos + step * j, 1 - core), 1)]
        rc(slot, slot, sib_s.at[ns, j], sib_r.at[ns, j], sib).wait_recv()
    par_out[...] = jnp.sum(pall[...], axis=0)
    for c in sends:
        c.wait_send()

def rs(gins, par, ndp):
    n, ns = ndp // 2, len(gins)
    hb, vm = pl.BlockSpec(memory_space=pl.ANY), pl.BlockSpec(memory_space=pltpu.VMEM)
    sh = [g.shape[1:] for g in gins]
    return pl.pallas_call(functools.partial(rs_kernel, n, ns),
        out_shape=[jax.ShapeDtypeStruct(s, F32) for s in sh] + [jax.ShapeDtypeStruct(par.shape, F32)],
        in_specs=[hb] * ns + [vm], out_specs=[vm] * (ns + 1),
        scratch_shapes=[pltpu.VMEM((n,) + s, BF16) for s in sh] * 2 + [pltpu.VMEM((n - 1,) + s, BF16) for s in sh]
            + [pltpu.VMEM((ndp,) + par.shape, F32)] + [pltpu.SemaphoreType.DMA((ns + 1, n))] * 4 + [pltpu.SemaphoreType.DMA((ns, n))],
        compiler_params=pltpu.CompilerParams(collective_id=2, has_side_effects=True, vmem_limit_bytes=48 << 20), name="scatter")(*gins, par)


def taps_in(weight):
    blocks = weight.reshape(-1, 8, 48, 8, 48)
    return blocks.transpose(0, 3, 2, 1, 4).reshape(-1, 384, 384)


def taps_out(grad):
    blocks = grad.reshape(-1, 8, 48, 8, 48)
    return blocks.transpose(0, 3, 2, 1, 4).reshape(-1, 384)


def body(ndp, frames, segment_ids, live, conv_weight, qkv_weight, out_weight, up_weight, down_weight,
         up_bias, gains, biases, out_grad):
    regular = conv_weight.shape[0] == 384 and qkv_weight.shape[0] == 48
    wa = jnp.concatenate([qkv_weight.reshape(-1, 3 * H), out_weight.T], axis=1)
    wb = jnp.concatenate([up_weight, down_weight.T], axis=1)
    act = jnp.stack([frames, out_grad])
    par = jnp.concatenate([gains, biases, jnp.zeros((5, H), F32)], axis=0)
    if regular:
        convw, wa, wb, act, par = ag((taps_in(conv_weight)[0], wa, wb), act, par, ndp)
    else:
        convw = taps_in(lax.all_gather(conv_weight, "dp", axis=0, tiled=True))
        wa, wb = (lax.all_gather(w, "dp", axis=0, tiled=True).reshape(16, 48, -1) for w in (wa, wb))
        act, par = (lax.all_gather(w, "mp", axis=w.ndim - 1, tiled=True) for w in (act, par))
    mixed, grad_in, g_conv, g_a, g_b, sums = mid(
        convw, wa, wb, act, par, up_bias[None], segment_ids[:, :, None], segment_ids[:, None], live[:, :, None]
    )
    if regular:
        g_conv, g_a, g_b, sums = rs((g_conv, g_a, g_b), sums, ndp)
        g_conv = taps_out(g_conv)
    else:
        g_conv, g_a, g_b = (
            lax.psum_scatter(g, "dp", scatter_dimension=0, tiled=True).astype(F32)
            for g in (taps_out(g_conv), g_a.reshape(D, -1), g_b.reshape(D, -1))
        )
        sums = lax.psum(sums, "dp")
    return (
        mixed,
        grad_in,
        g_conv,
        g_a[:, :1152].reshape(-1, 3, H),
        g_a[:, 1152:].T,
        g_b[:, :FF],
        g_b[:, FF:].T,
        sums[12:16].reshape(FF),
        sums[0:3],
        sums[3:11],
    )


def solution(mesh):
    placed = (
        P("dp", None, "mp"),
        P("dp", None),
        P("dp", None),
        P("dp", "mp"),
        P("dp", None, "mp"),
        P("mp", "dp"),
        P("dp", "mp"),
        P("mp", "dp"),
        P("mp"),
        P(None, "mp"),
        P(None, "mp"),
        P("dp", None, "mp"),
    )
    return jax.shard_map(
        functools.partial(body, mesh.shape["dp"]),
        mesh=mesh,
        in_specs=placed,
        out_specs=(
            P("dp", None, "mp"),
            P("dp", None, "mp"),
            P("dp", "mp"),
            P("dp", None, "mp"),
            P("mp", "dp"),
            P("dp", "mp"),
            P("mp", "dp"),
            P("mp"),
            P(None, "mp"),
            P(None, "mp"),
        ),
        check_vma=False,
    )
```

```python
import functools

import jax
import jax.numpy as jnp
from jax import lax
from jax.experimental import pallas as pl
from jax.experimental.pallas import tpu as pltpu
from jax.sharding import PartitionSpec as P

MESH = pl.DeviceIdType.MESH
F32, BF16 = jnp.float32, jnp.bfloat16
D, H, FF, HD = 768, 384, 1536, 64
R, T, L = 2, 320, 384
NB, GW, NA = 8, 48, 16
TM = 64
EPS = 1e-5
QKV, OUT, UP, DOWN = 0, 1152, 1536, 3072
NN = (((1,), (0,)), ((), ()))
NT = (((1,), (1,)), ((), ()))
TN = (((0,), (0,)), ((), ()))

def mm(a, b, dims=NN):
    return lax.dot_general(a, b, dims, preferred_element_type=F32)

def gelu_both(v):
    p = 0.5 + 0.5 * lax.erf(v * 0.7071067811865476)
    return v * p, p + v * (0.3989422804014327 * jnp.exp(-0.5 * v * v))

def tiles(body, count=T // TM, init=0):
    return lax.fori_loop(0, count, body, init)

def at(i, size=TM):
    return pl.ds(pl.multiple_of(i * size, size), size)

class Mid:
    def shift_inputs(self, g):
        rows = at(g, GW)
        for r in range(R):
            xg = self.xt[r, rows, :]
            for a in range(NA):
                sh = (64 - 8 * a) % L
                v = pltpu.roll(xg, sh, axis=1) if sh else xg
                self.x16[a * GW:(a + 1) * GW, r * L:(r + 1) * L] = v.astype(BF16)

    def turn_in(self, dst, r, rows):
        dst[r] = jnp.concatenate([rows, jnp.zeros((L - T, H), F32)], axis=0).T

    def lanes(self, ref, r):
        return jnp.concatenate([ref[r:r + 1, :].astype(F32), jnp.zeros((1, L - T), F32)], axis=1)

    def turn_frames(self):
        for r in range(R):
            self.turn_in(self.xt, r, self.act[0, r, :, self.own].astype(F32))
            self.xt[r] = self.xt[r] * self.lanes(self.live, r)

    def conv_forward(self):

        def group(g, c):
            self.shift_inputs(g)
            w = self.convw[:, at(g, GW), :].reshape(NA * GW, NB * GW)
            y = mm(w, self.x16[...], TN)
            for r in range(R):
                acc = y[0:GW, r * L:(r + 1) * L]
                for b in range(1, NB):
                    acc = acc + pltpu.roll(y[b * GW:(b + 1) * GW, r * L:(r + 1) * L], L - b, axis=1)
                self.ot[r, at(g, GW), :] = acc
            return c
        for q in range(4):
            lax.fori_loop(2 * q, 2 * q + 2, group, 0)
            self.pump(2)

    def conv_finish(self, r):
        v = self.ot[r].T[:T] + self.par[3:4, self.own]
        gel, dg = gelu_both(v)
        self.dconv[r] = dg
        self.gc[r, :, self.own] = gel.astype(BF16)

    def norm_first(self, r):
        def tile(i, c):
            v = self.act[0, r, at(i), :].astype(F32) + self.gc[r, at(i), :].astype(F32)
            cen = v - jnp.sum(v, axis=1, keepdims=True) * (1.0 / D)
            inv = lax.rsqrt(jnp.sum(cen * cen, axis=1, keepdims=True) * (1.0 / D) + EPS)
            xh = cen * inv
            n = xh * self.par[0:1, :] + self.par[4:5, :]
            self.xh0[r, at(i), :] = xh
            self.inv0[r, at(i), :] = inv
            self.fn[r, at(i), :] = n
            self.flow[r, at(i), :] = n.astype(BF16)
            return c
        tiles(tile)

    def wall_cols(self, start, size):
        return self.wall[:, :, pl.ds(start, size)].reshape(D, size)

    def wall_rows(self, n, start, size):
        return self.wall[pl.ds(n * 8, 8), :, start:start + size].reshape(H, size)

    def project(self, r):
        for c in range(3):
            v = mm(self.flow[r], self.wall_cols(QKV + c * H, H))
            if c != 1:
                v = v + self.par[5 + c // 2:6 + c // 2, self.own]
            self.qkv[r, :, c * H:(c + 1) * H] = v.astype(BF16)
            self.pump()

    def lane_masks(self):
        lane = lax.broadcasted_iota(jnp.int32, (1, 128), 1)
        return [(lane < HD).astype(F32).astype(BF16), (lane >= HD).astype(F32).astype(BF16)]

    def pair(self, ref, r, p, c=0):
        return ref[r, :, p * 128 + c * H:p * 128 + c * H + 128]

    def attend(self, r):
        masks = self.lane_masks()
        ids = self.lanes(self.seg, r)
        same = jnp.broadcast_to(ids, (128, L)).T[:T, 0:1] == ids[:, :T]

        for p in range(3):
            q, k, v = (self.pair(self.qkv, r, p, i) for i in range(3))
            acc = None
            for h in range(2):
                s = mm(q * masks[h], k, NT) * 0.125
                s = jnp.where(same, s, -1e30)
                w = jnp.exp(s - jnp.max(s, axis=1, keepdims=True))
                pr = (w * (1.0 / jnp.sum(w, axis=1, keepdims=True))).astype(BF16)
                self.big[r * 6 + p * 2 + h, 0:T, 0:T] = pr
                o = mm(pr, v * masks[h])
                acc = o if acc is None else acc + o
            self.ctx[r, :, p * 128:(p + 1) * 128] = acc.astype(BF16)
            self.pump()
        for n in range(2):
            self.a_own[r, :, n * H:(n + 1) * H] = mm(self.ctx[r], self.wall_rows(n, OUT, H), NT).astype(BF16)

    def norm_second(self, r):
        def tile(i, c):
            v = self.fn[r, at(i), :] + (self.a_own[r, at(i), :].astype(F32) + self.a_peer[r, at(i), :].astype(F32)) + self.par[7:8, :]
            cen = v - jnp.sum(v, axis=1, keepdims=True) * (1.0 / D)
            inv = lax.rsqrt(jnp.sum(cen * cen, axis=1, keepdims=True) * (1.0 / D) + EPS)
            xh = cen * inv
            n = xh * self.par[1:2, :] + self.par[8:9, :]
            self.xh1[r, at(i), :] = xh
            self.inv1[r, at(i), :] = inv
            self.sn[r, at(i), :] = n
            self.slow[r, at(i), :] = n.astype(BF16)
            return c
        tiles(tile)

    def feed_forward(self, r):
        for n in range(4):
            u = mm(self.slow[r], self.wall_cols(UP + n * H, H)) + self.upb[:, n * H:(n + 1) * H]
            gel, dg = gelu_both(u)
            self.hid[r, :, n * H:(n + 1) * H] = gel.astype(BF16)
            self.dg[r, :, n * H:(n + 1) * H] = dg.astype(BF16)
        for n in range(2):
            self.b_own[r, :, n * H:(n + 1) * H] = mm(self.hid[r], self.wall_rows(n, DOWN, FF), NT).astype(BF16)

    def add_sums(self, row, value):
        self.psum[row:row + 1, :] += value

    def norm_third(self, r):
        def tile(i, c):
            v = self.sn[r, at(i), :] + (self.b_own[r, at(i), :].astype(F32) + self.b_peer[r, at(i), :].astype(F32)) + self.par[9:10, :]
            cen = v - jnp.sum(v, axis=1, keepdims=True) * (1.0 / D)
            inv = lax.rsqrt(jnp.sum(cen * cen, axis=1, keepdims=True) * (1.0 / D) + EPS)
            xh = cen * inv
            self.mixf[...] = xh * self.par[2:3, :] + self.par[10:11, :]
            self.mixed[r, at(i), :] = self.mixf[:, self.own].astype(BF16)
            e = self.act[1, r, at(i), :].astype(F32)
            sc = e * self.par[2:3, :]
            ex = e * xh
            m1 = jnp.sum(sc, axis=1, keepdims=True) * (1.0 / D)
            m2 = jnp.sum(sc * xh, axis=1, keepdims=True) * (1.0 / D)
            g = inv * (sc - m1 - xh * m2)
            self.sn[r, at(i), :] = g
            self.gdl[r, at(i), :] = g.astype(BF16)
            sums = [jnp.sum(w, axis=0, keepdims=True) for w in (ex, e, g)]
            return tuple(x + y for x, y in zip(c, sums))
        z = jnp.zeros((1, D), F32)
        s = tiles(tile, init=(z, z, z))
        for row, val in zip((2, 10, 9), s):
            self.add_sums(row, val)

    def feed_backward(self, r):
        for n in range(4):
            gh = mm(self.gdl[r], self.wall_cols(DOWN + n * H, H))
            g = (gh * self.dg[r, :, n * H:(n + 1) * H].astype(F32)).astype(BF16)
            self.dg[r, :, n * H:(n + 1) * H] = g
            self.pub[n:n + 1, :] += jnp.sum(g.astype(F32), axis=0, keepdims=True)
        for n in range(2):
            self.a_own[r, :, n * H:(n + 1) * H] = mm(self.dg[r], self.wall_rows(n, UP, FF), NT).astype(BF16)

    def weight_grad(self, src, other, count, start):
        for n in range(count):
            o = other[:, :, n * H:(n + 1) * H].reshape(R * T, H)
            g = mm(src[...].reshape(R * T, D), o, TN)
            self.wall[:, :, start + n * H:start + (n + 1) * H] = g.reshape(16, 48, H).astype(BF16)

    def norm_second_back(self, r):
        def tile(i, c):
            e = self.sn[r, at(i), :] + (self.a_own[r, at(i), :].astype(F32) + self.a_peer[r, at(i), :].astype(F32))
            xh = self.xh1[r, at(i), :]
            sc = e * self.par[1:2, :]
            m1 = jnp.sum(sc, axis=1, keepdims=True) * (1.0 / D)
            m2 = jnp.sum(sc * xh, axis=1, keepdims=True) * (1.0 / D)
            g = self.inv1[r, at(i), :] * (sc - m1 - xh * m2)
            self.sn[r, at(i), :] = g
            self.gal[r, at(i), :] = g.astype(BF16)
            sums = [jnp.sum(w, axis=0, keepdims=True) for w in (e * xh, e, g)]
            return tuple(x + y for x, y in zip(c, sums))
        z = jnp.zeros((1, D), F32)
        s = tiles(tile, init=(z, z, z))
        for row, val in zip((1, 8, 7), s):
            self.add_sums(row, val)

    def attend_back(self, r):
        self.gctx[r] = mm(self.gal[r], self.wall_cols(OUT, H)).astype(BF16)
        masks = self.lane_masks()

        for p in range(3):
            q, k, v = (self.pair(self.qkv, r, p, i) for i in range(3))
            go = self.pair(self.gctx, r, p)
            gq = gk = gv = None
            for h in range(2):
                gom = go * masks[h]
                gp = mm(gom, v, NT)
                pr = self.big[r * 6 + p * 2 + h, 0:T, 0:T]
                pf = pr.astype(F32)
                gs = (pf * (gp - jnp.sum(gp * pf, axis=1, keepdims=True))).astype(BF16)
                a, b, d = mm(gs, k * masks[h]), mm(gs, q * masks[h], TN), mm(pr, gom, TN)
                gq, gk, gv = (a, b, d) if gq is None else (gq + a, gk + b, gv + d)
            for i, w in enumerate((gq * 0.125, gk * 0.125, gv)):
                self.gst[r, :, p * 128 + i * H:p * 128 + i * H + 128] = w.astype(BF16)
            self.pump()
        for row, c in ((5, 0), (6, 2)):
            self.psum[row:row + 1, self.own] += jnp.sum(self.gst[r, :, c * H:(c + 1) * H].astype(F32), axis=0, keepdims=True)

    def project_back(self, r):
        po = mm(self.gst[r], self.wall_rows(1 - self.mp, QKV, 1152), NT)
        pw = mm(self.gst[r], self.wall_rows(self.mp, QKV, 1152), NT)
        self.b_own[r, :, 0:H] = po.astype(BF16)
        self.ot[r, 0:T, :] = pw
        so = po * self.par[0:1, self.oth]
        sw = pw * self.par[0:1, self.own]
        s1 = jnp.sum(so + sw, axis=1, keepdims=True)
        s2 = jnp.sum(so * self.xh0[r, :, self.oth] + sw * self.xh0[r, :, self.own], axis=1, keepdims=True)
        lane = lax.broadcasted_iota(jnp.int32, (T, 128), 1)
        st = jnp.where(lane == 0, s1, jnp.where(lane == 1, s2, 0.0))
        self.st[r] = st
        st = jnp.concatenate([st, jnp.zeros((L - T, 128), F32)], axis=0).T
        self.st_own[r] = st[0:8, :]

    def norm_first_back(self, r):
        stp = jnp.concatenate([self.st_peer[r], jnp.zeros((120, L), F32)], axis=0).T[:T]
        self.st[r] += stp
        gain = self.par[0:1, :]

        def tile(i, c):
            g1 = self.sn[r, at(i), :]
            sc1 = g1 * gain
            st = self.st[r, at(i), :]
            m1 = (jnp.sum(sc1, axis=1, keepdims=True) + st[:, 0:1]) * (1.0 / D)
            m2 = (jnp.sum(sc1 * self.xh0[r, at(i), :], axis=1, keepdims=True) + st[:, 1:2]) * (1.0 / D)
            xh = self.xh0[r, at(i), self.own]
            e = self.sn[r, at(i), self.own] + self.ot[r, at(i), :] + self.b_peer[r, at(i), 0:H].astype(F32)
            g = self.inv0[r, at(i), :] * (e * self.par[0:1, self.own] - m1 - xh * m2)
            self.gf[r, at(i), :] = g
            low = (g * self.dconv[r, at(i), :]).astype(BF16)
            lf = low.astype(F32)
            self.dconv[r, at(i), :] = lf
            sums = [jnp.sum(w, axis=0, keepdims=True) for w in (e * xh, e, lf)]
            return tuple(x + y for x, y in zip(c, sums))
        z = jnp.zeros((1, H), F32)
        s = tiles(tile, init=(z, z, z))
        for row, val in zip((0, 4, 3), s):
            self.psum[row:row + 1, self.own] += val
        self.turn_in(self.gt, r, self.dconv[r])

    def shift_grads(self, g):
        for r in range(R):
            gg = self.gt[r, at(g, GW), :]
            for b in range(NB):
                v = pltpu.roll(gg, b, axis=1) if b else gg
                self.g8[b * GW:(b + 1) * GW, r * L:(r + 1) * L] = v.astype(BF16)

    def conv_weight_grad(self, first):
        def group(g, c):
            self.shift_inputs(g)
            self.shift_grads(g)
            gr = mm(self.x16[...], self.g8[...], NT)
            self.big[:, at(g, GW), :] = gr.reshape(NA, GW, NB * GW).astype(BF16)
            return c
        lax.fori_loop(first, first + 2, group, 0)

    def conv_input_grad(self, first):
        def group(g, c):
            self.shift_grads(g)
            w = self.convw[:, at(g, GW), :].reshape(NA * GW, NB * GW)
            z = mm(w, self.g8[...])
            for r in range(R):
                acc = None
                for a in range(NA):
                    sh = (8 * a - 64) % L
                    v = z[a * GW:(a + 1) * GW, r * L:(r + 1) * L]
                    v = pltpu.roll(v, sh, axis=1) if sh else v
                    acc = v if acc is None else acc + v
                self.ot[r, at(g, GW), :] = acc
            return c
        lax.fori_loop(first, first + 2, group, 0)

    def add_input_grad(self):
        for r in range(R):
            self.gf[r] += (self.ot[r] * self.lanes(self.live, r)).T[:T]

    def put(self, i, t, v):
        rows = at(t, 16)
        if i < 4:
            self.xt[0, pl.ds(pl.multiple_of(i * 96 + t * 16, 16), 16), :] = v
        elif i == 4:
            for c in range(3):
                self.gqkv[c, rows, :] = v[:, c * H:(c + 1) * H]
            self.gout[rows, :] = v[:, OUT:UP]
        elif i == 5:
            self.gup[rows, :] = v
        else:
            self.gdown[rows, :] = v


def swap_blocks(x, buf):
    lane = lax.broadcasted_iota(jnp.int32, (GW, H), 1)
    for d in range(8):
        turned = pltpu.roll(x, GW * d, axis=1) if d else x
        for p in range(8):
            q = (p - d) % 8
            rows = turned[GW * p:GW * (p + 1), :]
            if d:
                rows = jnp.where((lane >= GW * p) & (lane < GW * (p + 1)), rows, buf[GW * q:GW * (q + 1), :])
            buf[GW * q:GW * (q + 1), :] = rows


class Ring:
    def __init__(self, n, m, sems):
        self.n, self.m = n, m
        (self.gas, self.gar, self.gbs, self.gbr, self.gss, self.gsr, self.sas, self.sar, self.sbs, self.sbr, self.sss, self.ssr) = sems
        me = lax.axis_index("dp")
        core = lax.rem(me, 2)
        chip = me // 2
        odd = lax.rem(chip, 2)
        half = chip // 2
        self.me, self.core, self.step = me, core, 1 - 2 * core
        self.pos = (1 - odd) * half + odd * (n - 1 - half)
        self.nxt = self.dev(self.step, core)
        self.prv = self.dev(-self.step, core)
        self.sib = me + self.step
        conv = lambda q: lambda d, w=m.convw: w.at[d, 96 * q:96 * (q + 1), :]
        self.views = [conv(q) for q in range(4)] + [
            lambda d: m.wall.at[d, :, 0:UP],
            lambda d: m.wall.at[d, :, UP:DOWN],
            lambda d: m.wall.at[d, :, DOWN:4608],
            lambda d: m.pall.at[pl.ds(d, 1)],
        ]
        self.out = {}

    def dev(self, k, core):
        n = self.n
        p = lax.rem(self.pos + k + 8 * n, n)
        q = p // (n // 2)
        return 2 * ((1 - q) * 2 * p + q * (2 * (n - 1 - p) + 1)) + core

    def copy(self, src, dst, send, recv, dp):
        return pltpu.make_async_remote_copy(src, dst, send, recv, device_id={"dp": dp}, device_id_type=MESH)

    def go(self, key, copy):
        copy.start()
        self.out.setdefault(key, []).append(copy)

    def sent(self, key):
        for copy in self.out.pop(key):
            copy.wait_send()

    def gather(self, i, s):
        key = ("g", i)
        ahead = (self.gas, self.gar, self.nxt, 4, -self.step, 0)
        back = (self.gbs, self.gbr, self.prv, 3, self.step, 4)
        for send, recv, to, far, way, k in (ahead, back):
            if s > far:
                continue
            slot = self.views[i](self.dev(way * s, self.core))
            if s > 0:
                self.copy(slot, slot, send.at[i, s - 1], recv.at[i, s - 1], to).wait_recv()
            if s < far:
                self.go(key, self.copy(slot, slot, send.at[i, s], recv.at[i, s], to))
            if s > 0 or k == 0:
                self.go(key, self.copy(slot, slot, self.gss.at[i, k + s], self.gsr.at[i, k + s], self.sib))

    def gathered(self, i):
        for k, way in [(s, self.step * s) for s in range(5)] + [(4 + s, -self.step * s) for s in range(1, 4)]:
            slot = self.views[i](self.dev(way, 1 - self.core))
            self.copy(slot, slot, self.gss.at[i, k], self.gsr.at[i, k], self.sib).wait_recv()
        self.sent(("g", i))

    def grads(self, i, d):
        if i < 4:
            return self.m.big.at[d, 96 * i:96 * (i + 1), :]
        return self.views[i](d)

    def scatter_begin(self, i):
        for k, way in ((0, -4), (4, 3), (1, -3), (5, 2), (2, -2), (6, 1), (3, -1), (7, 0)):
            src = self.grads(i, self.dev(way * self.step, 1 - self.core))
            self.go(("s", i), self.copy(src, self.m.sb[i].at[k], self.sss.at[i, k], self.ssr.at[i, k], self.sib))

    def scatter(self, i, j):
        sb, rr = self.m.sb[i], self.m.rr[i]
        ahead = (self.sas, self.sar, self.nxt, 4, self.step, 0)
        back = (self.sbs, self.sbr, self.prv, 3, -self.step, 4)
        if j < 4:
            for send, recv, to, far, way, k in (ahead, back):
                if j >= far:
                    continue
                terms = []
                if j > 0:
                    terms.append(rr.at[k + j - 1])
                    self.copy(terms[0], terms[0], send.at[i, j - 1], recv.at[i, j - 1], to).wait_recv()
                self.add(i, k + j, self.dev(way * (far - j), self.core), terms, sb.at[k + j])
                self.go(("s", i), self.copy(sb.at[k + j], rr.at[k + j], send.at[i, j], recv.at[i, j], to))
        else:
            terms = [rr.at[3], rr.at[6]]
            self.copy(terms[0], terms[0], self.sas.at[i, 3], self.sar.at[i, 3], self.nxt).wait_recv()
            self.copy(terms[1], terms[1], self.sbs.at[i, 2], self.sbr.at[i, 2], self.prv).wait_recv()
            self.add(i, 7, self.me, terms, None)

    def add(self, i, k, dev, terms, into):
        held = self.m.sb[i].at[k]
        self.copy(held, held, self.sss.at[i, k], self.ssr.at[i, k], self.sib).wait_recv()
        mine = self.grads(i, dev)

        def tile(t, c):
            rows = at(t, 16)
            v = mine[rows, :].astype(F32) + held[rows, :].astype(F32)
            for term in terms:
                v = v + term[rows, :].astype(F32)
            if into is None:
                self.m.put(i, t, v)
            else:
                into[rows, :] = v.astype(BF16)
            return c
        tiles(tile, held.shape[0] // 16)


SCRATCH = dict(
    act=((2, R, T, D), BF16), par=((16, D), F32),
    convw=((16, H, H), BF16), wall=((16, 48, 4608), BF16),
    xt=((R, H, L), F32), ot=((R, H, L), F32), gt=((R, H, L), F32), x16=((768, R * L), BF16), g8=((H, R * L), BF16),
    gc=((R, T, D), BF16), dconv=((R, T, H), F32), xh0=((R, T, D), F32), inv0=((R, T, 1), F32), fn=((R, T, D), F32), flow=((R, T, D), BF16),
    qkv=((R, T, 1152), BF16), big=((16, H, H), BF16), ctx=((R, T, H), BF16),
    a_own=((R, T, D), BF16), a_peer=((R, T, D), BF16), b_own=((R, T, D), BF16), b_peer=((R, T, D), BF16),
    xh1=((R, T, D), F32), inv1=((R, T, 1), F32),
    hid=((R, T, FF), BF16), dg=((R, T, FF), BF16), mixf=((TM, D), F32), gdl=((R, T, D), BF16),
    gctx=((R, T, H), BF16), gst=((R, T, 1152), BF16), st=((R, T, 128), F32),
    st_own=((R, 8, L), F32), st_peer=((R, 8, L), F32), psum=((16, D), F32), pub=((4, H), F32),
)
RING_SCRATCH = dict(pall=((16, 16, H), F32))
for _i in range(7):
    _tail = (96, H) if _i < 4 else (48, FF)
    RING_SCRATCH["sb%d" % _i] = ((8,) + _tail, BF16)
    RING_SCRATCH["rr%d" % _i] = ((7,) + _tail, BF16)
RING_INS = ("frames", "ograd", "seg", "live", "upb", "gains", "biases", "cw", "qkvw", "outw", "upw", "downw")
RING_OUTS = ("mixed", "gf", "gcw", "gqkv", "gout", "gup", "gdown", "gupb", "ggains", "gbiases")
INS = ("frames", "ograd", "seg", "live", "upb", "gains", "biases", "convw_hbm", "wa_hbm", "wb_hbm")
OUTS = ("mixed", "gf", "gconv_hbm", "ga_hbm", "gb_hbm", "pout")


def layer_kernel(ring, *refs):
    m = Mid()
    names = (RING_INS + RING_OUTS + tuple(SCRATCH) + tuple(RING_SCRATCH)) if ring else (INS + OUTS + tuple(SCRATCH))
    for name, ref in zip(names, refs):
        setattr(m, name, ref)
    loc, snd, rcv = refs[len(names):len(names) + 3]
    m.slow, m.sn, m.gal = m.gc, m.fn, m.gdl
    mp = lax.axis_index("mp")
    m.mp = mp
    m.own = pl.ds(pl.multiple_of(mp * H, 128), H)
    m.oth = pl.ds(pl.multiple_of((1 - mp) * H, 128), H)
    peer = {"mp": 1 - mp}
    bar = pltpu.get_barrier_semaphore()
    acts = [pltpu.make_async_copy(x, m.act.at[i, :, :, m.own], loc.at[i]) for i, x in enumerate((m.frames, m.ograd))]
    if ring:
        rg = Ring(8, m, refs[len(names) + 3:])
        m.sb, m.rr = ([getattr(m, "%s%d" % (w, i)) for i in range(7)] for w in ("sb", "rr"))
        loads = [pltpu.make_async_copy(m.qkvw.at[c], m.wall.at[rg.me, :, c * H:(c + 1) * H], loc.at[2 + c]) for c in range(3)]
        loads += [
            pltpu.make_async_copy(m.outw, m.wall.at[rg.me, :, OUT:UP], loc.at[5]),
            pltpu.make_async_copy(m.upw, m.wall.at[rg.me, :, UP:DOWN], loc.at[6]),
            pltpu.make_async_copy(m.downw, m.wall.at[rg.me, :, DOWN:4608], loc.at[7]),
        ]
        near = [{"dp": rg.nxt}, {"dp": rg.prv}, {"dp": rg.sib}, peer]
    else:
        loads = [
            pltpu.make_async_copy(m.convw_hbm, m.convw, loc.at[2]),
            pltpu.make_async_copy(m.wa_hbm, m.wall.at[:, :, 0:UP], loc.at[3]),
            pltpu.make_async_copy(m.wb_hbm, m.wall.at[:, :, UP:4608], loc.at[4]),
        ]
        near = [peer]
    for d in near:
        pl.semaphore_signal(bar, inc=1, device_id=d, device_id_type=MESH)
    for c in acts + loads:
        c.start()
    m.par[0:3, m.own] = m.gains[...]
    m.par[3:11, m.own] = m.biases[...]
    m.psum[...] = jnp.zeros((16, D), F32)
    m.pub[...] = jnp.zeros((4, H), F32)
    if ring:
        swap_blocks(m.cw[...].astype(F32), m.ot.at[0])
        m.convw[rg.me] = m.ot[0].astype(BF16)
    pl.semaphore_wait(bar, len(near))
    if ring:
        for q in range(4):
            rg.gather(q, 0)

    def swap(i, r, src, dst, land):
        c = pltpu.make_async_remote_copy(src, dst, snd.at[i, r], rcv.at[i, r], device_id=peer, device_id_type=MESH)
        c.start()
        return c, pltpu.make_async_remote_copy(land, land, snd.at[i, r], rcv.at[i, r], device_id=peer, device_id_type=MESH)

    pend = {}
    own, oth = m.own, m.oth
    pend[7, 0] = swap(7, 0, m.par.at[:, own], m.par.at[:, own], m.par.at[:, oth])
    for i in range(2):
        acts[i].wait()
        pend[6, i] = swap(6, i, m.act.at[i, :, :, own], m.act.at[i, :, :, own], m.act.at[i, :, :, oth])
    queue = []

    def pump(count=1):
        for f, i, s in queue[:count]:
            f(i, s)
        del queue[:count]

    m.pump = pump
    m.turn_frames()
    if ring:
        G, S = rg.gather, rg.scatter
        for s in range(1, 5):
            for q in range(4):
                G(q, s)
            if s == 2:
                for c in loads:
                    c.wait()
                G(4, 0)
            if s == 3:
                G(4, 1)
                G(5, 0)
        for q in range(4):
            rg.gathered(q)
        queue += [(G, i, s) for i, s in ((4, 2), (5, 1), (6, 0), (4, 3), (5, 2), (4, 4), (6, 1), (5, 3), (6, 2), (5, 4), (6, 3), (6, 4))]
    else:
        for c in loads:
            c.wait()
    m.conv_forward()
    for r in range(R):
        m.conv_finish(r)
        pend[0, r] = swap(0, r, m.gc.at[r, :, own], m.gc.at[r, :, own], m.gc.at[r, :, oth])
        m.pump()
    pend[7, 0][1].wait_recv()
    pend[6, 0][1].wait_recv()
    for r in range(R):
        pend[0, r][1].wait_recv()
        m.norm_first(r)
        m.pump()
        if ring and r == 0:
            rg.gathered(4)
        m.project(r)
        m.attend(r)
        pend[1, r] = swap(1, r, m.a_own.at[r], m.a_peer.at[r], m.a_peer.at[r])
    m.pump(len(queue))
    if ring:
        rg.gathered(5)
        rg.gathered(6)
    for r in range(R):
        pend[1, r][1].wait_recv()
        pend[0, r][0].wait_send()
        m.norm_second(r)
        m.feed_forward(r)
        pend[2, r] = swap(2, r, m.b_own.at[r], m.b_peer.at[r], m.b_peer.at[r])
    pend[6, 1][1].wait_recv()
    for r in range(R):
        pend[2, r][1].wait_recv()
        m.norm_third(r)
        pend[1, r][0].wait_send()
        m.feed_backward(r)
        pend[3, r] = swap(3, r, m.a_own.at[r], m.a_peer.at[r], m.a_peer.at[r])
    m.weight_grad(m.gdl, m.hid, 4, DOWN)
    if ring:
        rg.scatter_begin(6)
    m.weight_grad(m.slow, m.dg, 4, UP)
    if ring:
        rg.scatter_begin(5)
        queue += [(S, i, j) for j in range(5) for i in (6, 5)]
    else:
        gb = pltpu.make_async_copy(m.wall.at[:, :, UP:4608], m.gb_hbm, loc.at[4])
        gb.start()
    for r in range(R):
        pend[3, r][1].wait_recv()
        m.norm_second_back(r)
        m.pump(2)
        m.attend_back(r)
        pend[2, r][0].wait_send()
        m.project_back(r)
        pend[4, r] = swap(4, r, m.b_own.at[r, :, 0:H], m.b_peer.at[r, :, 0:H], m.b_peer.at[r, :, 0:H])
        pend[5, r] = swap(5, r, m.st_own.at[r], m.st_peer.at[r], m.st_peer.at[r])
    m.weight_grad(m.gal, m.ctx, 1, OUT)
    m.weight_grad(m.flow, m.gst, 3, QKV)
    if ring:
        m.pump(len(queue))
        rg.scatter_begin(4)
        S(4, 0)
    else:
        ga = pltpu.make_async_copy(m.wall.at[:, :, 0:UP], m.ga_hbm, loc.at[3])
        ga.start()
    for r in range(R):
        pend[5, r][1].wait_recv()
        pend[4, r][1].wait_recv()
        m.norm_first_back(r)
    if ring:
        S(4, 1)
        m.pall[pl.ds(rg.me, 1), 0:11, :] = m.psum[0:11, own][None]
        m.pall[pl.ds(rg.me, 1), 11:12, :] = jnp.zeros((1, 1, H), F32)
        m.pall[pl.ds(rg.me, 1), 12:16, :] = m.pub[...][None]
        G(7, 0)
        m.conv_weight_grad(0)
        rg.scatter_begin(0)
        G(7, 1)
        S(0, 0)
        m.conv_weight_grad(2)
        rg.scatter_begin(1)
        S(4, 2)
        S(0, 1)
        S(1, 0)
        m.conv_weight_grad(4)
        rg.scatter_begin(2)
        G(7, 2)
        S(4, 3)
        S(0, 2)
        S(1, 1)
        S(2, 0)
        m.conv_weight_grad(6)
        rg.scatter_begin(3)
        S(0, 3)
        S(1, 2)
        S(2, 1)
        S(3, 0)
        G(7, 3)
        S(4, 4)
        m.conv_input_grad(0)
        S(0, 4)
        S(1, 3)
        S(2, 2)
        S(3, 1)
        m.conv_input_grad(2)
        S(1, 4)
        S(2, 3)
        S(3, 2)
        G(7, 4)
        m.conv_input_grad(4)
        S(2, 4)
        S(3, 3)
        m.conv_input_grad(6)
        m.add_input_grad()
        S(3, 4)
        rg.gathered(7)
        tot = jnp.sum(m.pall[...], axis=0)
        m.ggains[...] = tot[0:3]
        m.gbiases[...] = tot[3:11]
        for k in range(4):
            m.gupb[0:1, k * H:(k + 1) * H] = tot[12 + k:13 + k]
        swap_blocks(m.xt[0], m.gcw)
        for i in range(7):
            rg.sent(("s", i))
    else:
        for g in range(0, 8, 2):
            m.conv_weight_grad(g)
            m.conv_input_grad(g)
        m.add_input_grad()
        gc = pltpu.make_async_copy(m.big, m.gconv_hbm, loc.at[2])
        gc.start()
        m.pout[0:11, :] = m.psum[0:11, own]
        m.pout[11:12, :] = jnp.zeros((1, H), F32)
        m.pout[12:16, :] = m.pub[...]
        for c in (ga, gb, gc):
            c.wait()
    for i, r in ((3, 0), (3, 1), (4, 0), (4, 1), (5, 0), (5, 1), (6, 0), (6, 1), (7, 0)):
        pend[i, r][0].wait_send()


def layer(ring, *args):
    vm, hb = pl.BlockSpec(memory_space=pltpu.VMEM), pl.BlockSpec(memory_space=pl.ANY)
    S = jax.ShapeDtypeStruct
    outs = [S((R, T, H), BF16), S((R, T, H), F32)]
    dma = pltpu.SemaphoreType.DMA
    scratch = dict(SCRATCH)
    if ring:
        scratch.update(RING_SCRATCH)
        outs += [S((H, H), F32), S((3, 48, H), F32), S((48, H), F32), S((48, FF), F32), S((48, FF), F32), S((1, FF), F32), S((3, H), F32), S((8, H), F32)]
        in_specs, out_specs = [hb] * 2 + [vm] * 6 + [hb] * 4, [vm] * 10
        sems = [dma((8,)), dma((8, R)), dma((8, R))] + [dma((8, w)) for w in (4, 4, 3, 3, 8, 8)] + [dma((7, w)) for w in (4, 4, 3, 3, 8, 8)]
    else:
        outs += [S((16, H, H), BF16), S((16, 48, UP), BF16), S((16, 48, 4608 - UP), BF16), S((16, H), F32)]
        in_specs, out_specs = [hb] * 2 + [vm] * 5 + [hb] * 3, [vm] * 2 + [hb] * 3 + [vm]
        sems = [dma((5,)), dma((8, R)), dma((8, R))]
    return pl.pallas_call(
        functools.partial(layer_kernel, ring),
        out_shape=outs,
        in_specs=in_specs,
        out_specs=out_specs,
        scratch_shapes=[pltpu.VMEM(s, d) for s, d in scratch.values()] + sems,
        compiler_params=pltpu.CompilerParams(collective_id=0, has_side_effects=True, vmem_limit_bytes=63 << 20),
        name="layer",
    )(*args)


def taps_in(weight):
    blocks = weight.reshape(-1, 8, 48, 8, 48)
    return blocks.transpose(0, 3, 2, 1, 4).reshape(-1, 384, 384)


def taps_out(grad):
    blocks = grad.reshape(-1, 8, 48, 8, 48)
    return blocks.transpose(0, 3, 2, 1, 4).reshape(-1, 384)


def body(frames, segment_ids, live, conv_weight, qkv_weight, out_weight, up_weight, down_weight,
         up_bias, gains, biases, out_grad):
    common = (frames, out_grad, segment_ids, live, up_bias[None], gains, biases)
    if conv_weight.shape[0] == 384 and qkv_weight.shape[0] == 48:
        mixed, grad_in, g_conv, g_qkv, g_out, g_up, g_down, g_upb, g_gains, g_biases = layer(
            True, *common, conv_weight, qkv_weight.transpose(1, 0, 2), out_weight.T, up_weight, down_weight.T
        )
        return (mixed, grad_in, g_conv, g_qkv.transpose(1, 0, 2), g_out.T, g_up, g_down.T, g_upb.reshape(FF), g_gains, g_biases)
    wa = jnp.concatenate([qkv_weight.reshape(-1, 3 * H), out_weight.T], axis=1)
    wb = jnp.concatenate([up_weight, down_weight.T], axis=1)
    convw = taps_in(lax.all_gather(conv_weight, "dp", axis=0, tiled=True))
    wa, wb = (lax.all_gather(w, "dp", axis=0, tiled=True).reshape(16, 48, -1) for w in (wa, wb))
    mixed, grad_in, g_conv, g_a, g_b, sums = layer(False, *common, convw, wa, wb)
    g_conv, g_a, g_b = (
        lax.psum_scatter(g, "dp", scatter_dimension=0, tiled=True).astype(F32)
        for g in (taps_out(g_conv), g_a.reshape(D, -1), g_b.reshape(D, -1))
    )
    sums = lax.psum(sums, "dp")
    return (
        mixed,
        grad_in,
        g_conv,
        g_a[:, :OUT].reshape(-1, 3, H),
        g_a[:, OUT:].T,
        g_b[:, :FF],
        g_b[:, FF:].T,
        sums[12:16].reshape(FF),
        sums[0:3],
        sums[3:11],
    )


def solution(mesh):
    placed = (
        P("dp", None, "mp"),
        P("dp", None),
        P("dp", None),
        P("dp", "mp"),
        P("dp", None, "mp"),
        P("mp", "dp"),
        P("dp", "mp"),
        P("mp", "dp"),
        P("mp"),
        P(None, "mp"),
        P(None, "mp"),
        P("dp", None, "mp"),
    )
    return jax.shard_map(
        body,
        mesh=mesh,
        in_specs=placed,
        out_specs=(
            P("dp", None, "mp"),
            P("dp", None, "mp"),
            P("dp", "mp"),
            P("dp", None, "mp"),
            P("mp", "dp"),
            P("dp", "mp"),
            P("mp", "dp"),
            P("mp"),
            P(None, "mp"),
            P(None, "mp"),
        ),
        check_vma=False,
    )
```

```python
import functools

import jax
import jax.numpy as jnp
from jax import lax
from jax.experimental import pallas as pl
from jax.experimental.pallas import tpu as pltpu
from jax.sharding import PartitionSpec as P

MESH = pl.DeviceIdType.MESH
F32, BF16 = jnp.float32, jnp.bfloat16
D, H, FF, HD = 768, 384, 1536, 64
R, T, L = 2, 320, 384
NB, GW, NA = 8, 48, 16
TM = 64
EPS = 1e-5
THEIRS, QKV, OUT, UP, DOWN, ALL = 0, 384, 1536, 1920, 3456, 4992
NN = (((1,), (0,)), ((), ()))
NT = (((1,), (1,)), ((), ()))
TN = (((0,), (0,)), ((), ()))

def mm(a, b, dims=NN):
    return lax.dot_general(a, b, dims, preferred_element_type=F32)

def gelu_both(v):
    p = 0.5 + 0.5 * lax.erf(v * 0.7071067811865476)
    return v * p, p + v * (0.3989422804014327 * jnp.exp(-0.5 * v * v))

def tiles(body, count=T // TM, init=0):
    return lax.fori_loop(0, count, body, init)

def at(i, size=TM):
    return pl.ds(pl.multiple_of(i * size, size), size)

class Mid:
    def shift_inputs(self, g):
        rows = at(g, GW)
        for r in range(R):
            xg = self.xt[r, rows, :]
            for a in range(NA):
                sh = (64 - 8 * a) % L
                v = pltpu.roll(xg, sh, axis=1) if sh else xg
                self.x16[a * GW:(a + 1) * GW, r * L:(r + 1) * L] = v.astype(BF16)

    def turn_in(self, dst, r, rows):
        dst[r] = jnp.concatenate([rows, jnp.zeros((L - T, H), F32)], axis=0).T

    def lanes(self, ref, r):
        return jnp.concatenate([ref[r:r + 1, :].astype(F32), jnp.zeros((1, L - T), F32)], axis=1)

    def turn_frames(self):
        for r in range(R):
            self.turn_in(self.xt, r, self.act[0, r, :, self.own].astype(F32))
            self.xt[r] = self.xt[r] * self.lanes(self.live, r)

    def conv_forward(self):

        def group(g, c):
            self.shift_inputs(g)
            w = self.convw[:, at(g, GW), :].reshape(NA * GW, NB * GW)
            y = mm(w, self.x16[...], TN)
            for r in range(R):
                acc = y[0:GW, r * L:(r + 1) * L]
                for b in range(1, NB):
                    acc = acc + pltpu.roll(y[b * GW:(b + 1) * GW, r * L:(r + 1) * L], L - b, axis=1)
                self.ot[r, at(g, GW), :] = acc
            return c
        tiles(group, 8)
    def conv_finish(self, r):
        v = self.ot[r].T[:T] + self.par[3:4, self.own]
        gel, dg = gelu_both(v)
        self.dconv[r] = dg
        self.gc[r, :, self.own] = gel.astype(BF16)

    def norm_first(self, r):
        def tile(i, c):
            v = self.act[0, r, at(i), :].astype(F32) + self.gc[r, at(i), :].astype(F32)
            cen = v - jnp.sum(v, axis=1, keepdims=True) * (1.0 / D)
            inv = lax.rsqrt(jnp.sum(cen * cen, axis=1, keepdims=True) * (1.0 / D) + EPS)
            xh = cen * inv
            n = xh * self.par[0:1, :] + self.par[4:5, :]
            self.xh0[r, at(i), :] = xh
            self.inv0[r, at(i), :] = inv
            self.fn[r, at(i), :] = n
            self.flow[r, at(i), :] = n.astype(BF16)
            return c
        tiles(tile)

    def wall_cols(self, start, size):
        return self.wall[:, :, pl.ds(start, size)].reshape(D, size)

    def wall_rows(self, n, start, size):
        return self.wall[pl.ds(n * 8, 8), :, start:start + size].reshape(H, size)

    def project(self, r):
        for c in range(3):
            v = mm(self.flow[r], self.wall_cols(QKV + c * H, H))
            if c != 1:
                v = v + self.par[5 + c // 2:6 + c // 2, self.own]
            self.qkv[r, :, c * H:(c + 1) * H] = v.astype(BF16)

    def lane_masks(self):
        lane = lax.broadcasted_iota(jnp.int32, (1, 128), 1)
        return [(lane < HD).astype(F32).astype(BF16), (lane >= HD).astype(F32).astype(BF16)]

    def pair(self, ref, r, p, c=0):
        return ref[r, :, p * 128 + c * H:p * 128 + c * H + 128]

    def attend(self, r):
        masks = self.lane_masks()
        ids = self.lanes(self.seg, r)
        same = jnp.broadcast_to(ids, (128, L)).T[:T, 0:1] == ids[:, :T]

        for p in range(3):
            q, k, v = (self.pair(self.qkv, r, p, i) for i in range(3))
            acc = None
            for h in range(2):
                s = mm(q * masks[h], k, NT) * 0.125
                s = jnp.where(same, s, -1e30)
                w = jnp.exp(s - jnp.max(s, axis=1, keepdims=True))
                pr = (w * (1.0 / jnp.sum(w, axis=1, keepdims=True))).astype(BF16)
                self.big[r * 6 + p * 2 + h, 0:T, 0:T] = pr
                o = mm(pr, v * masks[h])
                acc = o if acc is None else acc + o
            self.ctx[r, :, p * 128:(p + 1) * 128] = acc.astype(BF16)

    def add_attended(self, r, ctx, start):
        for n in range(2):
            self.fn[r, :, n * H:(n + 1) * H] += mm(ctx, self.wall_rows(n, start, H), NT)

    def norm_second(self, r):
        def tile(i, c):
            v = self.fn[r, at(i), :] + self.par[7:8, :]
            cen = v - jnp.sum(v, axis=1, keepdims=True) * (1.0 / D)
            inv = lax.rsqrt(jnp.sum(cen * cen, axis=1, keepdims=True) * (1.0 / D) + EPS)
            xh = cen * inv
            n = xh * self.par[1:2, :] + self.par[8:9, :]
            self.xh1[r, at(i), :] = xh
            self.inv1[r, at(i), :] = inv
            self.sn[r, at(i), :] = n
            self.slow[r, at(i), :] = n.astype(BF16)
            return c
        tiles(tile)

    def feed_up(self, r):
        for n in range(4):
            u = mm(self.slow[r], self.wall_cols(UP + n * H, H)) + self.upb[n * H:(n + 1) * H].reshape(1, H)
            gel, dg = gelu_both(u)
            self.hid[r, :, n * H:(n + 1) * H] = gel.astype(BF16)
            self.dg[r, :, n * H:(n + 1) * H] = dg.astype(BF16)

    def feed_down(self, r):
        for n in range(2):
            self.b_own[r, :, n * H:(n + 1) * H] = mm(self.hid[r], self.wall_rows(n, DOWN, FF), NT).astype(BF16)

    def add_sums(self, row, value):
        self.psum[row:row + 1, :] += value

    def norm_third(self, r):
        def tile(i, c):
            v = self.sn[r, at(i), :] + (self.b_own[r, at(i), :].astype(F32) + self.b_peer[r, at(i), :].astype(F32)) + self.par[9:10, :]
            cen = v - jnp.sum(v, axis=1, keepdims=True) * (1.0 / D)
            inv = lax.rsqrt(jnp.sum(cen * cen, axis=1, keepdims=True) * (1.0 / D) + EPS)
            xh = cen * inv
            self.mixf[...] = xh * self.par[2:3, :] + self.par[10:11, :]
            self.mixed[r, at(i), :] = self.mixf[:, self.own].astype(BF16)
            e = self.act[1, r, at(i), :].astype(F32)
            sc = e * self.par[2:3, :]
            ex = e * xh
            m1 = jnp.sum(sc, axis=1, keepdims=True) * (1.0 / D)
            m2 = jnp.sum(sc * xh, axis=1, keepdims=True) * (1.0 / D)
            g = inv * (sc - m1 - xh * m2)
            self.sn[r, at(i), :] = g
            self.gdl[r, at(i), :] = g.astype(BF16)
            sums = [jnp.sum(w, axis=0, keepdims=True) for w in (ex, e, g)]
            return tuple(x + y for x, y in zip(c, sums))
        z = jnp.zeros((1, D), F32)
        s = tiles(tile, init=(z, z, z))
        for row, val in zip((2, 10, 9), s):
            self.add_sums(row, val)

    def feed_backward(self, r):
        for n in range(4):
            gh = mm(self.gdl[r], self.wall_cols(DOWN + n * H, H))
            g = (gh * self.dg[r, :, n * H:(n + 1) * H].astype(F32)).astype(BF16)
            self.dg[r, :, n * H:(n + 1) * H] = g
            self.pub[n:n + 1, :] += jnp.sum(g.astype(F32), axis=0, keepdims=True)

    def feed_back_up(self, r):
        for n in range(2):
            self.a_own[r, :, n * H:(n + 1) * H] = mm(self.dg[r], self.wall_rows(n, UP, FF), NT).astype(BF16)

    def weight_grad(self, src, other, count, start):
        for n in range(count):
            o = other[:, :, n * H:(n + 1) * H].reshape(R * T, H)
            g = mm(src[...].reshape(R * T, D), o, TN)
            self.wall[:, :, start + n * H:start + (n + 1) * H] = g.reshape(16, 48, H).astype(BF16)

    def norm_second_back(self, r):
        def tile(i, c):
            e = self.sn[r, at(i), :] + (self.a_own[r, at(i), :].astype(F32) + self.a_peer[r, at(i), :].astype(F32))
            xh = self.xh1[r, at(i), :]
            sc = e * self.par[1:2, :]
            m1 = jnp.sum(sc, axis=1, keepdims=True) * (1.0 / D)
            m2 = jnp.sum(sc * xh, axis=1, keepdims=True) * (1.0 / D)
            g = self.inv1[r, at(i), :] * (sc - m1 - xh * m2)
            self.sn[r, at(i), :] = g
            self.gal[r, at(i), :] = g.astype(BF16)
            sums = [jnp.sum(w, axis=0, keepdims=True) for w in (e * xh, e, g)]
            return tuple(x + y for x, y in zip(c, sums))
        z = jnp.zeros((1, D), F32)
        s = tiles(tile, init=(z, z, z))
        for row, val in zip((1, 8, 7), s):
            self.add_sums(row, val)

    def attend_back(self, r):
        self.gctx[r] = mm(self.gal[r], self.wall_cols(OUT, H)).astype(BF16)
        masks = self.lane_masks()

        for p in range(3):
            q, k, v = (self.pair(self.qkv, r, p, i) for i in range(3))
            go = self.pair(self.gctx, r, p)
            gq = gk = gv = None
            for h in range(2):
                gom = go * masks[h]
                gp = mm(gom, v, NT)
                pr = self.big[r * 6 + p * 2 + h, 0:T, 0:T]
                pf = pr.astype(F32)
                gs = (pf * (gp - jnp.sum(gp * pf, axis=1, keepdims=True))).astype(BF16)
                a, b, d = mm(gs, k * masks[h]), mm(gs, q * masks[h], TN), mm(pr, gom, TN)
                gq, gk, gv = (a, b, d) if gq is None else (gq + a, gk + b, gv + d)
            for i, w in enumerate((gq * 0.125, gk * 0.125, gv)):
                self.gst[r, :, p * 128 + i * H:p * 128 + i * H + 128] = w.astype(BF16)
        for row, c in ((5, 0), (6, 2)):
            self.psum[row:row + 1, self.own] += jnp.sum(self.gst[r, :, c * H:(c + 1) * H].astype(F32), axis=0, keepdims=True)

    def project_back(self, r):
        po = mm(self.gst[r], self.wall_rows(1 - self.mp, QKV, 1152), NT)
        pw = mm(self.gst[r], self.wall_rows(self.mp, QKV, 1152), NT)
        self.b_own[r, :, 0:H] = po.astype(BF16)
        self.ot[r, 0:T, :] = pw
        so = po * self.par[0:1, self.oth]
        sw = pw * self.par[0:1, self.own]
        s1 = jnp.sum(so + sw, axis=1, keepdims=True)
        s2 = jnp.sum(so * self.xh0[r, :, self.oth] + sw * self.xh0[r, :, self.own], axis=1, keepdims=True)
        lane = lax.broadcasted_iota(jnp.int32, (T, 128), 1)
        st = jnp.where(lane == 0, s1, jnp.where(lane == 1, s2, 0.0))
        self.st[r] = st
        st = jnp.concatenate([st, jnp.zeros((L - T, 128), F32)], axis=0).T
        self.st_own[r] = st[0:8, :]

    def norm_first_back(self, r):
        stp = jnp.concatenate([self.st_peer[r], jnp.zeros((120, L), F32)], axis=0).T[:T]
        self.st[r] += stp
        gain = self.par[0:1, :]

        def tile(i, c):
            g1 = self.sn[r, at(i), :]
            sc1 = g1 * gain
            st = self.st[r, at(i), :]
            m1 = (jnp.sum(sc1, axis=1, keepdims=True) + st[:, 0:1]) * (1.0 / D)
            m2 = (jnp.sum(sc1 * self.xh0[r, at(i), :], axis=1, keepdims=True) + st[:, 1:2]) * (1.0 / D)
            xh = self.xh0[r, at(i), self.own]
            e = self.sn[r, at(i), self.own] + self.ot[r, at(i), :] + self.b_peer[r, at(i), 0:H].astype(F32)
            g = self.inv0[r, at(i), :] * (e * self.par[0:1, self.own] - m1 - xh * m2)
            self.gf[r, at(i), :] = g
            low = (g * self.dconv[r, at(i), :]).astype(BF16)
            lf = low.astype(F32)
            self.dconv[r, at(i), :] = lf
            sums = [jnp.sum(w, axis=0, keepdims=True) for w in (e * xh, e, lf)]
            return tuple(x + y for x, y in zip(c, sums))
        z = jnp.zeros((1, H), F32)
        s = tiles(tile, init=(z, z, z))
        for row, val in zip((0, 4, 3), s):
            self.psum[row:row + 1, self.own] += val
        self.turn_in(self.gt, r, self.dconv[r])

    def shift_grads(self, g):
        for r in range(R):
            gg = self.gt[r, at(g, GW), :]
            for b in range(NB):
                v = pltpu.roll(gg, b, axis=1) if b else gg
                self.g8[b * GW:(b + 1) * GW, r * L:(r + 1) * L] = v.astype(BF16)

    def conv_weight_grad(self, first):
        def group(g, c):
            self.shift_inputs(g)
            self.shift_grads(g)
            gr = mm(self.x16[...], self.g8[...], NT)
            self.big[:, at(g, GW), :] = gr.reshape(NA, GW, NB * GW).astype(BF16)
            return c
        lax.fori_loop(first, first + 2, group, 0)

    def conv_input_grad(self, first):
        def group(g, c):
            self.shift_grads(g)
            w = self.convw[:, at(g, GW), :].reshape(NA * GW, NB * GW)
            z = mm(w, self.g8[...])
            for r in range(R):
                acc = None
                for a in range(NA):
                    sh = (8 * a - 64) % L
                    v = z[a * GW:(a + 1) * GW, r * L:(r + 1) * L]
                    v = pltpu.roll(v, sh, axis=1) if sh else v
                    acc = v if acc is None else acc + v
                self.ot[r, at(g, GW), :] = acc
            return c
        lax.fori_loop(first, first + 2, group, 0)

    def add_input_grad(self):
        for r in range(R):
            self.gf[r] += (self.ot[r] * self.lanes(self.live, r)).T[:T]

    def put(self, i, t, v):
        rows = at(t, 16)
        if i < 4:
            self.xt[0, pl.ds(pl.multiple_of(i * 96 + t * 16, 16), 16), :] = v
        elif i == 4:
            for c in range(3):
                self.gqkv[c, rows, :] = v[:, c * H:(c + 1) * H]
            self.gout[rows, :] = v[:, 3 * H:4 * H]
        elif i == 5:
            self.gup[rows, :] = v
        else:
            self.gdown[rows, :] = v


def swap_blocks(x, buf):
    lane = lax.broadcasted_iota(jnp.int32, (GW, H), 1)
    for d in range(8):
        turned = pltpu.roll(x, GW * d, axis=1) if d else x
        for p in range(8):
            q = (p - d) % 8
            rows = turned[GW * p:GW * (p + 1), :]
            if d:
                rows = jnp.where((lane >= GW * p) & (lane < GW * (p + 1)), rows, buf[GW * q:GW * (q + 1), :])
            buf[GW * q:GW * (q + 1), :] = rows


class Ring:
    def __init__(self, n, m, sems):
        self.n, self.m = n, m
        (self.gas, self.gar, self.gbs, self.gbr, self.gss, self.gsr, self.sas, self.sar, self.sbs, self.sbr, self.sss, self.ssr) = sems
        me = lax.axis_index("dp")
        core = lax.rem(me, 2)
        chip = me // 2
        odd = lax.rem(chip, 2)
        half = chip // 2
        self.me, self.core, self.step = me, core, 1 - 2 * core
        self.pos = (1 - odd) * half + odd * (n - 1 - half)
        self.nxt = self.dev(self.step, core)
        self.prv = self.dev(-self.step, core)
        self.sib = me + self.step
        conv = lambda q: lambda d, w=m.convw: w.at[d, 96 * q:96 * (q + 1), :]
        self.views = [conv(q) for q in range(4)] + [
            lambda d: m.wall.at[d, :, 0:UP],
            lambda d: m.wall.at[d, :, UP:DOWN],
            lambda d: m.wall.at[d, :, DOWN:ALL],
            lambda d: m.pall.at[pl.ds(d, 1)],
        ]
        self.out = {}

    def dev(self, k, core):
        n = self.n
        p = lax.rem(self.pos + k + 8 * n, n)
        q = p // (n // 2)
        return 2 * ((1 - q) * 2 * p + q * (2 * (n - 1 - p) + 1)) + core

    def copy(self, src, dst, send, recv, dp):
        return pltpu.make_async_remote_copy(src, dst, send, recv, device_id={"dp": dp}, device_id_type=MESH)

    def go(self, key, copy):
        copy.start()
        self.out.setdefault(key, []).append(copy)

    def sent(self, key):
        for copy in self.out.pop(key):
            copy.wait_send()

    def gather(self, i, s):
        key = ("g", i)
        ahead = (self.gas, self.gar, self.nxt, 4, -self.step, 0)
        back = (self.gbs, self.gbr, self.prv, 3, self.step, 4)
        for send, recv, to, far, way, k in (ahead, back):
            if s > far:
                continue
            slot = self.views[i](self.dev(way * s, self.core))
            if s > 0:
                self.copy(slot, slot, send.at[i, s - 1], recv.at[i, s - 1], to).wait_recv()
            if s < far:
                self.go(key, self.copy(slot, slot, send.at[i, s], recv.at[i, s], to))
            if s > 0 or k == 0:
                self.go(key, self.copy(slot, slot, self.gss.at[i, k + s], self.gsr.at[i, k + s], self.sib))

    def gathered(self, i):
        for k, way in [(s, self.step * s) for s in range(5)] + [(4 + s, -self.step * s) for s in range(1, 4)]:
            slot = self.views[i](self.dev(way, 1 - self.core))
            self.copy(slot, slot, self.gss.at[i, k], self.gsr.at[i, k], self.sib).wait_recv()
        self.sent(("g", i))

    def grads(self, i, d):
        if i < 4:
            return self.m.big.at[d, 96 * i:96 * (i + 1), :]
        if i == 4:
            return self.m.wall.at[d, :, QKV:UP]
        return self.views[i](d)

    def scatter_begin(self, i):
        for k, way in ((0, -4), (4, 3), (1, -3), (5, 2), (2, -2), (6, 1), (3, -1), (7, 0)):
            src = self.grads(i, self.dev(way * self.step, 1 - self.core))
            self.go(("s", i), self.copy(src, self.m.sb[i].at[k], self.sss.at[i, k], self.ssr.at[i, k], self.sib))

    def scatter(self, i, j):
        sb, rr = self.m.sb[i], self.m.rr[i]
        ahead = (self.sas, self.sar, self.nxt, 4, self.step, 0)
        back = (self.sbs, self.sbr, self.prv, 3, -self.step, 4)
        if j < 4:
            for send, recv, to, far, way, k in (ahead, back):
                if j >= far:
                    continue
                terms = []
                if j > 0:
                    terms.append(rr.at[k + j - 1])
                    self.copy(terms[0], terms[0], send.at[i, j - 1], recv.at[i, j - 1], to).wait_recv()
                self.add(i, k + j, self.dev(way * (far - j), self.core), terms, sb.at[k + j])
                self.go(("s", i), self.copy(sb.at[k + j], rr.at[k + j], send.at[i, j], recv.at[i, j], to))
        else:
            terms = [rr.at[3], rr.at[6]]
            self.copy(terms[0], terms[0], self.sas.at[i, 3], self.sar.at[i, 3], self.nxt).wait_recv()
            self.copy(terms[1], terms[1], self.sbs.at[i, 2], self.sbr.at[i, 2], self.prv).wait_recv()
            self.add(i, 7, self.me, terms, None)

    def add(self, i, k, dev, terms, into):
        held = self.m.sb[i].at[k]
        self.copy(held, held, self.sss.at[i, k], self.ssr.at[i, k], self.sib).wait_recv()
        mine = self.grads(i, dev)

        def tile(t, c):
            rows = at(t, 16)
            v = mine[rows, :].astype(F32) + held[rows, :].astype(F32)
            for term in terms:
                v = v + term[rows, :].astype(F32)
            if into is None:
                self.m.put(i, t, v)
            else:
                into[rows, :] = v.astype(BF16)
            return c
        tiles(tile, held.shape[0] // 16)


SCRATCH = dict(
    act=((2, R, T, D), BF16), par=((16, D), F32),
    convw=((16, H, H), BF16), wall=((16, 48, ALL), BF16),
    xt=((R, H, L), F32), ot=((R, H, L), F32), gt=((R, H, L), F32), x16=((768, R * L), BF16), g8=((H, R * L), BF16),
    gc=((R, T, D), BF16), dconv=((R, T, H), F32), xh0=((R, T, D), F32), inv0=((R, T, 1), F32), fn=((R, T, D), F32), flow=((R, T, D), BF16),
    qkv=((R, T, 1152), BF16), big=((16, H, H), BF16), ctx=((R, T, H), BF16),
    a_own=((R, T, D), BF16), a_peer=((R, T, D), BF16), b_own=((R, T, D), BF16), b_peer=((R, T, D), BF16),
    xh1=((R, T, D), F32), inv1=((R, T, 1), F32),
    hid=((R, T, FF), BF16), dg=((R, T, FF), BF16), mixf=((TM, D), F32), gdl=((R, T, D), BF16),
    gctx=((R, T, H), BF16), st=((R, T, 128), F32),
    st_own=((R, 8, L), F32), st_peer=((R, 8, L), F32), psum=((16, D), F32), pub=((4, H), F32),
)
RING_SCRATCH = dict(pall=((16, 16, H), F32))
for _i in range(7):
    _tail = (96, H) if _i < 4 else (48, FF)
    RING_SCRATCH["sb%d" % _i] = ((8,) + _tail, BF16)
    RING_SCRATCH["rr%d" % _i] = ((7,) + _tail, BF16)
RING_INS = ("frames", "ograd", "seg", "live", "upb", "gains", "biases", "cw", "qkvw", "outw", "upw", "downw")
RING_OUTS = ("mixed", "gf", "gcw", "gqkv", "gout", "gup", "gdown", "gupb", "ggains", "gbiases")
INS = ("frames", "ograd", "seg", "live", "upb", "gains", "biases", "convw_hbm", "wa_hbm", "wb_hbm")
OUTS = ("mixed", "gf", "gconv_hbm", "ga_hbm", "gb_hbm", "pout")


def layer_kernel(ring, *refs):
    m = Mid()
    names = (RING_INS + RING_OUTS + tuple(SCRATCH) + tuple(RING_SCRATCH)) if ring else (INS + OUTS + tuple(SCRATCH))
    for name, ref in zip(names, refs):
        setattr(m, name, ref)
    loc, snd, rcv = refs[len(names):len(names) + 3]
    m.slow, m.sn, m.gal, m.gst = m.gc, m.fn, m.gdl, m.qkv
    mp = lax.axis_index("mp")
    m.mp = mp
    m.own = pl.ds(pl.multiple_of(mp * H, 128), H)
    m.oth = pl.ds(pl.multiple_of((1 - mp) * H, 128), H)
    peer = {"mp": 1 - mp}
    bar = pltpu.get_barrier_semaphore()
    acts = [pltpu.make_async_copy(x, m.act.at[i, :, :, m.own], loc.at[i]) for i, x in enumerate((m.frames, m.ograd))]
    if ring:
        rg = Ring(8, m, refs[len(names) + 3:])
        m.sb, m.rr = ([getattr(m, "%s%d" % (w, i)) for i in range(7)] for w in ("sb", "rr"))
        loads = [pltpu.make_async_copy(m.qkvw.at[c], m.wall.at[rg.me, :, QKV + c * H:QKV + (c + 1) * H], loc.at[2 + c]) for c in range(3)]
        loads += [
            pltpu.make_async_copy(m.outw, m.wall.at[rg.me, :, OUT:UP], loc.at[5]),
            pltpu.make_async_copy(m.upw, m.wall.at[rg.me, :, UP:DOWN], loc.at[6]),
            pltpu.make_async_copy(m.downw, m.wall.at[rg.me, :, DOWN:ALL], loc.at[7]),
        ]
        near = [{"dp": rg.nxt}, {"dp": rg.prv}, {"dp": rg.sib}, peer]
    else:
        loads = [
            pltpu.make_async_copy(m.convw_hbm, m.convw, loc.at[2]),
            pltpu.make_async_copy(m.wa_hbm, m.wall.at[:, :, 0:UP], loc.at[3]),
            pltpu.make_async_copy(m.wb_hbm, m.wall.at[:, :, UP:ALL], loc.at[4]),
        ]
        near = [peer]
    for d in near:
        pl.semaphore_signal(bar, inc=1, device_id=d, device_id_type=MESH)
    for c in acts + loads:
        c.start()
    m.par[0:3, m.own] = m.gains[...]
    m.par[3:11, m.own] = m.biases[...]
    m.psum[...] = jnp.zeros((16, D), F32)
    m.pub[...] = jnp.zeros((4, H), F32)
    if ring:
        swap_blocks(m.cw[...].astype(F32), m.ot.at[0])
        m.convw[rg.me] = m.ot[0].astype(BF16)
    pl.semaphore_wait(bar, len(near))
    if ring:
        for q in range(4):
            rg.gather(q, 0)

    def swap(i, r, src, dst, land):
        c = pltpu.make_async_remote_copy(src, dst, snd.at[i, r], rcv.at[i, r], device_id=peer, device_id_type=MESH)
        c.start()
        return c, pltpu.make_async_remote_copy(land, land, snd.at[i, r], rcv.at[i, r], device_id=peer, device_id_type=MESH)

    pend = {}
    own, oth = m.own, m.oth
    if ring:
        theirs = m.wall.at[rg.me, :, THEIRS:QKV]
        pend[7, 1] = swap(7, 1, m.outw, theirs, theirs)
    pend[7, 0] = swap(7, 0, m.par.at[:, own], m.par.at[:, own], m.par.at[:, oth])
    for i in range(2):
        acts[i].wait()
        pend[6, i] = swap(6, i, m.act.at[i, :, :, own], m.act.at[i, :, :, own], m.act.at[i, :, :, oth])
    def gather(*items):
        if ring:
            for i, s in items:
                rg.gather(i, s)

    def scatter(*items):
        if ring:
            for i, s in items:
                rg.scatter(i, s)

    m.turn_frames()
    if ring:
        G, S = rg.gather, rg.scatter
        for s in range(1, 5):
            for q in range(4):
                G(q, s)
            if s == 3:
                for c in loads:
                    c.wait()
                pend[7, 1][1].wait_recv()
                G(4, 0)
        gather((4, 1), (5, 0), (6, 0))
        for q in range(4):
            rg.gathered(q)
    else:
        for c in loads:
            c.wait()
    m.conv_forward()
    gather((4, 2), (5, 1))
    for r in range(R):
        m.conv_finish(r)
        pend[0, r] = swap(0, r, m.gc.at[r, :, own], m.gc.at[r, :, own], m.gc.at[r, :, oth])
    gather((6, 1))
    pend[7, 0][1].wait_recv()
    pend[6, 0][1].wait_recv()
    pend[0, 0][1].wait_recv()
    m.norm_first(0)
    gather((4, 3))
    pend[0, 1][1].wait_recv()
    m.norm_first(1)
    gather((5, 2), (6, 2), (4, 4))
    if ring:
        rg.gathered(4)
    for r in range(R):
        m.project(r)
        m.attend(r)
        pend[1, r] = swap(1, r, m.ctx.at[r], m.a_peer.at[r, :, 0:H], m.a_peer.at[r, :, 0:H])
        m.add_attended(r, m.ctx[r], OUT)
        gather((5 + r, 3))
    gather((5, 4))
    if ring:
        rg.gathered(5)
    for r in range(R):
        pend[1, r][1].wait_recv()
        m.add_attended(r, m.a_peer[r, :, 0:H], THEIRS)
        pend[0, r][0].wait_send()
        m.norm_second(r)
        m.feed_up(r)
        if ring and r == 0:
            rg.gather(6, 4)
            rg.gathered(6)
        m.feed_down(r)
        pend[2, r] = swap(2, r, m.b_own.at[r], m.b_peer.at[r], m.b_peer.at[r])
    pend[6, 1][1].wait_recv()
    for r in range(R):
        pend[2, r][1].wait_recv()
        m.norm_third(r)
        m.feed_backward(r)
        if r == 1:
            m.weight_grad(m.gdl, m.hid, 4, DOWN)
            if ring:
                rg.scatter_begin(6)
        pend[1, r][0].wait_send()
        m.feed_back_up(r)
        pend[3, r] = swap(3, r, m.a_own.at[r], m.a_peer.at[r], m.a_peer.at[r])
    scatter((6, 0))
    m.weight_grad(m.slow, m.dg, 4, UP)
    if ring:
        rg.scatter_begin(5)
    else:
        gb = pltpu.make_async_copy(m.wall.at[:, :, UP:ALL], m.gb_hbm, loc.at[4])
        gb.start()
    for r in range(R):
        pend[3, r][1].wait_recv()
        m.norm_second_back(r)
        if r == 0:
            scatter((5, 0))
        m.attend_back(r)
        scatter(((6, 1), (5, 2))[r])
        pend[2, r][0].wait_send()
        m.project_back(r)
        pend[4, r] = swap(4, r, m.b_own.at[r, :, 0:H], m.b_peer.at[r, :, 0:H], m.b_peer.at[r, :, 0:H])
        pend[5, r] = swap(5, r, m.st_own.at[r], m.st_peer.at[r], m.st_peer.at[r])
        if r == 0:
            scatter((5, 1), (6, 2))
    m.weight_grad(m.gal, m.ctx, 1, OUT)
    m.weight_grad(m.flow, m.gst, 3, QKV)
    if ring:
        rg.scatter_begin(4)
        rg.scatter(6, 3)
    else:
        ga = pltpu.make_async_copy(m.wall.at[:, :, QKV:UP], m.ga_hbm, loc.at[3])
        ga.start()
    for r in range(R):
        pend[5, r][1].wait_recv()
        pend[4, r][1].wait_recv()
        m.norm_first_back(r)
        if r == 0:
            scatter((5, 3), (4, 0))
    if ring:
        m.pall[pl.ds(rg.me, 1), 0:11, :] = m.psum[0:11, own][None]
        m.pall[pl.ds(rg.me, 1), 11:12, :] = jnp.zeros((1, 1, H), F32)
        m.pall[pl.ds(rg.me, 1), 12:16, :] = m.pub[...][None]
        G(7, 0)
        for q in range(4):
            m.conv_weight_grad(2 * q)
            rg.scatter_begin(q)
            if q == 0:
                S(6, 4)
            if q == 1:
                scatter((4, 1), (0, 0), (5, 4))
                G(7, 1)
            if q == 2:
                S(1, 0)
        S(2, 0)
        S(3, 0)
        G(7, 2)
        S(4, 2)
        m.conv_input_grad(0)
        for q in range(4):
            S(q, 1)
        S(4, 3)
        G(7, 3)
        m.conv_input_grad(2)
        m.conv_input_grad(4)
        for q in range(4):
            S(q, 2)
        S(4, 4)
        G(7, 4)
        m.conv_input_grad(6)
        m.add_input_grad()
        for s in (3, 4):
            for q in range(4):
                S(q, s)
        rg.gathered(7)
        tot = jnp.sum(m.pall[...], axis=0)
        m.ggains[...] = tot[0:3]
        m.gbiases[...] = tot[3:11]
        for k in range(4):
            m.gupb[k * H:(k + 1) * H] = tot[12 + k]
        swap_blocks(m.xt[0], m.gcw)
        for i in range(7):
            rg.sent(("s", i))
    else:
        for g in range(0, 8, 2):
            m.conv_weight_grad(g)
            m.conv_input_grad(g)
        m.add_input_grad()
        gc = pltpu.make_async_copy(m.big, m.gconv_hbm, loc.at[2])
        gc.start()
        m.pout[0:11, :] = m.psum[0:11, own]
        m.pout[11:12, :] = jnp.zeros((1, H), F32)
        m.pout[12:16, :] = m.pub[...]
        for c in (ga, gb, gc):
            c.wait()
    if ring:
        pend[7, 1][0].wait_send()
    for i, r in ((3, 0), (3, 1), (4, 0), (4, 1), (5, 0), (5, 1), (6, 0), (6, 1), (7, 0)):
        pend[i, r][0].wait_send()


def layer(ring, *args):
    vm, hb = pl.BlockSpec(memory_space=pltpu.VMEM), pl.BlockSpec(memory_space=pl.ANY)
    S = jax.ShapeDtypeStruct
    outs = [S((R, T, H), BF16), S((R, T, H), F32)]
    dma = pltpu.SemaphoreType.DMA
    scratch = dict(SCRATCH)
    if ring:
        scratch.update(RING_SCRATCH)
        outs += [S((H, H), F32), S((3, 48, H), F32), S((48, H), F32), S((48, FF), F32), S((48, FF), F32), S((FF,), F32), S((3, H), F32), S((8, H), F32)]
        in_specs, out_specs = [hb] * 2 + [vm] * 6 + [hb] * 4, [vm] * 10
        sems = [dma((8,)), dma((8, R)), dma((8, R))] + [dma((8, w)) for w in (4, 4, 3, 3, 8, 8)] + [dma((7, w)) for w in (4, 4, 3, 3, 8, 8)]
    else:
        outs += [S((16, H, H), BF16), S((16, 48, UP - QKV), BF16), S((16, 48, ALL - UP), BF16), S((16, H), F32)]
        in_specs, out_specs = [hb] * 2 + [vm] * 5 + [hb] * 3, [vm] * 2 + [hb] * 3 + [vm]
        sems = [dma((5,)), dma((8, R)), dma((8, R))]
    return pl.pallas_call(
        functools.partial(layer_kernel, ring),
        out_shape=outs,
        in_specs=in_specs,
        out_specs=out_specs,
        scratch_shapes=[pltpu.VMEM(s, d) for s, d in scratch.values()] + sems,
        compiler_params=pltpu.CompilerParams(collective_id=0, has_side_effects=True, vmem_limit_bytes=63 << 20),
        name="layer",
    )(*args)


def pass_on(*arrays):
    count = len(arrays)

    def kernel(*refs):
        ins, outs, held, sems = refs[:count], refs[count:2 * count], refs[2 * count:3 * count], refs[3 * count]
        loads = [pltpu.make_async_copy(ins[i], held[i], sems.at[0, i]) for i in range(count)]
        stores = [pltpu.make_async_copy(held[i], outs[i], sems.at[1, i]) for i in range(count)]
        for c in loads:
            c.start()
        for i in range(count):
            loads[i].wait()
            stores[i].start()
        for c in stores:
            c.wait()

    hb = pl.BlockSpec(memory_space=pl.ANY)
    return pl.pallas_call(
        kernel,
        out_shape=[jax.ShapeDtypeStruct(a.shape, a.dtype) for a in arrays],
        in_specs=[hb] * count,
        out_specs=[hb] * count,
        scratch_shapes=[pltpu.VMEM(a.shape, a.dtype) for a in arrays] + [pltpu.SemaphoreType.DMA((2, count))],
        name="pass_on",
    )(*arrays)


def taps_in(weight):
    blocks = weight.reshape(-1, 8, 48, 8, 48)
    return blocks.transpose(0, 3, 2, 1, 4).reshape(-1, 384, 384)


def taps_out(grad):
    blocks = grad.reshape(-1, 8, 48, 8, 48)
    return blocks.transpose(0, 3, 2, 1, 4).reshape(-1, 384)


def body(frames, segment_ids, live, conv_weight, qkv_weight, out_weight, up_weight, down_weight,
         up_bias, gains, biases, out_grad):
    common = (frames, out_grad, segment_ids, live, up_bias, gains, biases)
    if conv_weight.shape[0] == 384 and qkv_weight.shape[0] == 48:
        mixed, grad_in, g_conv, g_qkv, g_out, g_up, g_down, g_upb, g_gains, g_biases = pass_on(
            *layer(True, *common, conv_weight, qkv_weight.transpose(1, 0, 2), out_weight.T, up_weight, down_weight.T)
        )
        return (mixed, grad_in, g_conv, g_qkv.transpose(1, 0, 2), g_out.T, g_up, g_down.T, g_upb, g_gains, g_biases)
    theirs = lax.ppermute(out_weight.T, "mp", [(0, 1), (1, 0)])
    wa = jnp.concatenate([theirs, qkv_weight.reshape(-1, 3 * H), out_weight.T], axis=1)
    wb = jnp.concatenate([up_weight, down_weight.T], axis=1)
    convw = taps_in(lax.all_gather(conv_weight, "dp", axis=0, tiled=True))
    wa, wb = (lax.all_gather(w, "dp", axis=0, tiled=True).reshape(16, 48, -1) for w in (wa, wb))
    mixed, grad_in, g_conv, g_a, g_b, sums = layer(False, *common, convw, wa, wb)
    g_conv, g_a, g_b = (
        lax.psum_scatter(g, "dp", scatter_dimension=0, tiled=True).astype(F32)
        for g in (taps_out(g_conv), g_a.reshape(D, -1), g_b.reshape(D, -1))
    )
    sums = lax.psum(sums, "dp")
    return (
        mixed,
        grad_in,
        g_conv,
        g_a[:, : 3 * H].reshape(-1, 3, H),
        g_a[:, 3 * H :].T,
        g_b[:, :FF],
        g_b[:, FF:].T,
        sums[12:16].reshape(FF),
        sums[0:3],
        sums[3:11],
    )


def solution(mesh):
    placed = (
        P("dp", None, "mp"),
        P("dp", None),
        P("dp", None),
        P("dp", "mp"),
        P("dp", None, "mp"),
        P("mp", "dp"),
        P("dp", "mp"),
        P("mp", "dp"),
        P("mp"),
        P(None, "mp"),
        P(None, "mp"),
        P("dp", None, "mp"),
    )
    return jax.shard_map(
        body,
        mesh=mesh,
        in_specs=placed,
        out_specs=(
            P("dp", None, "mp"),
            P("dp", None, "mp"),
            P("dp", "mp"),
            P("dp", None, "mp"),
            P("mp", "dp"),
            P("dp", "mp"),
            P("mp", "dp"),
            P("mp"),
            P(None, "mp"),
            P(None, "mp"),
        ),
        check_vma=False,
    )
```

```python
import functools

import jax
import jax.numpy as jnp
from jax import lax
from jax.experimental import pallas as pl
from jax.experimental.pallas import tpu as pltpu
from jax.sharding import PartitionSpec as P

MESH = pl.DeviceIdType.MESH
F32, BF16 = jnp.float32, jnp.bfloat16
D, H, FF, HD = 768, 384, 1536, 64
R, T, L = 2, 320, 384
NB, GW, NA = 8, 48, 16
TM = 64
EPS = 1e-5
THEIRS, QKV, OUT, UP, DOWN, ALL = 0, 384, 1536, 1920, 3456, 4992
NN = (((1,), (0,)), ((), ()))
NT = (((1,), (1,)), ((), ()))
TN = (((0,), (0,)), ((), ()))

def mm(a, b, dims=NN):
    return lax.dot_general(a, b, dims, preferred_element_type=F32)

def gelu_both(v):
    p = 0.5 + 0.5 * lax.erf(v * 0.7071067811865476)
    return v * p, p + v * (0.3989422804014327 * jnp.exp(-0.5 * v * v))

def tiles(body, count=T // TM, init=0):
    return lax.fori_loop(0, count, body, init)

def cols(start, size=H):
    return pl.ds(pl.multiple_of(start, 128), size)


def at(i, size=TM):
    return pl.ds(pl.multiple_of(i * size, size), size)

class Mid:
    def shift_inputs(self, g):
        rows = at(g, GW)
        for r in range(R):
            xg = self.xt[r, rows, :]
            for a in range(NA):
                sh = (64 - 8 * a) % L
                v = pltpu.roll(xg, sh, axis=1) if sh else xg
                self.x16[a * GW:(a + 1) * GW, r * L:(r + 1) * L] = v.astype(BF16)

    def turn_in(self, dst, r, rows):
        dst[r] = jnp.concatenate([rows, jnp.zeros((L - T, H), F32)], axis=0).T

    def lanes(self, ref, r):
        return jnp.concatenate([ref[r:r + 1, :].astype(F32), jnp.zeros((1, L - T), F32)], axis=1)

    def turn_frames(self):
        for r in range(R):
            self.turn_in(self.xt, r, self.act[0, r, :, self.own].astype(F32))
            self.xt[r] = self.xt[r] * self.lanes(self.live, r)

    def conv_forward(self):

        def group(g, c):
            self.shift_inputs(g)
            w = self.convw[:, at(g, GW), :].reshape(NA * GW, NB * GW)
            y = mm(w, self.x16[...], TN)
            for r in range(R):
                acc = y[0:GW, r * L:(r + 1) * L]
                for b in range(1, NB):
                    acc = acc + pltpu.roll(y[b * GW:(b + 1) * GW, r * L:(r + 1) * L], L - b, axis=1)
                self.ot[r, at(g, GW), :] = acc
            return c
        tiles(group, 8)
    def conv_finish(self, r):
        v = self.ot[r].T[:T] + self.par[3:4, self.own]
        gel, dg = gelu_both(v)
        self.dconv[r] = dg
        self.gc[r, :, self.own] = gel.astype(BF16)

    def norm_first(self, r):
        def tile(i, c):
            v = self.act[0, r, at(i), :].astype(F32) + self.gc[r, at(i), :].astype(F32)
            cen = v - jnp.sum(v, axis=1, keepdims=True) * (1.0 / D)
            inv = lax.rsqrt(jnp.sum(cen * cen, axis=1, keepdims=True) * (1.0 / D) + EPS)
            xh = cen * inv
            n = xh * self.par[0:1, :] + self.par[4:5, :]
            self.xh0[r, at(i), :] = xh
            self.inv0[r, at(i), :] = inv
            self.fn[r, at(i), :] = n
            self.flow[r, at(i), :] = n.astype(BF16)
            return c
        tiles(tile)

    def wall_cols(self, start, size):
        return self.wall[:, :, cols(start, size)].reshape(D, size)

    def wall_rows(self, n, start, size):
        return self.wall[pl.ds(n * 8, 8), :, start:start + size].reshape(H, size)

    def project(self, r):
        def part(c, k):
            bias = self.par[pl.ds(5 + c // 2, 1), self.own] * ((c - 1) * (c - 1)).astype(F32)
            v = mm(self.flow[r], self.wall_cols(QKV + c * H, H)) + bias
            self.qkv[r, :, cols(c * H)] = v.astype(BF16)
            return k
        tiles(part, 3)

    def lane_masks(self):
        lane = lax.broadcasted_iota(jnp.int32, (1, 128), 1)
        return [(lane < HD).astype(F32).astype(BF16), (lane >= HD).astype(F32).astype(BF16)]

    def pair(self, ref, r, p, c=0):
        return ref[r, :, cols(p * 128 + c * H, 128)]

    def attend(self, r):
        masks = self.lane_masks()
        ids = self.lanes(self.seg, r)
        same = jnp.broadcast_to(ids, (128, L)).T[:T, 0:1] == ids[:, :T]

        def step(p, c):
            q, k, v = (self.pair(self.qkv, r, p, i) for i in range(3))
            acc = None
            for h in range(2):
                s = mm(q * masks[h], k, NT) * 0.125
                s = jnp.where(same, s, -1e30)
                w = jnp.exp(s - jnp.max(s, axis=1, keepdims=True))
                pr = (w * (1.0 / jnp.sum(w, axis=1, keepdims=True))).astype(BF16)
                self.big[r * 6 + p * 2 + h, 0:T, 0:T] = pr
                o = mm(pr, v * masks[h])
                acc = o if acc is None else acc + o
            self.ctx[r, :, cols(p * 128, 128)] = acc.astype(BF16)
            return c
        tiles(step, 3)

    def add_attended(self, r, ctx, start):
        def part(n, c):
            self.fn[r, :, cols(n * H)] += mm(ctx, self.wall_rows(n, start, H), NT)
            return c
        tiles(part, 2)

    def norm_second(self, r):
        def tile(i, c):
            v = self.fn[r, at(i), :] + self.par[7:8, :]
            cen = v - jnp.sum(v, axis=1, keepdims=True) * (1.0 / D)
            inv = lax.rsqrt(jnp.sum(cen * cen, axis=1, keepdims=True) * (1.0 / D) + EPS)
            xh = cen * inv
            n = xh * self.par[1:2, :] + self.par[8:9, :]
            self.xh1[r, at(i), :] = xh
            self.inv1[r, at(i), :] = inv
            self.sn[r, at(i), :] = n
            self.slow[r, at(i), :] = n.astype(BF16)
            return c
        tiles(tile)

    def feed_up(self, r):
        def part(n, c):
            u = mm(self.slow[r], self.wall_cols(UP + n * H, H)) + self.ub[pl.ds(n, 1), :]
            gel, dg = gelu_both(u)
            self.hid[r, :, cols(n * H)] = gel.astype(BF16)
            self.dg[r, :, cols(n * H)] = dg.astype(BF16)
            return c
        tiles(part, 4)

    def feed_down(self, r):
        def part(n, c):
            self.b_own[r, :, cols(n * H)] = mm(self.hid[r], self.wall_rows(n, DOWN, FF), NT).astype(BF16)
            return c
        tiles(part, 2)

    def add_sums(self, row, value):
        self.psum[row:row + 1, :] += value

    def norm_third(self, r):
        def tile(i, c):
            v = self.sn[r, at(i), :] + (self.b_own[r, at(i), :].astype(F32) + self.b_peer[r, at(i), :].astype(F32)) + self.par[9:10, :]
            cen = v - jnp.sum(v, axis=1, keepdims=True) * (1.0 / D)
            inv = lax.rsqrt(jnp.sum(cen * cen, axis=1, keepdims=True) * (1.0 / D) + EPS)
            xh = cen * inv
            self.mixf[...] = xh * self.par[2:3, :] + self.par[10:11, :]
            self.mixed[r, at(i), :] = self.mixf[:, self.own].astype(BF16)
            e = self.act[1, r, at(i), :].astype(F32)
            sc = e * self.par[2:3, :]
            ex = e * xh
            m1 = jnp.sum(sc, axis=1, keepdims=True) * (1.0 / D)
            m2 = jnp.sum(sc * xh, axis=1, keepdims=True) * (1.0 / D)
            g = inv * (sc - m1 - xh * m2)
            self.sn[r, at(i), :] = g
            self.gdl[r, at(i), :] = g.astype(BF16)
            sums = [jnp.sum(w, axis=0, keepdims=True) for w in (ex, e, g)]
            return tuple(x + y for x, y in zip(c, sums))
        z = jnp.zeros((1, D), F32)
        s = tiles(tile, init=(z, z, z))
        for row, val in zip((2, 10, 9), s):
            self.add_sums(row, val)

    def feed_backward(self, r):
        def part(n, c):
            gh = mm(self.gdl[r], self.wall_cols(DOWN + n * H, H))
            g = (gh * self.dg[r, :, cols(n * H)].astype(F32)).astype(BF16)
            self.dg[r, :, cols(n * H)] = g
            self.pub[pl.ds(n, 1), :] += jnp.sum(g.astype(F32), axis=0, keepdims=True)
            return c
        tiles(part, 4)

    def feed_back_up(self, r):
        def part(n, c):
            self.a_own[r, :, cols(n * H)] = mm(self.dg[r], self.wall_rows(n, UP, FF), NT).astype(BF16)
            return c
        tiles(part, 2)

    def weight_grad(self, src, other, count, start):
        def part(n, c):
            o = other[:, :, cols(n * H)].reshape(R * T, H)
            g = mm(src[...].reshape(R * T, D), o, TN)
            self.wall[:, :, cols(start + n * H)] = g.reshape(16, 48, H).astype(BF16)
            return c
        tiles(part, count)

    def norm_second_back(self, r):
        def tile(i, c):
            e = self.sn[r, at(i), :] + (self.a_own[r, at(i), :].astype(F32) + self.a_peer[r, at(i), :].astype(F32))
            xh = self.xh1[r, at(i), :]
            sc = e * self.par[1:2, :]
            m1 = jnp.sum(sc, axis=1, keepdims=True) * (1.0 / D)
            m2 = jnp.sum(sc * xh, axis=1, keepdims=True) * (1.0 / D)
            g = self.inv1[r, at(i), :] * (sc - m1 - xh * m2)
            self.sn[r, at(i), :] = g
            self.gal[r, at(i), :] = g.astype(BF16)
            sums = [jnp.sum(w, axis=0, keepdims=True) for w in (e * xh, e, g)]
            return tuple(x + y for x, y in zip(c, sums))
        z = jnp.zeros((1, D), F32)
        s = tiles(tile, init=(z, z, z))
        for row, val in zip((1, 8, 7), s):
            self.add_sums(row, val)

    def attend_back(self, r):
        self.gctx[r] = mm(self.gal[r], self.wall_cols(OUT, H)).astype(BF16)
        masks = self.lane_masks()

        def step(p, c):
            q, k, v = (self.pair(self.qkv, r, p, i) for i in range(3))
            go = self.pair(self.gctx, r, p)
            gq = gk = gv = None
            for h in range(2):
                gom = go * masks[h]
                gp = mm(gom, v, NT)
                pr = self.big[r * 6 + p * 2 + h, 0:T, 0:T]
                pf = pr.astype(F32)
                gs = (pf * (gp - jnp.sum(gp * pf, axis=1, keepdims=True))).astype(BF16)
                a, b, d = mm(gs, k * masks[h]), mm(gs, q * masks[h], TN), mm(pr, gom, TN)
                gq, gk, gv = (a, b, d) if gq is None else (gq + a, gk + b, gv + d)
            for i, w in enumerate((gq * 0.125, gk * 0.125, gv)):
                self.gst[r, :, cols(p * 128 + i * H, 128)] = w.astype(BF16)
            return c
        tiles(step, 3)
        for row, c in ((5, 0), (6, 2)):
            self.psum[row:row + 1, self.own] += jnp.sum(self.gst[r, :, c * H:(c + 1) * H].astype(F32), axis=0, keepdims=True)

    def project_back(self, r):
        po = mm(self.gst[r], self.wall_rows(1 - self.mp, QKV, 1152), NT)
        pw = mm(self.gst[r], self.wall_rows(self.mp, QKV, 1152), NT)
        self.b_own[r, :, 0:H] = po.astype(BF16)
        self.ot[r, 0:T, :] = pw
        so = po * self.par[0:1, self.oth]
        sw = pw * self.par[0:1, self.own]
        s1 = jnp.sum(so + sw, axis=1, keepdims=True)
        s2 = jnp.sum(so * self.xh0[r, :, self.oth] + sw * self.xh0[r, :, self.own], axis=1, keepdims=True)
        lane = lax.broadcasted_iota(jnp.int32, (T, 128), 1)
        st = jnp.where(lane == 0, s1, jnp.where(lane == 1, s2, 0.0))
        self.st[r] = st
        st = jnp.concatenate([st, jnp.zeros((L - T, 128), F32)], axis=0).T
        self.st_own[r] = st[0:8, :]

    def norm_first_back(self, r):
        stp = jnp.concatenate([self.st_peer[r], jnp.zeros((120, L), F32)], axis=0).T[:T]
        self.st[r] += stp
        gain = self.par[0:1, :]

        def tile(i, c):
            g1 = self.sn[r, at(i), :]
            sc1 = g1 * gain
            st = self.st[r, at(i), :]
            m1 = (jnp.sum(sc1, axis=1, keepdims=True) + st[:, 0:1]) * (1.0 / D)
            m2 = (jnp.sum(sc1 * self.xh0[r, at(i), :], axis=1, keepdims=True) + st[:, 1:2]) * (1.0 / D)
            xh = self.xh0[r, at(i), self.own]
            e = self.sn[r, at(i), self.own] + self.ot[r, at(i), :] + self.b_peer[r, at(i), 0:H].astype(F32)
            g = self.inv0[r, at(i), :] * (e * self.par[0:1, self.own] - m1 - xh * m2)
            self.gf[r, at(i), :] = g
            low = (g * self.dconv[r, at(i), :]).astype(BF16)
            lf = low.astype(F32)
            self.dconv[r, at(i), :] = lf
            sums = [jnp.sum(w, axis=0, keepdims=True) for w in (e * xh, e, lf)]
            return tuple(x + y for x, y in zip(c, sums))
        z = jnp.zeros((1, H), F32)
        s = tiles(tile, init=(z, z, z))
        for row, val in zip((0, 4, 3), s):
            self.psum[row:row + 1, self.own] += val
        self.turn_in(self.gt, r, self.dconv[r])

    def shift_grads(self, g):
        for r in range(R):
            gg = self.gt[r, at(g, GW), :]
            for b in range(NB):
                v = pltpu.roll(gg, b, axis=1) if b else gg
                self.g8[b * GW:(b + 1) * GW, r * L:(r + 1) * L] = v.astype(BF16)

    def conv_weight_grad(self, first):
        def group(g, c):
            self.shift_inputs(g)
            self.shift_grads(g)
            gr = mm(self.x16[...], self.g8[...], NT)
            self.big[:, at(g, GW), :] = gr.reshape(NA, GW, NB * GW).astype(BF16)
            return c
        lax.fori_loop(first, first + 2, group, 0)

    def conv_input_grad(self, first):
        def group(g, c):
            self.shift_grads(g)
            w = self.convw[:, at(g, GW), :].reshape(NA * GW, NB * GW)
            z = mm(w, self.g8[...])
            for r in range(R):
                acc = None
                for a in range(NA):
                    sh = (8 * a - 64) % L
                    v = z[a * GW:(a + 1) * GW, r * L:(r + 1) * L]
                    v = pltpu.roll(v, sh, axis=1) if sh else v
                    acc = v if acc is None else acc + v
                self.ot[r, at(g, GW), :] = acc
            return c
        lax.fori_loop(first, first + 2, group, 0)

    def add_input_grad(self):
        for r in range(R):
            self.gf[r] += (self.ot[r] * self.lanes(self.live, r)).T[:T]

    def put(self, i, t, v):
        rows = at(t, 16)
        if i == 4:
            for c in range(3):
                self.gqkv[c, rows, :] = v[:, c * H:(c + 1) * H]
            self.gout[rows, :] = v[:, 3 * H:4 * H]
        elif i == 5:
            self.gup[rows, :] = v
        else:
            self.gdown[rows, :] = v


def swap_blocks(x, buf):
    lane = lax.broadcasted_iota(jnp.int32, (GW, H), 1)
    for d in range(8):
        turned = pltpu.roll(x, GW * d, axis=1) if d else x
        for p in range(8):
            q = (p - d) % 8
            rows = turned[GW * p:GW * (p + 1), :]
            if d:
                rows = jnp.where((lane >= GW * p) & (lane < GW * (p + 1)), rows, buf[GW * q:GW * (q + 1), :])
            buf[GW * q:GW * (q + 1), :] = rows


class Ring:
    def __init__(self, n, m, sems):
        self.n, self.m = n, m
        (self.gas, self.gar, self.gbs, self.gbr, self.gss, self.gsr, self.sas, self.sar, self.sbs, self.sbr, self.sss, self.ssr) = sems
        me = lax.axis_index("dp")
        core = lax.rem(me, 2)
        chip = me // 2
        odd = lax.rem(chip, 2)
        half = chip // 2
        self.me, self.core, self.step = me, core, 1 - 2 * core
        self.pos = (1 - odd) * half + odd * (n - 1 - half)
        self.nxt = self.dev(self.step, core)
        self.prv = self.dev(-self.step, core)
        self.sib = me + self.step
        conv = lambda q: lambda d, w=m.convw: w.at[d, 96 * q:96 * (q + 1), :]
        self.views = [conv(q) for q in range(4)] + [
            lambda d: m.wall.at[d, :, 0:UP],
            lambda d: m.wall.at[d, :, UP:DOWN],
            lambda d: m.wall.at[d, :, DOWN:ALL],
            lambda d: m.pall.at[pl.ds(d, 1)],
        ]
        self.out = {}

    def dev(self, k, core):
        n = self.n
        p = lax.rem(self.pos + k + 8 * n, n)
        q = p // (n // 2)
        return 2 * ((1 - q) * 2 * p + q * (2 * (n - 1 - p) + 1)) + core

    def copy(self, src, dst, send, recv, dp):
        return pltpu.make_async_remote_copy(src, dst, send, recv, device_id={"dp": dp}, device_id_type=MESH)

    def go(self, key, copy):
        copy.start()
        self.out.setdefault(key, []).append(copy)

    def sent(self, key):
        for copy in self.out.pop(key):
            copy.wait_send()

    def gather(self, i, s):
        key = ("g", i)
        ahead = (self.gas, self.gar, self.nxt, 4, -self.step, 0)
        back = (self.gbs, self.gbr, self.prv, 3, self.step, 4)
        for send, recv, to, far, way, k in (ahead, back):
            if s > far:
                continue
            slot = self.views[i](self.dev(way * s, self.core))
            if s > 0:
                self.copy(slot, slot, send.at[i, s - 1], recv.at[i, s - 1], to).wait_recv()
            if s < far:
                self.go(key, self.copy(slot, slot, send.at[i, s], recv.at[i, s], to))
            if s > 0 or k == 0:
                self.go(key, self.copy(slot, slot, self.gss.at[i, k + s], self.gsr.at[i, k + s], self.sib))

    def gathered(self, i):
        for k, way in [(s, self.step * s) for s in range(5)] + [(4 + s, -self.step * s) for s in range(1, 4)]:
            slot = self.views[i](self.dev(way, 1 - self.core))
            self.copy(slot, slot, self.gss.at[i, k], self.gsr.at[i, k], self.sib).wait_recv()
        self.sent(("g", i))

    def grads(self, i, d, conv):
        if conv:
            return self.m.big.at[d, at(i, 96), :]
        if i == 4:
            return self.m.wall.at[d, :, QKV:UP]
        return self.views[i](d)

    def slots(self, i, conv):
        m = self.m
        if conv:
            return (lambda k: m.sbc.at[i, k]), (lambda k: m.rrc.at[i, k])
        return m.sb[i].at.__getitem__, m.rr[i].at.__getitem__

    def scatter_begin(self, i, conv=False, wait=False):
        sb, _ = self.slots(i, conv)
        for k, way in ((0, -4), (4, 3), (1, -3), (5, 2), (2, -2), (6, 1), (3, -1), (7, 0)):
            src = self.grads(i, self.dev(way * self.step, 1 - self.core), conv)
            copy = self.copy(src, sb(k), self.sss.at[i, k], self.ssr.at[i, k], self.sib)
            copy.wait_send() if wait else copy.start()

    def scatter(self, i, j, conv=False):
        sb, rr = self.slots(i, conv)
        ahead = (self.sas, self.sar, self.nxt, 4, self.step, 0)
        back = (self.sbs, self.sbr, self.prv, 3, -self.step, 4)
        if j < 4:
            for send, recv, to, far, way, k in (ahead, back):
                if j >= far:
                    continue
                terms = []
                if j > 0:
                    terms.append(rr(k + j - 1))
                    self.copy(terms[0], terms[0], send.at[i, j - 1], recv.at[i, j - 1], to).wait_recv()
                self.add(i, k + j, self.dev(way * (far - j), self.core), terms, sb(k + j), conv)
                self.copy(sb(k + j), rr(k + j), send.at[i, j], recv.at[i, j], to).start()
        else:
            terms = [rr(3), rr(6)]
            self.copy(terms[0], terms[0], self.sas.at[i, 3], self.sar.at[i, 3], self.nxt).wait_recv()
            self.copy(terms[1], terms[1], self.sbs.at[i, 2], self.sbr.at[i, 2], self.prv).wait_recv()
            self.add(i, 7, self.me, terms, None, conv)

    def scattered(self, i, conv=False):
        sb, rr = self.slots(i, conv)
        self.scatter_begin(i, conv, True)
        for send, recv, to, far, k in ((self.sas, self.sar, self.nxt, 4, 0), (self.sbs, self.sbr, self.prv, 3, 4)):
            for j in range(far):
                self.copy(sb(k + j), rr(k + j), send.at[i, j], recv.at[i, j], to).wait_send()

    def add(self, i, k, dev, terms, into, conv):
        held = self.slots(i, conv)[0](k)
        self.copy(held, held, self.sss.at[i, k], self.ssr.at[i, k], self.sib).wait_recv()
        mine = self.grads(i, dev, conv)

        def tile(t, c):
            rows = at(t, 16)
            v = mine[rows, :].astype(F32) + held[rows, :].astype(F32)
            for term in terms:
                v = v + term[rows, :].astype(F32)
            if into is not None:
                into[rows, :] = v.astype(BF16)
            elif conv:
                self.m.xt[0, at(6 * i + t, 16), :] = v
            else:
                self.m.put(i, t, v)
            return c
        tiles(tile, held.shape[0] // 16)


SCRATCH = dict(
    act=((2, R, T, D), BF16), par=((16, D), F32),
    convw=((16, H, H), BF16), wall=((16, 48, ALL), BF16),
    xt=((R, H, L), F32), ot=((R, H, L), F32), gt=((R, H, L), F32), x16=((768, R * L), BF16), g8=((H, R * L), BF16),
    gc=((R, T, D), BF16), dconv=((R, T, H), F32), xh0=((R, T, D), F32), inv0=((R, T, 1), F32), fn=((R, T, D), F32), flow=((R, T, D), BF16),
    qkv=((R, T, 1152), BF16), big=((16, H, H), BF16), ctx=((R, T, H), BF16),
    a_own=((R, T, D), BF16), a_peer=((R, T, D), BF16), b_own=((R, T, D), BF16), b_peer=((R, T, D), BF16),
    xh1=((R, T, D), F32), inv1=((R, T, 1), F32),
    hid=((R, T, FF), BF16), dg=((R, T, FF), BF16), mixf=((TM, D), F32), gdl=((R, T, D), BF16),
    gctx=((R, T, H), BF16), st=((R, T, 128), F32),
    st_own=((R, 8, L), F32), st_peer=((R, 8, L), F32), psum=((16, D), F32), pub=((4, H), F32), ub=((4, H), F32),
)
RING_SCRATCH = dict(pall=((16, 16, H), F32), sbc=((4, 8, 96, H), BF16), rrc=((4, 7, 96, H), BF16))
for _i in range(4, 7):
    RING_SCRATCH["sb%d" % _i] = ((8, 48, FF), BF16)
    RING_SCRATCH["rr%d" % _i] = ((7, 48, FF), BF16)


RING_INS = ("frames", "ograd", "seg", "live", "upb", "gains", "biases", "cw", "qkvw", "outw", "upw", "downw")
RING_OUTS = ("mixed", "gf", "gcw", "gqkv", "gout", "gup", "gdown", "gupb", "ggains", "gbiases")
INS = ("frames", "ograd", "seg", "live", "upb", "gains", "biases", "convw_hbm", "wa_hbm", "wb_hbm")
OUTS = ("mixed", "gf", "gconv_hbm", "ga_hbm", "gb_hbm", "pout")


def layer_kernel(ring, *refs):
    m = Mid()
    names = (RING_INS + RING_OUTS + tuple(SCRATCH) + tuple(RING_SCRATCH)) if ring else (INS + OUTS + tuple(SCRATCH))
    for name, ref in zip(names, refs):
        setattr(m, name, ref)
    loc, snd, rcv = refs[len(names):len(names) + 3]
    m.slow, m.sn, m.gal, m.gst = m.gc, m.fn, m.gdl, m.qkv
    mp = lax.axis_index("mp")
    m.mp = mp
    m.own = pl.ds(pl.multiple_of(mp * H, 128), H)
    m.oth = pl.ds(pl.multiple_of((1 - mp) * H, 128), H)
    peer = {"mp": 1 - mp}
    bar = pltpu.get_barrier_semaphore()
    acts = [pltpu.make_async_copy(x, m.act.at[i, :, :, m.own], loc.at[i]) for i, x in enumerate((m.frames, m.ograd))]
    if ring:
        rg = Ring(8, m, refs[len(names) + 3:])
        m.sb, m.rr = ({i: getattr(m, "%s%d" % (w, i)) for i in range(4, 7)} for w in ("sb", "rr"))
        loads = [pltpu.make_async_copy(m.qkvw.at[c], m.wall.at[rg.me, :, QKV + c * H:QKV + (c + 1) * H], loc.at[2 + c]) for c in range(3)]
        loads += [
            pltpu.make_async_copy(m.outw, m.wall.at[rg.me, :, OUT:UP], loc.at[5]),
            pltpu.make_async_copy(m.upw, m.wall.at[rg.me, :, UP:DOWN], loc.at[6]),
            pltpu.make_async_copy(m.downw, m.wall.at[rg.me, :, DOWN:ALL], loc.at[7]),
        ]
        near = [{"dp": rg.nxt}, {"dp": rg.prv}, {"dp": rg.sib}, peer]
    else:
        loads = [
            pltpu.make_async_copy(m.convw_hbm, m.convw, loc.at[2]),
            pltpu.make_async_copy(m.wa_hbm, m.wall.at[:, :, 0:UP], loc.at[3]),
            pltpu.make_async_copy(m.wb_hbm, m.wall.at[:, :, UP:ALL], loc.at[4]),
        ]
        near = [peer]
    for d in near:
        pl.semaphore_signal(bar, inc=1, device_id=d, device_id_type=MESH)
    for c in acts + loads:
        c.start()
    m.par[0:3, m.own] = m.gains[...]
    m.par[3:11, m.own] = m.biases[...]
    m.psum[...] = jnp.zeros((16, D), F32)
    m.pub[...] = jnp.zeros((4, H), F32)
    for k in range(4):
        m.ub[k:k + 1, :] = m.upb[k * H:(k + 1) * H].reshape(1, H)
    if ring:
        swap_blocks(m.cw[...].astype(F32), m.ot.at[0])
        m.convw[rg.me] = m.ot[0].astype(BF16)
    pl.semaphore_wait(bar, len(near))
    if ring:
        for q in range(4):
            rg.gather(q, 0)

    def swap(i, r, src, dst, land):
        c = pltpu.make_async_remote_copy(src, dst, snd.at[i, r], rcv.at[i, r], device_id=peer, device_id_type=MESH)
        c.start()
        return c, pltpu.make_async_remote_copy(land, land, snd.at[i, r], rcv.at[i, r], device_id=peer, device_id_type=MESH)

    pend = {}
    own, oth = m.own, m.oth
    if ring:
        theirs = m.wall.at[rg.me, :, THEIRS:QKV]
        pend[7, 1] = swap(7, 1, m.outw, theirs, theirs)
    pend[7, 0] = swap(7, 0, m.par.at[:, own], m.par.at[:, own], m.par.at[:, oth])
    for i in range(2):
        acts[i].wait()
        pend[6, i] = swap(6, i, m.act.at[i, :, :, own], m.act.at[i, :, :, own], m.act.at[i, :, :, oth])
    def gather(*items):
        if ring:
            for i, s in items:
                rg.gather(i, s)

    def scatter(*items):
        if ring:
            for i, s in items:
                rg.scatter(i, s)

    m.turn_frames()
    if ring:
        G, S = rg.gather, rg.scatter
        for s in range(1, 5):
            for q in range(4):
                G(q, s)
            if s == 3:
                for c in loads:
                    c.wait()
                pend[7, 1][1].wait_recv()
                G(4, 0)
        gather((4, 1), (5, 0), (6, 0))
        for q in range(4):
            rg.gathered(q)
    else:
        for c in loads:
            c.wait()
    m.conv_forward()
    gather((4, 2), (5, 1))
    for r in range(R):
        m.conv_finish(r)
        pend[0, r] = swap(0, r, m.gc.at[r, :, own], m.gc.at[r, :, own], m.gc.at[r, :, oth])
    gather((6, 1))
    pend[7, 0][1].wait_recv()
    pend[6, 0][1].wait_recv()
    pend[0, 0][1].wait_recv()
    m.norm_first(0)
    gather((4, 3))
    pend[0, 1][1].wait_recv()
    m.norm_first(1)
    gather((5, 2), (6, 2), (4, 4))
    if ring:
        rg.gathered(4)
    for r in range(R):
        m.project(r)
        m.attend(r)
        pend[1, r] = swap(1, r, m.ctx.at[r], m.a_peer.at[r, :, 0:H], m.a_peer.at[r, :, 0:H])
        m.add_attended(r, m.ctx[r], OUT)
        gather((5 + r, 3))
    gather((5, 4))
    if ring:
        rg.gathered(5)
    for r in range(R):
        pend[1, r][1].wait_recv()
        m.add_attended(r, m.a_peer[r, :, 0:H], THEIRS)
        pend[0, r][0].wait_send()
        m.norm_second(r)
        m.feed_up(r)
        if ring and r == 0:
            rg.gather(6, 4)
            rg.gathered(6)
        m.feed_down(r)
        pend[2, r] = swap(2, r, m.b_own.at[r], m.b_peer.at[r], m.b_peer.at[r])
    pend[6, 1][1].wait_recv()
    for r in range(R):
        pend[2, r][1].wait_recv()
        m.norm_third(r)
        m.feed_backward(r)
        if r == 1:
            m.weight_grad(m.gdl, m.hid, 4, DOWN)
            if ring:
                rg.scatter_begin(6)
        pend[1, r][0].wait_send()
        m.feed_back_up(r)
        pend[3, r] = swap(3, r, m.a_own.at[r], m.a_peer.at[r], m.a_peer.at[r])
    scatter((6, 0))
    m.weight_grad(m.slow, m.dg, 4, UP)
    if ring:
        rg.scatter_begin(5)
    else:
        gb = pltpu.make_async_copy(m.wall.at[:, :, UP:ALL], m.gb_hbm, loc.at[4])
        gb.start()
    for r in range(R):
        pend[3, r][1].wait_recv()
        m.norm_second_back(r)
        if r == 0:
            scatter((5, 0))
        m.attend_back(r)
        scatter(((6, 1), (5, 2))[r])
        pend[2, r][0].wait_send()
        m.project_back(r)
        pend[4, r] = swap(4, r, m.b_own.at[r, :, 0:H], m.b_peer.at[r, :, 0:H], m.b_peer.at[r, :, 0:H])
        pend[5, r] = swap(5, r, m.st_own.at[r], m.st_peer.at[r], m.st_peer.at[r])
        if r == 0:
            scatter((5, 1), (6, 2))
    m.weight_grad(m.gal, m.ctx, 1, OUT)
    m.weight_grad(m.flow, m.gst, 3, QKV)
    if ring:
        rg.scatter_begin(4)
        rg.scatter(6, 3)
    else:
        ga = pltpu.make_async_copy(m.wall.at[:, :, QKV:UP], m.ga_hbm, loc.at[3])
        ga.start()
    for r in range(R):
        pend[5, r][1].wait_recv()
        pend[4, r][1].wait_recv()
        m.norm_first_back(r)
        if r == 0:
            scatter((5, 3), (4, 0))
    if ring:
        m.pall[pl.ds(rg.me, 1), 0:11, :] = m.psum[0:11, own][None]
        m.pall[pl.ds(rg.me, 1), 11:12, :] = jnp.zeros((1, 1, H), F32)
        m.pall[pl.ds(rg.me, 1), 12:16, :] = m.pub[...][None]
        G(7, 0)

        def grads(q, c):
            m.conv_weight_grad(2 * q)
            rg.scatter_begin(q, True)

            @pl.when(q > 0)
            def _():
                S(q - 1, 0, True)
            return c

        def grads_in(q, c):
            m.conv_input_grad(2 * q)
            S(q, 1, True)
            return c

        def hop(j):
            def step(q, c):
                S(q, j, True)
                return c
            tiles(step, 4)

        scatter((6, 4))
        tiles(grads, 4)
        S(3, 0, True)
        scatter((4, 1), (5, 4))
        G(7, 1)
        tiles(grads_in, 4)
        scatter((4, 2))
        G(7, 2)
        hop(2)
        m.add_input_grad()
        scatter((4, 3))
        G(7, 3)
        hop(3)
        scatter((4, 4))
        G(7, 4)
        hop(4)
        rg.gathered(7)
        tot = jnp.sum(m.pall[...], axis=0)
        m.ggains[...] = tot[0:3]
        m.gbiases[...] = tot[3:11]
        for k in range(4):
            m.gupb[k * H:(k + 1) * H] = tot[12 + k]
        swap_blocks(m.xt[0], m.gcw)
        for i in range(4, 7):
            rg.scattered(i)
        for q in range(4):
            rg.scattered(q, True)
    else:
        for g in range(0, 8, 2):
            m.conv_weight_grad(g)
            m.conv_input_grad(g)
        m.add_input_grad()
        gc = pltpu.make_async_copy(m.big, m.gconv_hbm, loc.at[2])
        gc.start()
        m.pout[0:11, :] = m.psum[0:11, own]
        m.pout[11:12, :] = jnp.zeros((1, H), F32)
        m.pout[12:16, :] = m.pub[...]
        for c in (ga, gb, gc):
            c.wait()
    if ring:
        pend[7, 1][0].wait_send()
    for i, r in ((3, 0), (3, 1), (4, 0), (4, 1), (5, 0), (5, 1), (6, 0), (6, 1), (7, 0)):
        pend[i, r][0].wait_send()


def layer(ring, *args):
    vm, hb = pl.BlockSpec(memory_space=pltpu.VMEM), pl.BlockSpec(memory_space=pl.ANY)
    S = jax.ShapeDtypeStruct
    outs = [S((R, T, H), BF16), S((R, T, H), F32)]
    dma = pltpu.SemaphoreType.DMA
    scratch = dict(SCRATCH)
    if ring:
        scratch.update(RING_SCRATCH)
        outs += [S((H, H), F32), S((3, 48, H), F32), S((48, H), F32), S((48, FF), F32), S((48, FF), F32), S((FF,), F32), S((3, H), F32), S((8, H), F32)]
        in_specs, out_specs = [hb] * 2 + [vm] * 6 + [hb] * 4, [vm] * 10
        sems = [dma((8,)), dma((8, R)), dma((8, R))] + [dma((8, w)) for w in (4, 4, 3, 3, 8, 8)] + [dma((7, w)) for w in (4, 4, 3, 3, 8, 8)]
    else:
        outs += [S((16, H, H), BF16), S((16, 48, UP - QKV), BF16), S((16, 48, ALL - UP), BF16), S((16, H), F32)]
        in_specs, out_specs = [hb] * 2 + [vm] * 5 + [hb] * 3, [vm] * 2 + [hb] * 3 + [vm]
        sems = [dma((5,)), dma((8, R)), dma((8, R))]
    return pl.pallas_call(
        functools.partial(layer_kernel, ring),
        out_shape=outs,
        in_specs=in_specs,
        out_specs=out_specs,
        scratch_shapes=[pltpu.VMEM(s, d) for s, d in scratch.values()] + sems,
        compiler_params=pltpu.CompilerParams(collective_id=0, has_side_effects=True, vmem_limit_bytes=63 << 20),
        name="layer",
    )(*args)


def pass_on(*arrays):
    count = len(arrays)

    def kernel(*refs):
        ins, outs, held, sems = refs[:count], refs[count:2 * count], refs[2 * count:3 * count], refs[3 * count]
        loads = [pltpu.make_async_copy(ins[i], held[i], sems.at[0, i]) for i in range(count)]
        stores = [pltpu.make_async_copy(held[i], outs[i], sems.at[1, i]) for i in range(count)]
        for c in loads:
            c.start()
        for i in range(count):
            loads[i].wait()
            stores[i].start()
        for c in stores:
            c.wait()

    hb = pl.BlockSpec(memory_space=pl.ANY)
    return pl.pallas_call(
        kernel,
        out_shape=[jax.ShapeDtypeStruct(a.shape, a.dtype) for a in arrays],
        in_specs=[hb] * count,
        out_specs=[hb] * count,
        scratch_shapes=[pltpu.VMEM(a.shape, a.dtype) for a in arrays] + [pltpu.SemaphoreType.DMA((2, count))],
        name="pass_on",
    )(*arrays)


def taps_in(weight):
    blocks = weight.reshape(-1, 8, 48, 8, 48)
    return blocks.transpose(0, 3, 2, 1, 4).reshape(-1, 384, 384)


def taps_out(grad):
    blocks = grad.reshape(-1, 8, 48, 8, 48)
    return blocks.transpose(0, 3, 2, 1, 4).reshape(-1, 384)


def body(frames, segment_ids, live, conv_weight, qkv_weight, out_weight, up_weight, down_weight,
         up_bias, gains, biases, out_grad):
    common = (frames, out_grad, segment_ids, live, up_bias, gains, biases)
    if conv_weight.shape[0] == 384 and qkv_weight.shape[0] == 48:
        mixed, grad_in, g_conv, g_qkv, g_out, g_up, g_down, g_upb, g_gains, g_biases = pass_on(
            *layer(True, *common, conv_weight, qkv_weight.transpose(1, 0, 2), out_weight.T, up_weight, down_weight.T)
        )
        return (mixed, grad_in, g_conv, g_qkv.transpose(1, 0, 2), g_out.T, g_up, g_down.T, g_upb, g_gains, g_biases)
    theirs = lax.ppermute(out_weight.T, "mp", [(0, 1), (1, 0)])
    wa = jnp.concatenate([theirs, qkv_weight.reshape(-1, 3 * H), out_weight.T], axis=1)
    wb = jnp.concatenate([up_weight, down_weight.T], axis=1)
    convw = taps_in(lax.all_gather(conv_weight, "dp", axis=0, tiled=True))
    wa, wb = (lax.all_gather(w, "dp", axis=0, tiled=True).reshape(16, 48, -1) for w in (wa, wb))
    mixed, grad_in, g_conv, g_a, g_b, sums = layer(False, *common, convw, wa, wb)
    g_conv, g_a, g_b = (
        lax.psum_scatter(g, "dp", scatter_dimension=0, tiled=True).astype(F32)
        for g in (taps_out(g_conv), g_a.reshape(D, -1), g_b.reshape(D, -1))
    )
    sums = lax.psum(sums, "dp")
    return (
        mixed,
        grad_in,
        g_conv,
        g_a[:, : 3 * H].reshape(-1, 3, H),
        g_a[:, 3 * H :].T,
        g_b[:, :FF],
        g_b[:, FF:].T,
        sums[12:16].reshape(FF),
        sums[0:3],
        sums[3:11],
    )


def solution(mesh):
    placed = (
        P("dp", None, "mp"),
        P("dp", None),
        P("dp", None),
        P("dp", "mp"),
        P("dp", None, "mp"),
        P("mp", "dp"),
        P("dp", "mp"),
        P("mp", "dp"),
        P("mp"),
        P(None, "mp"),
        P(None, "mp"),
        P("dp", None, "mp"),
    )
    return jax.shard_map(
        body,
        mesh=mesh,
        in_specs=placed,
        out_specs=(
            P("dp", None, "mp"),
            P("dp", None, "mp"),
            P("dp", "mp"),
            P("dp", None, "mp"),
            P("mp", "dp"),
            P("dp", "mp"),
            P("mp", "dp"),
            P("mp"),
            P(None, "mp"),
            P(None, "mp"),
        ),
        check_vma=False,
    )
```

```python
import functools

import jax
import jax.numpy as jnp
from jax import lax
from jax.experimental import pallas as pl
from jax.experimental.pallas import tpu as pltpu
from jax.sharding import PartitionSpec as P

MESH = pl.DeviceIdType.MESH
F32, BF16 = jnp.float32, jnp.bfloat16
D, H, FF, HD = 768, 384, 1536, 64
R, T, L = 2, 320, 384
NB, GW, NA = 8, 48, 16
TM = 64
EPS = 1e-5
THEIRS, QKV, OUT, UP, DOWN, ALL = 0, 384, 1536, 1920, 3456, 4992
NN = (((1,), (0,)), ((), ()))
NT = (((1,), (1,)), ((), ()))
TN = (((0,), (0,)), ((), ()))

def mm(a, b, dims=NN):
    return lax.dot_general(a, b, dims, preferred_element_type=F32)

def gelu_both(v):
    p = 0.5 + 0.5 * lax.erf(v * 0.7071067811865476)
    return v * p, p + v * (0.3989422804014327 * jnp.exp(-0.5 * v * v))

def tiles(body, count=T // TM, init=0, unroll=1):
    return lax.fori_loop(0, count, body, init, unroll=unroll)

def cols(start, size=H):
    return pl.ds(pl.multiple_of(start, 128), size)


def at(i, size=TM):
    return pl.ds(pl.multiple_of(i * size, size), size)

class Mid:
    def shift_inputs(self, g):
        rows = at(g, GW)
        for r in range(R):
            xg = self.xt[r, rows, :]
            for a in range(NA):
                sh = (64 - 8 * a) % L
                v = pltpu.roll(xg, sh, axis=1) if sh else xg
                self.x16[a * GW:(a + 1) * GW, r * L:(r + 1) * L] = v.astype(BF16)

    def turn_in(self, dst, r, rows):
        dst[r] = jnp.concatenate([rows, jnp.zeros((L - T, H), F32)], axis=0).T

    def lanes(self, ref, r):
        return jnp.concatenate([ref[r:r + 1, :].astype(F32), jnp.zeros((1, L - T), F32)], axis=1)

    def turn_frames(self):
        for r in range(R):
            self.turn_in(self.xt, r, self.act[0, r, :, self.own].astype(F32))
            self.xt[r] = self.xt[r] * self.lanes(self.live, r)

    def conv_forward(self):

        def group(g, c):
            self.shift_inputs(g)
            w = self.convw[:, at(g, GW), :].reshape(NA * GW, NB * GW)
            y = mm(w, self.x16[...], TN)
            for r in range(R):
                acc = y[0:GW, r * L:(r + 1) * L]
                for b in range(1, NB):
                    acc = acc + pltpu.roll(y[b * GW:(b + 1) * GW, r * L:(r + 1) * L], L - b, axis=1)
                self.ot[r, at(g, GW), :] = acc
            return c
        tiles(group, 8)
    def conv_finish(self, r):
        v = self.ot[r].T[:T] + self.par[3:4, self.own]
        gel, dg = gelu_both(v)
        self.dconv[r] = dg
        self.gc[r, :, self.own] = gel.astype(BF16)

    def norm_first(self, r):
        def tile(i, c):
            v = self.act[0, r, at(i), :].astype(F32) + self.gc[r, at(i), :].astype(F32)
            cen = v - jnp.sum(v, axis=1, keepdims=True) * (1.0 / D)
            inv = lax.rsqrt(jnp.sum(cen * cen, axis=1, keepdims=True) * (1.0 / D) + EPS)
            xh = cen * inv
            n = xh * self.par[0:1, :] + self.par[4:5, :]
            self.xh0[r, at(i), :] = xh
            self.inv0[r, at(i), :] = inv
            self.fn[r, at(i), :] = n
            self.flow[r, at(i), :] = n.astype(BF16)
            return c
        tiles(tile)

    def wall_cols(self, start, size):
        return self.wall[:, :, cols(start, size)].reshape(D, size)

    def wall_rows(self, n, start, size):
        return self.wall[pl.ds(n * 8, 8), :, start:start + size].reshape(H, size)

    def project(self, r):
        def part(c, k):
            bias = self.par[pl.ds(5 + c // 2, 1), self.own] * ((c - 1) * (c - 1)).astype(F32)
            v = mm(self.flow[r], self.wall_cols(QKV + c * H, H)) + bias
            self.qkv[r, :, cols(c * H)] = v.astype(BF16)
            return k
        tiles(part, 3)

    def lane_masks(self):
        lane = lax.broadcasted_iota(jnp.int32, (1, 128), 1)
        return [(lane < HD).astype(F32).astype(BF16), (lane >= HD).astype(F32).astype(BF16)]

    def pair(self, ref, r, p, c=0):
        return ref[r, :, cols(p * 128 + c * H, 128)]

    def attend(self, r):
        masks = self.lane_masks()
        ids = self.lanes(self.seg, r)
        same = jnp.broadcast_to(ids, (128, L)).T[:T, 0:1] == ids[:, :T]

        def step(p, c):
            q, k, v = (self.pair(self.qkv, r, p, i) for i in range(3))
            acc = None
            for h in range(2):
                s = mm(q * masks[h], k, NT) * 0.125
                s = jnp.where(same, s, -1e30)
                w = jnp.exp(s - jnp.max(s, axis=1, keepdims=True))
                pr = (w * (1.0 / jnp.sum(w, axis=1, keepdims=True))).astype(BF16)
                self.big[r * 6 + p * 2 + h, 0:T, 0:T] = pr
                o = mm(pr, v * masks[h])
                acc = o if acc is None else acc + o
            self.ctx[r, :, cols(p * 128, 128)] = acc.astype(BF16)
            return c
        tiles(step, 3)

    def add_attended(self, r, ctx, start):
        def part(n, c):
            self.fn[r, :, cols(n * H)] += mm(ctx, self.wall_rows(n, start, H), NT)
            return c
        tiles(part, 2)

    def norm_second(self, r):
        def tile(i, c):
            v = self.fn[r, at(i), :] + self.par[7:8, :]
            cen = v - jnp.sum(v, axis=1, keepdims=True) * (1.0 / D)
            inv = lax.rsqrt(jnp.sum(cen * cen, axis=1, keepdims=True) * (1.0 / D) + EPS)
            xh = cen * inv
            n = xh * self.par[1:2, :] + self.par[8:9, :]
            self.xh1[r, at(i), :] = xh
            self.inv1[r, at(i), :] = inv
            self.sn[r, at(i), :] = n
            self.slow[r, at(i), :] = n.astype(BF16)
            return c
        tiles(tile)

    def feed_up(self, r):
        def part(n, c):
            u = mm(self.slow[r], self.wall_cols(UP + n * H, H)) + self.ub[pl.ds(n, 1), :]
            gel, dg = gelu_both(u)
            self.hid[r, :, cols(n * H)] = gel.astype(BF16)
            self.dg[r, :, cols(n * H)] = dg.astype(BF16)
            return c
        tiles(part, 4, unroll=4)

    def feed_down(self, r):
        def part(n, c):
            self.b_own[r, :, cols(n * H)] = mm(self.hid[r], self.wall_rows(n, DOWN, FF), NT).astype(BF16)
            return c
        tiles(part, 2, unroll=2)

    def add_sums(self, row, value):
        self.psum[row:row + 1, :] += value

    def norm_third(self, r):
        def tile(i, c):
            v = self.sn[r, at(i), :] + (self.b_own[r, at(i), :].astype(F32) + self.b_peer[r, at(i), :].astype(F32)) + self.par[9:10, :]
            cen = v - jnp.sum(v, axis=1, keepdims=True) * (1.0 / D)
            inv = lax.rsqrt(jnp.sum(cen * cen, axis=1, keepdims=True) * (1.0 / D) + EPS)
            xh = cen * inv
            self.mixf[...] = xh * self.par[2:3, :] + self.par[10:11, :]
            self.mixed[r, at(i), :] = self.mixf[:, self.own].astype(BF16)
            e = self.act[1, r, at(i), :].astype(F32)
            sc = e * self.par[2:3, :]
            ex = e * xh
            m1 = jnp.sum(sc, axis=1, keepdims=True) * (1.0 / D)
            m2 = jnp.sum(sc * xh, axis=1, keepdims=True) * (1.0 / D)
            g = inv * (sc - m1 - xh * m2)
            self.sn[r, at(i), :] = g
            self.gdl[r, at(i), :] = g.astype(BF16)
            sums = [jnp.sum(w, axis=0, keepdims=True) for w in (ex, e, g)]
            return tuple(x + y for x, y in zip(c, sums))
        z = jnp.zeros((1, D), F32)
        s = tiles(tile, init=(z, z, z), unroll=5)
        for row, val in zip((2, 10, 9), s):
            self.add_sums(row, val)

    def feed_backward(self, r):
        def part(n, c):
            gh = mm(self.gdl[r], self.wall_cols(DOWN + n * H, H))
            g = (gh * self.dg[r, :, cols(n * H)].astype(F32)).astype(BF16)
            self.dg[r, :, cols(n * H)] = g
            self.pub[pl.ds(n, 1), :] += jnp.sum(g.astype(F32), axis=0, keepdims=True)
            return c
        tiles(part, 4, unroll=4)

    def feed_back_up(self, r):
        def part(n, c):
            self.a_own[r, :, cols(n * H)] = mm(self.dg[r], self.wall_rows(n, UP, FF), NT).astype(BF16)
            return c
        tiles(part, 2, unroll=2)

    def weight_grad(self, src, other, count, start):
        def part(n, c):
            o = other[:, :, cols(n * H)].reshape(R * T, H)
            g = mm(src[...].reshape(R * T, D), o, TN)
            self.wall[:, :, cols(start + n * H)] = g.reshape(16, 48, H).astype(BF16)
            return c
        tiles(part, count)

    def norm_second_back(self, r):
        def tile(i, c):
            e = self.sn[r, at(i), :] + (self.a_own[r, at(i), :].astype(F32) + self.a_peer[r, at(i), :].astype(F32))
            xh = self.xh1[r, at(i), :]
            sc = e * self.par[1:2, :]
            m1 = jnp.sum(sc, axis=1, keepdims=True) * (1.0 / D)
            m2 = jnp.sum(sc * xh, axis=1, keepdims=True) * (1.0 / D)
            g = self.inv1[r, at(i), :] * (sc - m1 - xh * m2)
            self.sn[r, at(i), :] = g
            self.gal[r, at(i), :] = g.astype(BF16)
            sums = [jnp.sum(w, axis=0, keepdims=True) for w in (e * xh, e, g)]
            return tuple(x + y for x, y in zip(c, sums))
        z = jnp.zeros((1, D), F32)
        s = tiles(tile, init=(z, z, z))
        for row, val in zip((1, 8, 7), s):
            self.add_sums(row, val)

    def attend_back(self, r):
        self.gctx[r] = mm(self.gal[r], self.wall_cols(OUT, H)).astype(BF16)
        masks = self.lane_masks()

        def step(p, c):
            q, k, v = (self.pair(self.qkv, r, p, i) for i in range(3))
            go = self.pair(self.gctx, r, p)
            gq = gk = gv = None
            for h in range(2):
                gom = go * masks[h]
                gp = mm(gom, v, NT)
                pr = self.big[r * 6 + p * 2 + h, 0:T, 0:T]
                pf = pr.astype(F32)
                gs = (pf * (gp - jnp.sum(gp * pf, axis=1, keepdims=True))).astype(BF16)
                a, b, d = mm(gs, k * masks[h]), mm(gs, q * masks[h], TN), mm(pr, gom, TN)
                gq, gk, gv = (a, b, d) if gq is None else (gq + a, gk + b, gv + d)
            for i, w in enumerate((gq * 0.125, gk * 0.125, gv)):
                self.gst[r, :, cols(p * 128 + i * H, 128)] = w.astype(BF16)
            return c
        tiles(step, 3, unroll=3)
        for row, c in ((5, 0), (6, 2)):
            self.psum[row:row + 1, self.own] += jnp.sum(self.gst[r, :, c * H:(c + 1) * H].astype(F32), axis=0, keepdims=True)

    def project_back(self, r):
        po = mm(self.gst[r], self.wall_rows(1 - self.mp, QKV, 1152), NT)
        pw = mm(self.gst[r], self.wall_rows(self.mp, QKV, 1152), NT)
        self.b_own[r, :, 0:H] = po.astype(BF16)
        self.ot[r, 0:T, :] = pw
        so = po * self.par[0:1, self.oth]
        sw = pw * self.par[0:1, self.own]
        s1 = jnp.sum(so + sw, axis=1, keepdims=True)
        s2 = jnp.sum(so * self.xh0[r, :, self.oth] + sw * self.xh0[r, :, self.own], axis=1, keepdims=True)
        lane = lax.broadcasted_iota(jnp.int32, (T, 128), 1)
        st = jnp.where(lane == 0, s1, jnp.where(lane == 1, s2, 0.0))
        self.st[r] = st
        st = jnp.concatenate([st, jnp.zeros((L - T, 128), F32)], axis=0).T
        self.st_own[r] = st[0:8, :]

    def norm_first_back(self, r):
        stp = jnp.concatenate([self.st_peer[r], jnp.zeros((120, L), F32)], axis=0).T[:T]
        self.st[r] += stp
        gain = self.par[0:1, :]

        def tile(i, c):
            g1 = self.sn[r, at(i), :]
            sc1 = g1 * gain
            st = self.st[r, at(i), :]
            m1 = (jnp.sum(sc1, axis=1, keepdims=True) + st[:, 0:1]) * (1.0 / D)
            m2 = (jnp.sum(sc1 * self.xh0[r, at(i), :], axis=1, keepdims=True) + st[:, 1:2]) * (1.0 / D)
            xh = self.xh0[r, at(i), self.own]
            e = self.sn[r, at(i), self.own] + self.ot[r, at(i), :] + self.b_peer[r, at(i), 0:H].astype(F32)
            g = self.inv0[r, at(i), :] * (e * self.par[0:1, self.own] - m1 - xh * m2)
            self.gf[r, at(i), :] = g
            low = (g * self.dconv[r, at(i), :]).astype(BF16)
            lf = low.astype(F32)
            self.dconv[r, at(i), :] = lf
            sums = [jnp.sum(w, axis=0, keepdims=True) for w in (e * xh, e, lf)]
            return tuple(x + y for x, y in zip(c, sums))
        z = jnp.zeros((1, H), F32)
        s = tiles(tile, init=(z, z, z), unroll=5)
        for row, val in zip((0, 4, 3), s):
            self.psum[row:row + 1, self.own] += val
        self.turn_in(self.gt, r, self.dconv[r])

    def shift_grads(self, g):
        for r in range(R):
            gg = self.gt[r, at(g, GW), :]
            for b in range(NB):
                v = pltpu.roll(gg, b, axis=1) if b else gg
                self.g8[b * GW:(b + 1) * GW, r * L:(r + 1) * L] = v.astype(BF16)

    def conv_weight_grad(self, first):
        def group(g, c):
            self.shift_inputs(g)
            self.shift_grads(g)
            gr = mm(self.x16[...], self.g8[...], NT)
            self.big[:, at(g, GW), :] = gr.reshape(NA, GW, NB * GW).astype(BF16)
            return c
        lax.fori_loop(first, first + 2, group, 0)

    def conv_input_grad(self, first):
        def group(g, c):
            self.shift_grads(g)
            w = self.convw[:, at(g, GW), :].reshape(NA * GW, NB * GW)
            z = mm(w, self.g8[...])
            for r in range(R):
                acc = None
                for a in range(NA):
                    sh = (8 * a - 64) % L
                    v = z[a * GW:(a + 1) * GW, r * L:(r + 1) * L]
                    v = pltpu.roll(v, sh, axis=1) if sh else v
                    acc = v if acc is None else acc + v
                self.ot[r, at(g, GW), :] = acc
            return c
        lax.fori_loop(first, first + 4, group, 0)

    def add_input_grad(self):
        for r in range(R):
            self.gf[r] += (self.ot[r] * self.lanes(self.live, r)).T[:T]

    def put(self, i, t, v):
        rows = at(t, 16)
        if i == 4:
            for c in range(3):
                self.gqkv[c, rows, :] = v[:, c * H:(c + 1) * H]
            self.gout[rows, :] = v[:, 3 * H:4 * H]
        elif i == 5:
            self.gup[rows, :] = v
        else:
            self.gdown[rows, :] = v


def swap_blocks(x, buf):
    lane = lax.broadcasted_iota(jnp.int32, (GW, H), 1)
    for d in range(8):
        turned = pltpu.roll(x, GW * d, axis=1) if d else x
        for p in range(8):
            q = (p - d) % 8
            rows = turned[GW * p:GW * (p + 1), :]
            if d:
                rows = jnp.where((lane >= GW * p) & (lane < GW * (p + 1)), rows, buf[GW * q:GW * (q + 1), :])
            buf[GW * q:GW * (q + 1), :] = rows


class Ring:
    def __init__(self, n, m, sems):
        self.n, self.m = n, m
        (self.gas, self.gar, self.gbs, self.gbr, self.gss, self.gsr, self.sas, self.sar, self.sbs, self.sbr, self.sss, self.ssr) = sems
        me = lax.axis_index("dp")
        core = lax.rem(me, 2)
        chip = me // 2
        odd = lax.rem(chip, 2)
        half = chip // 2
        self.me, self.core, self.step = me, core, 1 - 2 * core
        self.pos = (1 - odd) * half + odd * (n - 1 - half)
        self.nxt = self.dev(self.step, core)
        self.prv = self.dev(-self.step, core)
        self.sib = me + self.step
        conv = lambda q: lambda d, w=m.convw: w.at[d, 96 * q:96 * (q + 1), :]
        self.views = [conv(q) for q in range(4)] + [
            lambda d: m.wall.at[d, :, 0:UP],
            lambda d: m.wall.at[d, :, UP:DOWN],
            lambda d: m.wall.at[d, :, DOWN:ALL],
            lambda d: m.pall.at[pl.ds(d, 1)],
        ]
        self.out = {}

    def dev(self, k, core):
        n = self.n
        p = lax.rem(self.pos + k + 8 * n, n)
        q = p // (n // 2)
        return 2 * ((1 - q) * 2 * p + q * (2 * (n - 1 - p) + 1)) + core

    def copy(self, src, dst, send, recv, dp):
        return pltpu.make_async_remote_copy(src, dst, send, recv, device_id={"dp": dp}, device_id_type=MESH)

    def go(self, key, copy):
        copy.start()
        self.out.setdefault(key, []).append(copy)

    def sent(self, key):
        for copy in self.out.pop(key):
            copy.wait_send()

    def gather(self, i, s):
        key = ("g", i)
        ahead = (self.gas, self.gar, self.nxt, 4, -self.step, 0)
        back = (self.gbs, self.gbr, self.prv, 3, self.step, 4)
        for send, recv, to, far, way, k in (ahead, back):
            if s > far:
                continue
            slot = self.views[i](self.dev(way * s, self.core))
            if s > 0:
                self.copy(slot, slot, send.at[i, s - 1], recv.at[i, s - 1], to).wait_recv()
            if s < far:
                self.go(key, self.copy(slot, slot, send.at[i, s], recv.at[i, s], to))
            if s > 0 or k == 0:
                self.go(key, self.copy(slot, slot, self.gss.at[i, k + s], self.gsr.at[i, k + s], self.sib))

    def gathered(self, i):
        for k, way in [(s, self.step * s) for s in range(5)] + [(4 + s, -self.step * s) for s in range(1, 4)]:
            slot = self.views[i](self.dev(way, 1 - self.core))
            self.copy(slot, slot, self.gss.at[i, k], self.gsr.at[i, k], self.sib).wait_recv()
        self.sent(("g", i))

    def grads(self, i, d, conv):
        if conv:
            return self.m.big.at[d, at(i, 96), :]
        if i == 4:
            return self.m.wall.at[d, :, QKV:UP]
        return self.views[i](d)

    def slots(self, i, conv):
        m = self.m
        if conv:
            return (lambda k: m.sbc.at[i, k]), (lambda k: m.rrc.at[i, k])
        return m.sb[i].at.__getitem__, m.rr[i].at.__getitem__

    def scatter_begin(self, i, conv=False, wait=False):
        sb, _ = self.slots(i, conv)
        for k, way in ((0, -4), (4, 3), (1, -3), (5, 2), (2, -2), (6, 1), (3, -1), (7, 0)):
            src = self.grads(i, self.dev(way * self.step, 1 - self.core), conv)
            copy = self.copy(src, sb(k), self.sss.at[i, k], self.ssr.at[i, k], self.sib)
            copy.wait_send() if wait else copy.start()

    def scatter(self, i, j, conv=False):
        sb, rr = self.slots(i, conv)
        ahead = (self.sas, self.sar, self.nxt, 4, self.step, 0)
        back = (self.sbs, self.sbr, self.prv, 3, -self.step, 4)
        if j < 4:
            for send, recv, to, far, way, k in (ahead, back):
                if j >= far:
                    continue
                terms = []
                if j > 0:
                    terms.append(rr(k + j - 1))
                    self.copy(terms[0], terms[0], send.at[i, j - 1], recv.at[i, j - 1], to).wait_recv()
                self.add(i, k + j, self.dev(way * (far - j), self.core), terms, sb(k + j), conv)
                self.copy(sb(k + j), rr(k + j), send.at[i, j], recv.at[i, j], to).start()
        else:
            terms = [rr(3), rr(6)]
            self.copy(terms[0], terms[0], self.sas.at[i, 3], self.sar.at[i, 3], self.nxt).wait_recv()
            self.copy(terms[1], terms[1], self.sbs.at[i, 2], self.sbr.at[i, 2], self.prv).wait_recv()
            self.add(i, 7, self.me, terms, None, conv)

    def scattered(self, i, conv=False):
        sb, rr = self.slots(i, conv)
        self.scatter_begin(i, conv, True)
        for send, recv, to, far, k in ((self.sas, self.sar, self.nxt, 4, 0), (self.sbs, self.sbr, self.prv, 3, 4)):
            for j in range(far):
                self.copy(sb(k + j), rr(k + j), send.at[i, j], recv.at[i, j], to).wait_send()

    def add(self, i, k, dev, terms, into, conv):
        held = self.slots(i, conv)[0](k)
        self.copy(held, held, self.sss.at[i, k], self.ssr.at[i, k], self.sib).wait_recv()
        mine = self.grads(i, dev, conv)

        def tile(t, c):
            rows = at(t, 16)
            v = mine[rows, :].astype(F32) + held[rows, :].astype(F32)
            for term in terms:
                v = v + term[rows, :].astype(F32)
            if into is not None:
                into[rows, :] = v.astype(BF16)
            elif conv:
                self.m.xt[0, at(6 * i + t, 16), :] = v
            else:
                self.m.put(i, t, v)
            return c
        tiles(tile, held.shape[0] // 16)


SCRATCH = dict(
    act=((2, R, T, D), BF16), par=((16, D), F32),
    convw=((16, H, H), BF16), wall=((16, 48, ALL), BF16),
    xt=((R, H, L), F32), ot=((R, H, L), F32), gt=((R, H, L), F32), x16=((768, R * L), BF16), g8=((H, R * L), BF16),
    gc=((R, T, D), BF16), dconv=((R, T, H), F32), xh0=((R, T, D), F32), inv0=((R, T, 1), F32), fn=((R, T, D), F32), flow=((R, T, D), BF16),
    qkv=((R, T, 1152), BF16), big=((16, H, H), BF16), ctx=((R, T, H), BF16),
    a_own=((R, T, D), BF16), a_peer=((R, T, D), BF16), b_own=((R, T, D), BF16), b_peer=((R, T, D), BF16),
    xh1=((R, T, D), F32), inv1=((R, T, 1), F32),
    hid=((R, T, FF), BF16), dg=((R, T, FF), BF16), mixf=((TM, D), F32), gdl=((R, T, D), BF16),
    gctx=((R, T, H), BF16), st=((R, T, 128), F32),
    st_own=((R, 8, L), F32), st_peer=((R, 8, L), F32), psum=((16, D), F32), pub=((4, H), F32), ub=((4, H), F32),
)
RING_SCRATCH = dict(cwv=((H, H), BF16), pall=((16, 16, H), F32), sbc=((4, 8, 96, H), BF16), rrc=((4, 7, 96, H), BF16))
for _i in range(4, 7):
    RING_SCRATCH["sb%d" % _i] = ((8, 48, FF), BF16)
    RING_SCRATCH["rr%d" % _i] = ((7, 48, FF), BF16)


RING_INS = ("frames", "ograd", "seg", "live", "upb", "gains", "biases", "cw", "qkvw", "outw", "upw", "downw")
RING_OUTS = ("mixed", "gf", "gcw", "gqkv", "gout", "gup", "gdown", "gupb", "ggains", "gbiases")
INS = ("frames", "ograd", "seg", "live", "upb", "gains", "biases", "convw_hbm", "wa_hbm", "wb_hbm")
OUTS = ("mixed", "gf", "gconv_hbm", "ga_hbm", "gb_hbm", "pout")


def layer_kernel(ring, *refs):
    m = Mid()
    names = (RING_INS + RING_OUTS + tuple(SCRATCH) + tuple(RING_SCRATCH)) if ring else (INS + OUTS + tuple(SCRATCH))
    for name, ref in zip(names, refs):
        setattr(m, name, ref)
    loc, snd, rcv = refs[len(names):len(names) + 3]
    m.slow, m.sn, m.gal, m.gst = m.gc, m.fn, m.gdl, m.qkv
    mp = lax.axis_index("mp")
    m.mp = mp
    m.own = pl.ds(pl.multiple_of(mp * H, 128), H)
    m.oth = pl.ds(pl.multiple_of((1 - mp) * H, 128), H)
    peer = {"mp": 1 - mp}
    bar = pltpu.get_barrier_semaphore()
    acts = [pltpu.make_async_copy(x, m.act.at[i, :, :, m.own], loc.at[i]) for i, x in enumerate((m.frames, m.ograd))]
    if ring:
        rg = Ring(8, m, refs[len(names) + 3:])
        m.sb, m.rr = ({i: getattr(m, "%s%d" % (w, i)) for i in range(4, 7)} for w in ("sb", "rr"))
        loads = [pltpu.make_async_copy(m.qkvw.at[c], m.wall.at[rg.me, :, QKV + c * H:QKV + (c + 1) * H], loc.at[2 + c]) for c in range(3)]
        loads += [
            pltpu.make_async_copy(m.outw, m.wall.at[rg.me, :, OUT:UP], loc.at[5]),
            pltpu.make_async_copy(m.upw, m.wall.at[rg.me, :, UP:DOWN], loc.at[6]),
            pltpu.make_async_copy(m.downw, m.wall.at[rg.me, :, DOWN:ALL], loc.at[7]),
        ]
        near = [{"dp": rg.nxt}, {"dp": rg.prv}, {"dp": rg.sib}, peer]
    else:
        loads = [
            pltpu.make_async_copy(m.convw_hbm, m.convw, loc.at[2]),
            pltpu.make_async_copy(m.wa_hbm, m.wall.at[:, :, 0:UP], loc.at[3]),
            pltpu.make_async_copy(m.wb_hbm, m.wall.at[:, :, UP:ALL], loc.at[4]),
        ]
        near = [peer]
    for d in near:
        pl.semaphore_signal(bar, inc=1, device_id=d, device_id_type=MESH)
    if ring:
        taps = pltpu.make_async_copy(m.cw, m.cwv, loc.at[8])
        taps.start()
    for c in acts + loads:
        c.start()
    m.par[0:3, m.own] = m.gains[...]
    m.par[3:11, m.own] = m.biases[...]
    m.psum[...] = jnp.zeros((16, D), F32)
    m.pub[...] = jnp.zeros((4, H), F32)
    for k in range(4):
        m.ub[k:k + 1, :] = m.upb[k * H:(k + 1) * H].reshape(1, H)
    if ring:
        taps.wait()
        swap_blocks(m.cwv[...].astype(F32), m.ot.at[0])
        m.convw[rg.me] = m.ot[0].astype(BF16)
    pl.semaphore_wait(bar, len(near))
    if ring:
        for q in range(4):
            rg.gather(q, 0)

    def swap(i, r, src, dst, land):
        c = pltpu.make_async_remote_copy(src, dst, snd.at[i, r], rcv.at[i, r], device_id=peer, device_id_type=MESH)
        c.start()
        return c, pltpu.make_async_remote_copy(land, land, snd.at[i, r], rcv.at[i, r], device_id=peer, device_id_type=MESH)

    pend = {}
    own, oth = m.own, m.oth
    if ring:
        theirs = m.wall.at[rg.me, :, THEIRS:QKV]
        pend[7, 1] = swap(7, 1, m.outw, theirs, theirs)
    pend[7, 0] = swap(7, 0, m.par.at[:, own], m.par.at[:, own], m.par.at[:, oth])
    for i in range(2):
        acts[i].wait()
        pend[6, i] = swap(6, i, m.act.at[i, :, :, own], m.act.at[i, :, :, own], m.act.at[i, :, :, oth])
    def gather(*items):
        if ring:
            for i, s in items:
                rg.gather(i, s)

    def scatter(*items):
        if ring:
            for i, s in items:
                rg.scatter(i, s)

    m.turn_frames()
    if ring:
        G, S = rg.gather, rg.scatter
        for s in range(1, 5):
            for q in range(4):
                G(q, s)
            if s == 3:
                for c in loads:
                    c.wait()
                pend[7, 1][1].wait_recv()
                G(4, 0)
        gather((4, 1), (5, 0), (6, 0))
        for q in range(4):
            rg.gathered(q)
    else:
        for c in loads:
            c.wait()
    m.conv_forward()
    gather((4, 2), (5, 1))
    for r in range(R):
        m.conv_finish(r)
        pend[0, r] = swap(0, r, m.gc.at[r, :, own], m.gc.at[r, :, own], m.gc.at[r, :, oth])
    gather((6, 1))
    pend[7, 0][1].wait_recv()
    pend[6, 0][1].wait_recv()
    pend[0, 0][1].wait_recv()
    m.norm_first(0)
    gather((4, 3))
    pend[0, 1][1].wait_recv()
    m.norm_first(1)
    gather((5, 2), (6, 2), (4, 4))
    if ring:
        rg.gathered(4)
    for r in range(R):
        m.project(r)
        m.attend(r)
        pend[1, r] = swap(1, r, m.ctx.at[r], m.a_peer.at[r, :, 0:H], m.a_peer.at[r, :, 0:H])
        m.add_attended(r, m.ctx[r], OUT)
        gather((5 + r, 3))
    gather((5, 4))
    if ring:
        rg.gathered(5)
    for r in range(R):
        pend[1, r][1].wait_recv()
        m.add_attended(r, m.a_peer[r, :, 0:H], THEIRS)
        pend[0, r][0].wait_send()
        m.norm_second(r)
        m.feed_up(r)
        if ring and r == 0:
            rg.gather(6, 4)
            rg.gathered(6)
        m.feed_down(r)
        pend[2, r] = swap(2, r, m.b_own.at[r], m.b_peer.at[r], m.b_peer.at[r])
    pend[6, 1][1].wait_recv()
    for r in range(R):
        pend[2, r][1].wait_recv()
        m.norm_third(r)
        m.feed_backward(r)
        if r == 1:
            m.weight_grad(m.gdl, m.hid, 4, DOWN)
            if ring:
                rg.scatter_begin(6)
        pend[1, r][0].wait_send()
        m.feed_back_up(r)
        pend[3, r] = swap(3, r, m.a_own.at[r], m.a_peer.at[r], m.a_peer.at[r])
    scatter((6, 0))
    m.weight_grad(m.slow, m.dg, 4, UP)
    if ring:
        rg.scatter_begin(5)
    else:
        gb = pltpu.make_async_copy(m.wall.at[:, :, UP:ALL], m.gb_hbm, loc.at[4])
        gb.start()
    for r in range(R):
        pend[3, r][1].wait_recv()
        m.norm_second_back(r)
        if r == 0:
            scatter((5, 0))
        m.attend_back(r)
        scatter(((6, 1), (5, 2))[r])
        pend[2, r][0].wait_send()
        m.project_back(r)
        pend[4, r] = swap(4, r, m.b_own.at[r, :, 0:H], m.b_peer.at[r, :, 0:H], m.b_peer.at[r, :, 0:H])
        pend[5, r] = swap(5, r, m.st_own.at[r], m.st_peer.at[r], m.st_peer.at[r])
        if r == 0:
            scatter((5, 1), (6, 2))
    m.weight_grad(m.gal, m.ctx, 1, OUT)
    m.weight_grad(m.flow, m.gst, 3, QKV)
    if ring:
        rg.scatter_begin(4)
        rg.scatter(6, 3)
    else:
        ga = pltpu.make_async_copy(m.wall.at[:, :, QKV:UP], m.ga_hbm, loc.at[3])
        ga.start()
    for r in range(R):
        pend[5, r][1].wait_recv()
        pend[4, r][1].wait_recv()
        m.norm_first_back(r)
        if r == 0:
            scatter((5, 3), (4, 0))
    if ring:
        m.pall[pl.ds(rg.me, 1), 0:11, :] = m.psum[0:11, own][None]
        m.pall[pl.ds(rg.me, 1), 11:12, :] = jnp.zeros((1, 1, H), F32)
        m.pall[pl.ds(rg.me, 1), 12:16, :] = m.pub[...][None]
        G(7, 0)

        def grads(q, c):
            m.conv_weight_grad(2 * q)
            rg.scatter_begin(q, True)

            @pl.when(q > 0)
            def _():
                S(q - 1, 0, True)

            @pl.when(q == 2)
            def _():
                S(4, 1)
            return c

        def hop(j, first=0, last=4):
            def step(q, c):
                S(q, j, True)
                return c
            lax.fori_loop(first, last, step, 0)

        tiles(grads, 4)
        S(3, 0, True)
        G(7, 1)
        hop(1, 0, 2)
        m.conv_input_grad(0)
        hop(1, 2, 4)
        scatter((4, 2))
        G(7, 2)
        hop(2, 0, 2)
        m.conv_input_grad(4)
        hop(2, 2, 4)
        scatter((4, 3))
        G(7, 3)
        m.add_input_grad()
        hop(3)
        scatter((6, 4), (5, 4), (4, 4))
        G(7, 4)
        hop(4)
        rg.gathered(7)
        tot = jnp.sum(m.pall[...], axis=0)
        m.ggains[...] = tot[0:3]
        m.gbiases[...] = tot[3:11]
        for k in range(4):
            m.gupb[k * H:(k + 1) * H] = tot[12 + k]
        swap_blocks(m.xt[0], m.gcw)
        for i in range(4, 7):
            rg.scattered(i)
        for q in range(4):
            rg.scattered(q, True)
    else:
        for g in range(0, 8, 2):
            m.conv_weight_grad(g)
            if g % 4 == 2:
                m.conv_input_grad(g - 2)
        m.add_input_grad()
        gc = pltpu.make_async_copy(m.big, m.gconv_hbm, loc.at[2])
        gc.start()
        m.pout[0:11, :] = m.psum[0:11, own]
        m.pout[11:12, :] = jnp.zeros((1, H), F32)
        m.pout[12:16, :] = m.pub[...]
        for c in (ga, gb, gc):
            c.wait()
    if ring:
        pend[7, 1][0].wait_send()
    for i, r in ((3, 0), (3, 1), (4, 0), (4, 1), (5, 0), (5, 1), (6, 0), (6, 1), (7, 0)):
        pend[i, r][0].wait_send()


def layer(ring, *args):
    vm, hb = pl.BlockSpec(memory_space=pltpu.VMEM), pl.BlockSpec(memory_space=pl.ANY)
    S = jax.ShapeDtypeStruct
    outs = [S((R, T, H), BF16), S((R, T, H), F32)]
    dma = pltpu.SemaphoreType.DMA
    scratch = dict(SCRATCH)
    if ring:
        scratch.update(RING_SCRATCH)
        outs += [S((H, H), F32), S((3, 48, H), F32), S((48, H), F32), S((48, FF), F32), S((48, FF), F32), S((FF,), F32), S((3, H), F32), S((8, H), F32)]
        in_specs, out_specs = [hb] * 2 + [vm] * 5 + [hb] * 5, [vm] * 10
        sems = [dma((9,)), dma((8, R)), dma((8, R))] + [dma((8, w)) for w in (4, 4, 3, 3, 8, 8)] + [dma((7, w)) for w in (4, 4, 3, 3, 8, 8)]
    else:
        outs += [S((16, H, H), BF16), S((16, 48, UP - QKV), BF16), S((16, 48, ALL - UP), BF16), S((16, H), F32)]
        in_specs, out_specs = [hb] * 2 + [vm] * 5 + [hb] * 3, [vm] * 2 + [hb] * 3 + [vm]
        sems = [dma((5,)), dma((8, R)), dma((8, R))]
    return pl.pallas_call(
        functools.partial(layer_kernel, ring),
        out_shape=outs,
        in_specs=in_specs,
        out_specs=out_specs,
        scratch_shapes=[pltpu.VMEM(s, d) for s, d in scratch.values()] + sems,
        compiler_params=pltpu.CompilerParams(collective_id=0, has_side_effects=True, vmem_limit_bytes=63 << 20),
        name="layer",
    )(*args)


def pass_on(*arrays):
    count = len(arrays)

    def kernel(*refs):
        ins, outs, held, sems = refs[:count], refs[count:2 * count], refs[2 * count:3 * count], refs[3 * count]
        loads = [pltpu.make_async_copy(ins[i], held[i], sems.at[0, i]) for i in range(count)]
        stores = [pltpu.make_async_copy(held[i], outs[i], sems.at[1, i]) for i in range(count)]
        for c in loads:
            c.start()
        for i in range(count):
            loads[i].wait()
            stores[i].start()
        for c in stores:
            c.wait()

    hb = pl.BlockSpec(memory_space=pl.ANY)
    return pl.pallas_call(
        kernel,
        out_shape=[jax.ShapeDtypeStruct(a.shape, a.dtype) for a in arrays],
        in_specs=[hb] * count,
        out_specs=[hb] * count,
        scratch_shapes=[pltpu.VMEM(a.shape, a.dtype) for a in arrays] + [pltpu.SemaphoreType.DMA((2, count))],
        name="pass_on",
    )(*arrays)


def taps_in(weight):
    blocks = weight.reshape(-1, 8, 48, 8, 48)
    return blocks.transpose(0, 3, 2, 1, 4).reshape(-1, 384, 384)


def taps_out(grad):
    blocks = grad.reshape(-1, 8, 48, 8, 48)
    return blocks.transpose(0, 3, 2, 1, 4).reshape(-1, 384)


def body(frames, segment_ids, live, conv_weight, qkv_weight, out_weight, up_weight, down_weight,
         up_bias, gains, biases, out_grad):
    common = (frames, out_grad, segment_ids, live, up_bias, gains, biases)
    if conv_weight.shape[0] == 384 and qkv_weight.shape[0] == 48:
        mixed, grad_in, g_conv, g_qkv, g_out, g_up, g_down, g_upb, g_gains, g_biases = pass_on(
            *layer(True, *common, conv_weight, qkv_weight.transpose(1, 0, 2), out_weight.T, up_weight, down_weight.T)
        )
        return (mixed, grad_in, g_conv, g_qkv.transpose(1, 0, 2), g_out.T, g_up, g_down.T, g_upb, g_gains, g_biases)
    theirs = lax.ppermute(out_weight.T, "mp", [(0, 1), (1, 0)])
    wa = jnp.concatenate([theirs, qkv_weight.reshape(-1, 3 * H), out_weight.T], axis=1)
    wb = jnp.concatenate([up_weight, down_weight.T], axis=1)
    convw = taps_in(lax.all_gather(conv_weight, "dp", axis=0, tiled=True))
    wa, wb = (lax.all_gather(w, "dp", axis=0, tiled=True).reshape(16, 48, -1) for w in (wa, wb))
    mixed, grad_in, g_conv, g_a, g_b, sums = layer(False, *common, convw, wa, wb)
    g_conv, g_a, g_b = (
        lax.psum_scatter(g, "dp", scatter_dimension=0, tiled=True).astype(F32)
        for g in (taps_out(g_conv), g_a.reshape(D, -1), g_b.reshape(D, -1))
    )
    sums = lax.psum(sums, "dp")
    return (
        mixed,
        grad_in,
        g_conv,
        g_a[:, : 3 * H].reshape(-1, 3, H),
        g_a[:, 3 * H :].T,
        g_b[:, :FF],
        g_b[:, FF:].T,
        sums[12:16].reshape(FF),
        sums[0:3],
        sums[3:11],
    )


def solution(mesh):
    placed = (
        P("dp", None, "mp"),
        P("dp", None),
        P("dp", None),
        P("dp", "mp"),
        P("dp", None, "mp"),
        P("mp", "dp"),
        P("dp", "mp"),
        P("mp", "dp"),
        P("mp"),
        P(None, "mp"),
        P(None, "mp"),
        P("dp", None, "mp"),
    )
    return jax.shard_map(
        body,
        mesh=mesh,
        in_specs=placed,
        out_specs=(
            P("dp", None, "mp"),
            P("dp", None, "mp"),
            P("dp", "mp"),
            P("dp", None, "mp"),
            P("mp", "dp"),
            P("dp", "mp"),
            P("mp", "dp"),
            P("mp"),
            P(None, "mp"),
            P(None, "mp"),
        ),
        check_vma=False,
    )
```

```python
import functools

import jax
import jax.numpy as jnp
from jax import lax
from jax.experimental import pallas as pl
from jax.experimental.pallas import tpu as pltpu
from jax.sharding import PartitionSpec as P

MESH = pl.DeviceIdType.MESH
F32, BF16 = jnp.float32, jnp.bfloat16
D, H, FF, HD = 768, 384, 1536, 64
R, T, L = 2, 320, 384
NB, GW, NA = 8, 48, 16
TM = 64
EPS = 1e-5
THEIRS, QKV, OUT, UP, DOWN, ALL = 0, 384, 1536, 1920, 3456, 4992
NN = (((1,), (0,)), ((), ()))
NT = (((1,), (1,)), ((), ()))
TN = (((0,), (0,)), ((), ()))

def mm(a, b, dims=NN):
    return lax.dot_general(a, b, dims, preferred_element_type=F32)

def gelu_both(v):
    p = 0.5 + 0.5 * lax.erf(v * 0.7071067811865476)
    return v * p, p + v * (0.3989422804014327 * jnp.exp(-0.5 * v * v))

def tiles(body, count=T // TM, init=0, unroll=1):
    return lax.fori_loop(0, count, body, init, unroll=unroll)

def cols(start, size=H):
    return pl.ds(pl.multiple_of(start, 128), size)


def at(i, size=TM):
    return pl.ds(pl.multiple_of(i * size, size), size)

class Mid:
    def shift_inputs(self, g):
        rows = at(g, GW)
        for r in range(R):
            xg = self.xt[r, rows, :]
            for a in range(NA):
                sh = (64 - 8 * a) % L
                v = pltpu.roll(xg, sh, axis=1) if sh else xg
                self.x16[a * GW:(a + 1) * GW, r * L:(r + 1) * L] = v.astype(BF16)

    def turn_in(self, dst, r, rows):
        dst[r] = jnp.concatenate([rows, jnp.zeros((L - T, H), F32)], axis=0).T

    def lanes(self, ref, r):
        return jnp.concatenate([ref[r:r + 1, :].astype(F32), jnp.zeros((1, L - T), F32)], axis=1)

    def turn_frames(self):
        for r in range(R):
            self.turn_in(self.xt, r, self.act[0, r, :, self.own].astype(F32))
            self.xt[r] = self.xt[r] * self.lanes(self.live, r)

    def conv_forward(self):

        def group(g, c):
            self.shift_inputs(g)
            w = self.convw[:, at(g, GW), :].reshape(NA * GW, NB * GW)
            y = mm(w, self.x16[...], TN)
            for r in range(R):
                acc = y[0:GW, r * L:(r + 1) * L]
                for b in range(1, NB):
                    acc = acc + pltpu.roll(y[b * GW:(b + 1) * GW, r * L:(r + 1) * L], L - b, axis=1)
                self.ot[r, at(g, GW), :] = acc
            return c
        tiles(group, 8)
    def conv_finish(self, r):
        v = self.ot[r].T[:T] + self.par[3:4, self.own]
        gel, dg = gelu_both(v)
        self.dconv[r] = dg
        self.gc[r, :, self.own] = gel.astype(BF16)

    def norm_first(self, r):
        def tile(i, c):
            v = self.act[0, r, at(i), :].astype(F32) + self.gc[r, at(i), :].astype(F32)
            cen = v - jnp.sum(v, axis=1, keepdims=True) * (1.0 / D)
            inv = lax.rsqrt(jnp.sum(cen * cen, axis=1, keepdims=True) * (1.0 / D) + EPS)
            xh = cen * inv
            n = xh * self.par[0:1, :] + self.par[4:5, :]
            self.xh0[r, at(i), :] = xh
            self.inv0[r, at(i), :] = inv
            self.fn[r, at(i), :] = n
            self.flow[r, at(i), :] = n.astype(BF16)
            return c
        tiles(tile)

    def wall_cols(self, start, size):
        return self.wall[:, :, cols(start, size)].reshape(D, size)

    def wall_rows(self, n, start, size):
        return self.wall[pl.ds(n * 8, 8), :, start:start + size].reshape(H, size)

    def project(self, r):
        def part(c, k):
            bias = self.par[pl.ds(5 + c // 2, 1), self.own] * ((c - 1) * (c - 1)).astype(F32)
            v = mm(self.flow[r], self.wall_cols(QKV + c * H, H)) + bias
            self.qkv[r, :, cols(c * H)] = v.astype(BF16)
            return k
        tiles(part, 3)

    def lane_masks(self):
        lane = lax.broadcasted_iota(jnp.int32, (1, 128), 1)
        return [(lane < HD).astype(F32).astype(BF16), (lane >= HD).astype(F32).astype(BF16)]

    def pair(self, ref, r, p, c=0):
        return ref[r, :, cols(p * 128 + c * H, 128)]

    def attend(self, r):
        masks = self.lane_masks()
        ids = self.lanes(self.seg, r)
        same = jnp.broadcast_to(ids, (128, L)).T[:T, 0:1] == ids[:, :T]

        def step(p, c):
            q, k, v = (self.pair(self.qkv, r, p, i) for i in range(3))
            acc = None
            for h in range(2):
                s = mm(q * masks[h], k, NT) * 0.125
                s = jnp.where(same, s, -1e30)
                w = jnp.exp(s - jnp.max(s, axis=1, keepdims=True))
                pr = (w * (1.0 / jnp.sum(w, axis=1, keepdims=True))).astype(BF16)
                self.big[r * 6 + p * 2 + h, 0:T, 0:T] = pr
                o = mm(pr, v * masks[h])
                acc = o if acc is None else acc + o
            self.ctx[r, :, cols(p * 128, 128)] = acc.astype(BF16)
            return c
        tiles(step, 3)

    def add_attended(self, r, ctx, start):
        def part(n, c):
            self.fn[r, :, cols(n * H)] += mm(ctx, self.wall_rows(n, start, H), NT)
            return c
        tiles(part, 2)

    def norm_second(self, r):
        def tile(i, c):
            v = self.fn[r, at(i), :] + self.par[7:8, :]
            cen = v - jnp.sum(v, axis=1, keepdims=True) * (1.0 / D)
            inv = lax.rsqrt(jnp.sum(cen * cen, axis=1, keepdims=True) * (1.0 / D) + EPS)
            xh = cen * inv
            n = xh * self.par[1:2, :] + self.par[8:9, :]
            self.xh1[r, at(i), :] = xh
            self.inv1[r, at(i), :] = inv
            self.sn[r, at(i), :] = n
            self.slow[r, at(i), :] = n.astype(BF16)
            return c
        tiles(tile)

    def feed_up(self, r):
        def part(n, c):
            u = mm(self.slow[r], self.wall_cols(UP + n * H, H)) + self.ub[pl.ds(n, 1), :]
            gel, dg = gelu_both(u)
            self.hid[r, :, cols(n * H)] = gel.astype(BF16)
            self.dg[r, :, cols(n * H)] = dg.astype(BF16)
            return c
        tiles(part, 4, unroll=4)

    def feed_down(self, r, n):
        self.b_own[r, :, n * H:(n + 1) * H] = mm(self.hid[r], self.wall_rows(n, DOWN, FF), NT).astype(BF16)

    def add_sums(self, row, value):
        self.psum[row:row + 1, :] += value

    def norm_third(self, r):
        def tile(i, c):
            v = self.sn[r, at(i), :] + (self.b_own[r, at(i), :].astype(F32) + self.b_peer[r, at(i), :].astype(F32)) + self.par[9:10, :]
            cen = v - jnp.sum(v, axis=1, keepdims=True) * (1.0 / D)
            inv = lax.rsqrt(jnp.sum(cen * cen, axis=1, keepdims=True) * (1.0 / D) + EPS)
            xh = cen * inv
            self.mixf[...] = xh * self.par[2:3, :] + self.par[10:11, :]
            self.mixed[r, at(i), :] = self.mixf[:, self.own].astype(BF16)
            e = self.act[1, r, at(i), :].astype(F32)
            sc = e * self.par[2:3, :]
            ex = e * xh
            m1 = jnp.sum(sc, axis=1, keepdims=True) * (1.0 / D)
            m2 = jnp.sum(sc * xh, axis=1, keepdims=True) * (1.0 / D)
            g = inv * (sc - m1 - xh * m2)
            self.sn[r, at(i), :] = g
            self.gdl[r, at(i), :] = g.astype(BF16)
            sums = [jnp.sum(w, axis=0, keepdims=True) for w in (ex, e, g)]
            return tuple(x + y for x, y in zip(c, sums))
        z = jnp.zeros((1, D), F32)
        s = tiles(tile, init=(z, z, z), unroll=5)
        for row, val in zip((2, 10, 9), s):
            self.add_sums(row, val)

    def feed_backward(self, r):
        def part(n, c):
            gh = mm(self.gdl[r], self.wall_cols(DOWN + n * H, H))
            g = (gh * self.dg[r, :, cols(n * H)].astype(F32)).astype(BF16)
            self.dg[r, :, cols(n * H)] = g
            self.pub[pl.ds(n, 1), :] += jnp.sum(g.astype(F32), axis=0, keepdims=True)
            return c
        tiles(part, 4, unroll=4)

    def feed_back_up(self, r):
        def part(n, c):
            self.a_own[r, :, cols(n * H)] = mm(self.dg[r], self.wall_rows(n, UP, FF), NT).astype(BF16)
            return c
        tiles(part, 2, unroll=2)

    def weight_grad(self, src, other, count, start):
        def part(n, c):
            o = other[:, :, cols(n * H)].reshape(R * T, H)
            g = mm(src[...].reshape(R * T, D), o, TN)
            self.wall[:, :, cols(start + n * H)] = g.reshape(16, 48, H).astype(BF16)
            return c
        tiles(part, count)

    def norm_second_back(self, r):
        def tile(i, c):
            e = self.sn[r, at(i), :] + (self.a_own[r, at(i), :].astype(F32) + self.a_peer[r, at(i), :].astype(F32))
            xh = self.xh1[r, at(i), :]
            sc = e * self.par[1:2, :]
            m1 = jnp.sum(sc, axis=1, keepdims=True) * (1.0 / D)
            m2 = jnp.sum(sc * xh, axis=1, keepdims=True) * (1.0 / D)
            g = self.inv1[r, at(i), :] * (sc - m1 - xh * m2)
            self.sn[r, at(i), :] = g
            self.gal[r, at(i), :] = g.astype(BF16)
            sums = [jnp.sum(w, axis=0, keepdims=True) for w in (e * xh, e, g)]
            return tuple(x + y for x, y in zip(c, sums))
        z = jnp.zeros((1, D), F32)
        s = tiles(tile, init=(z, z, z))
        for row, val in zip((1, 8, 7), s):
            self.add_sums(row, val)

    def attend_back(self, r):
        self.gctx[r] = mm(self.gal[r], self.wall_cols(OUT, H)).astype(BF16)
        masks = self.lane_masks()

        def step(p, c):
            q, k, v = (self.pair(self.qkv, r, p, i) for i in range(3))
            go = self.pair(self.gctx, r, p)
            gq = gk = gv = None
            for h in range(2):
                gom = go * masks[h]
                gp = mm(gom, v, NT)
                pr = self.big[r * 6 + p * 2 + h, 0:T, 0:T]
                pf = pr.astype(F32)
                gs = (pf * (gp - jnp.sum(gp * pf, axis=1, keepdims=True))).astype(BF16)
                a, b, d = mm(gs, k * masks[h]), mm(gs, q * masks[h], TN), mm(pr, gom, TN)
                gq, gk, gv = (a, b, d) if gq is None else (gq + a, gk + b, gv + d)
            for i, w in enumerate((gq * 0.125, gk * 0.125, gv)):
                self.gst[r, :, cols(p * 128 + i * H, 128)] = w.astype(BF16)
            return c
        tiles(step, 3, unroll=3)
        for row, c in ((5, 0), (6, 2)):
            self.psum[row:row + 1, self.own] += jnp.sum(self.gst[r, :, c * H:(c + 1) * H].astype(F32), axis=0, keepdims=True)

    def project_back(self, r, send):
        po = mm(self.gst[r], self.wall_rows(1 - self.mp, QKV, 1152), NT)
        self.b_own[r, :, 0:H] = po.astype(BF16)
        send()
        pw = mm(self.gst[r], self.wall_rows(self.mp, QKV, 1152), NT)
        self.ot[r, 0:T, :] = pw
        so = po * self.par[0:1, self.oth]
        sw = pw * self.par[0:1, self.own]
        s1 = jnp.sum(so + sw, axis=1, keepdims=True)
        s2 = jnp.sum(so * self.xh0[r, :, self.oth] + sw * self.xh0[r, :, self.own], axis=1, keepdims=True)
        lane = lax.broadcasted_iota(jnp.int32, (T, 128), 1)
        st = jnp.where(lane == 0, s1, jnp.where(lane == 1, s2, 0.0))
        self.st[r] = st
        st = jnp.concatenate([st, jnp.zeros((L - T, 128), F32)], axis=0).T
        self.st_own[r] = st[0:8, :]

    def norm_first_back(self, r):
        stp = jnp.concatenate([self.st_peer[r], jnp.zeros((120, L), F32)], axis=0).T[:T]
        self.st[r] += stp
        gain = self.par[0:1, :]

        def tile(i, c):
            g1 = self.sn[r, at(i), :]
            sc1 = g1 * gain
            st = self.st[r, at(i), :]
            m1 = (jnp.sum(sc1, axis=1, keepdims=True) + st[:, 0:1]) * (1.0 / D)
            m2 = (jnp.sum(sc1 * self.xh0[r, at(i), :], axis=1, keepdims=True) + st[:, 1:2]) * (1.0 / D)
            xh = self.xh0[r, at(i), self.own]
            e = self.sn[r, at(i), self.own] + self.ot[r, at(i), :] + self.b_peer[r, at(i), 0:H].astype(F32)
            g = self.inv0[r, at(i), :] * (e * self.par[0:1, self.own] - m1 - xh * m2)
            self.gf[r, at(i), :] = g
            low = (g * self.dconv[r, at(i), :]).astype(BF16)
            lf = low.astype(F32)
            self.dconv[r, at(i), :] = lf
            sums = [jnp.sum(w, axis=0, keepdims=True) for w in (e * xh, e, lf)]
            return tuple(x + y for x, y in zip(c, sums))
        z = jnp.zeros((1, H), F32)
        s = tiles(tile, init=(z, z, z), unroll=5)
        for row, val in zip((0, 4, 3), s):
            self.psum[row:row + 1, self.own] += val
        self.turn_in(self.gt, r, self.dconv[r])

    def shift_grads(self, g):
        for r in range(R):
            gg = self.gt[r, at(g, GW), :]
            for b in range(NB):
                v = pltpu.roll(gg, b, axis=1) if b else gg
                self.g8[b * GW:(b + 1) * GW, r * L:(r + 1) * L] = v.astype(BF16)

    def conv_weight_grad(self, first):
        def group(g, c):
            self.shift_inputs(g)
            self.shift_grads(g)
            gr = mm(self.x16[...], self.g8[...], NT)
            self.big[:, at(g, GW), :] = gr.reshape(NA, GW, NB * GW).astype(BF16)
            return c
        lax.fori_loop(first, first + 2, group, 0)

    def conv_input_grad(self, first):
        def group(g, c):
            self.shift_grads(g)
            w = self.convw[:, at(g, GW), :].reshape(NA * GW, NB * GW)
            z = mm(w, self.g8[...])
            for r in range(R):
                acc = None
                for a in range(NA):
                    sh = (8 * a - 64) % L
                    v = z[a * GW:(a + 1) * GW, r * L:(r + 1) * L]
                    v = pltpu.roll(v, sh, axis=1) if sh else v
                    acc = v if acc is None else acc + v
                self.ot[r, at(g, GW), :] = acc
            return c
        lax.fori_loop(first, first + 4, group, 0)

    def add_input_grad(self):
        for r in range(R):
            self.gf[r] += (self.ot[r] * self.lanes(self.live, r)).T[:T]

    def put(self, i, t, v):
        rows = at(t, 16)
        if i == 4:
            for c in range(3):
                self.gqkv[c, rows, :] = v[:, c * H:(c + 1) * H]
            self.gout[rows, :] = v[:, 3 * H:4 * H]
        elif i == 5:
            self.gup[rows, :] = v
        else:
            self.gdown[rows, :] = v


def swap_blocks(x, buf):
    lane = lax.broadcasted_iota(jnp.int32, (GW, H), 1)
    for d in range(8):
        turned = pltpu.roll(x, GW * d, axis=1) if d else x
        for p in range(8):
            q = (p - d) % 8
            rows = turned[GW * p:GW * (p + 1), :]
            if d:
                rows = jnp.where((lane >= GW * p) & (lane < GW * (p + 1)), rows, buf[GW * q:GW * (q + 1), :])
            buf[GW * q:GW * (q + 1), :] = rows


class Ring:
    def __init__(self, n, m, sems):
        self.n, self.m = n, m
        (self.gas, self.gar, self.gbs, self.gbr, self.gss, self.gsr, self.sas, self.sar, self.sbs, self.sbr, self.sss, self.ssr) = sems
        me = lax.axis_index("dp")
        core = lax.rem(me, 2)
        chip = me // 2
        odd = lax.rem(chip, 2)
        half = chip // 2
        self.me, self.core, self.step = me, core, 1 - 2 * core
        self.pos = (1 - odd) * half + odd * (n - 1 - half)
        self.nxt = self.dev(self.step, core)
        self.prv = self.dev(-self.step, core)
        self.sib = me + self.step
        conv = lambda q: lambda d, w=m.convw: w.at[d, 96 * q:96 * (q + 1), :]
        self.views = [conv(q) for q in range(4)] + [
            lambda d: m.wall.at[d, :, 0:UP],
            lambda d: m.wall.at[d, :, UP:DOWN],
            lambda d: m.wall.at[d, :, DOWN:ALL],
            lambda d: m.pall.at[pl.ds(d, 1)],
        ]
        self.out = {}

    def dev(self, k, core):
        n = self.n
        p = lax.rem(self.pos + k + 8 * n, n)
        q = p // (n // 2)
        return 2 * ((1 - q) * 2 * p + q * (2 * (n - 1 - p) + 1)) + core

    def copy(self, src, dst, send, recv, dp):
        return pltpu.make_async_remote_copy(src, dst, send, recv, device_id={"dp": dp}, device_id_type=MESH)

    def go(self, key, copy):
        copy.start()
        self.out.setdefault(key, []).append(copy)

    def sent(self, key):
        for copy in self.out.pop(key):
            copy.wait_send()

    def gather(self, i, s):
        key = ("g", i)
        ahead = (self.gas, self.gar, self.nxt, 4, -self.step, 0)
        back = (self.gbs, self.gbr, self.prv, 3, self.step, 4)
        for send, recv, to, far, way, k in (ahead, back):
            if s > far:
                continue
            slot = self.views[i](self.dev(way * s, self.core))
            if s > 0:
                self.copy(slot, slot, send.at[i, s - 1], recv.at[i, s - 1], to).wait_recv()
            if s < far:
                self.go(key, self.copy(slot, slot, send.at[i, s], recv.at[i, s], to))
            if s > 0 or k == 0:
                self.go(key, self.copy(slot, slot, self.gss.at[i, k + s], self.gsr.at[i, k + s], self.sib))

    def gathered(self, i):
        for k, way in [(s, self.step * s) for s in range(5)] + [(4 + s, -self.step * s) for s in range(1, 4)]:
            slot = self.views[i](self.dev(way, 1 - self.core))
            self.copy(slot, slot, self.gss.at[i, k], self.gsr.at[i, k], self.sib).wait_recv()
        self.sent(("g", i))

    def grads(self, i, d, conv):
        if conv:
            return self.m.big.at[d, at(i, 96), :]
        if i == 4:
            return self.m.wall.at[d, :, QKV:UP]
        return self.views[i](d)

    def slots(self, i, conv):
        m = self.m
        if conv:
            return (lambda k: m.sbc.at[i, k]), (lambda k: m.rrc.at[i, k])
        return m.sb[i].at.__getitem__, m.rr[i].at.__getitem__

    def scatter_begin(self, i, conv=False, wait=False):
        sb, _ = self.slots(i, conv)
        for k, way in ((0, -4), (4, 3), (1, -3), (5, 2), (2, -2), (6, 1), (3, -1), (7, 0)):
            src = self.grads(i, self.dev(way * self.step, 1 - self.core), conv)
            copy = self.copy(src, sb(k), self.sss.at[i, k], self.ssr.at[i, k], self.sib)
            copy.wait_send() if wait else copy.start()

    def scatter(self, i, j, conv=False):
        sb, rr = self.slots(i, conv)
        ahead = (self.sas, self.sar, self.nxt, 4, self.step, 0)
        back = (self.sbs, self.sbr, self.prv, 3, -self.step, 4)
        if j < 4:
            for send, recv, to, far, way, k in (ahead, back):
                if j >= far:
                    continue
                terms = []
                if j > 0:
                    terms.append(rr(k + j - 1))
                    self.copy(terms[0], terms[0], send.at[i, j - 1], recv.at[i, j - 1], to).wait_recv()
                self.add(i, k + j, self.dev(way * (far - j), self.core), terms, sb(k + j), conv)
                self.copy(sb(k + j), rr(k + j), send.at[i, j], recv.at[i, j], to).start()
        else:
            terms = [rr(3), rr(6)]
            self.copy(terms[0], terms[0], self.sas.at[i, 3], self.sar.at[i, 3], self.nxt).wait_recv()
            self.copy(terms[1], terms[1], self.sbs.at[i, 2], self.sbr.at[i, 2], self.prv).wait_recv()
            self.add(i, 7, self.me, terms, None, conv)

    def scattered(self, i, conv=False):
        sb, rr = self.slots(i, conv)
        self.scatter_begin(i, conv, True)
        for send, recv, to, far, k in ((self.sas, self.sar, self.nxt, 4, 0), (self.sbs, self.sbr, self.prv, 3, 4)):
            for j in range(far):
                self.copy(sb(k + j), rr(k + j), send.at[i, j], recv.at[i, j], to).wait_send()

    def add(self, i, k, dev, terms, into, conv):
        held = self.slots(i, conv)[0](k)
        self.copy(held, held, self.sss.at[i, k], self.ssr.at[i, k], self.sib).wait_recv()
        mine = self.grads(i, dev, conv)

        def tile(t, c):
            rows = at(t, 16)
            v = mine[rows, :].astype(F32) + held[rows, :].astype(F32)
            for term in terms:
                v = v + term[rows, :].astype(F32)
            if into is not None:
                into[rows, :] = v.astype(BF16)
            elif conv:
                self.m.gcw[at(6 * i + t, 16), :] = v
            else:
                self.m.put(i, t, v)
            return c
        tiles(tile, held.shape[0] // 16)


SCRATCH = dict(
    mixed=((R, T, H), BF16), gf=((R, T, H), F32),
    act=((2, R, T, D), BF16), par=((16, D), F32),
    convw=((16, H, H), BF16), wall=((16, 48, ALL), BF16),
    xt=((R, H, L), F32), ot=((R, H, L), F32), gt=((R, H, L), F32), x16=((768, R * L), BF16), g8=((H, R * L), BF16),
    gc=((R, T, D), BF16), dconv=((R, T, H), F32), xh0=((R, T, D), F32), inv0=((R, T, 1), F32), fn=((R, T, D), F32), flow=((R, T, D), BF16),
    qkv=((R, T, 1152), BF16), big=((16, H, H), BF16), ctx=((R, T, H), BF16),
    a_own=((R, T, D), BF16), a_peer=((R, T, D), BF16), b_own=((R, T, D), BF16), b_peer=((R, T, D), BF16),
    xh1=((R, T, D), F32), inv1=((R, T, 1), F32),
    hid=((R, T, FF), BF16), dg=((R, T, FF), BF16), mixf=((TM, D), F32), gdl=((R, T, D), BF16),
    gctx=((R, T, H), BF16), st=((R, T, 128), F32),
    st_own=((R, 8, L), F32), st_peer=((R, 8, L), F32), psum=((16, D), F32), pub=((4, H), F32), ub=((4, H), F32),
)
RING_SCRATCH = dict(cwv=((H, H), BF16), pall=((16, 16, H), F32), sbc=((4, 8, 96, H), BF16), rrc=((4, 7, 96, H), BF16))
for _i in range(4, 7):
    RING_SCRATCH["sb%d" % _i] = ((8, 48, FF), BF16)
    RING_SCRATCH["rr%d" % _i] = ((7, 48, FF), BF16)


RING_INS = ("frames", "ograd", "seg", "live", "upb", "gains", "biases", "cw", "qkvw", "outw", "upw", "downw")
RING_OUTS = ("mixed_hbm", "gf_hbm", "gcw", "gqkv", "gout", "gup", "gdown", "gupb", "ggains", "gbiases")
INS = ("frames", "ograd", "seg", "live", "upb", "gains", "biases", "convw_hbm", "wa_hbm", "wb_hbm")
OUTS = ("mixed_hbm", "gf_hbm", "gconv_hbm", "ga_hbm", "gb_hbm", "pout")


def layer_kernel(ring, *refs):
    m = Mid()
    names = (RING_INS + RING_OUTS + tuple(SCRATCH) + tuple(RING_SCRATCH)) if ring else (INS + OUTS + tuple(SCRATCH))
    for name, ref in zip(names, refs):
        setattr(m, name, ref)
    loc, snd, rcv = refs[len(names):len(names) + 3]
    m.slow, m.sn, m.gal, m.gst = m.gc, m.fn, m.gdl, m.qkv
    mp = lax.axis_index("mp")
    m.mp = mp
    m.own = pl.ds(pl.multiple_of(mp * H, 128), H)
    m.oth = pl.ds(pl.multiple_of((1 - mp) * H, 128), H)
    peer = {"mp": 1 - mp}
    bar = pltpu.get_barrier_semaphore()
    acts = [pltpu.make_async_copy(x, m.act.at[i, :, :, m.own], loc.at[i]) for i, x in enumerate((m.frames, m.ograd))]
    if ring:
        rg = Ring(8, m, refs[len(names) + 3:])
        m.sb, m.rr = ({i: getattr(m, "%s%d" % (w, i)) for i in range(4, 7)} for w in ("sb", "rr"))
        loads = [pltpu.make_async_copy(m.qkvw.at[c], m.wall.at[rg.me, :, QKV + c * H:QKV + (c + 1) * H], loc.at[2 + c]) for c in range(3)]
        loads += [
            pltpu.make_async_copy(m.outw, m.wall.at[rg.me, :, OUT:UP], loc.at[5]),
            pltpu.make_async_copy(m.upw, m.wall.at[rg.me, :, UP:DOWN], loc.at[6]),
            pltpu.make_async_copy(m.downw, m.wall.at[rg.me, :, DOWN:ALL], loc.at[7]),
        ]
        near = [{"dp": rg.nxt}, {"dp": rg.prv}, {"dp": rg.sib}, peer]
    else:
        loads = [
            pltpu.make_async_copy(m.convw_hbm, m.convw, loc.at[2]),
            pltpu.make_async_copy(m.wa_hbm, m.wall.at[:, :, 0:UP], loc.at[3]),
            pltpu.make_async_copy(m.wb_hbm, m.wall.at[:, :, UP:ALL], loc.at[4]),
        ]
        near = [peer]
    for d in near:
        pl.semaphore_signal(bar, inc=1, device_id=d, device_id_type=MESH)
    if ring:
        taps = pltpu.make_async_copy(m.cw, m.cwv, loc.at[8])
        taps.start()
    for c in acts + loads:
        c.start()
    m.par[0:3, m.own] = m.gains[...]
    m.par[3:11, m.own] = m.biases[...]
    m.psum[...] = jnp.zeros((16, D), F32)
    m.pub[...] = jnp.zeros((4, H), F32)
    for k in range(4):
        m.ub[k:k + 1, :] = m.upb[k * H:(k + 1) * H].reshape(1, H)
    if ring:
        taps.wait()
        swap_blocks(m.cwv[...].astype(F32), m.ot.at[0])
        m.convw[rg.me] = m.ot[0].astype(BF16)
    pl.semaphore_wait(bar, len(near))
    if ring:
        for q in range(4):
            rg.gather(q, 0)

    def swap(i, r, src, dst, land):
        c = pltpu.make_async_remote_copy(src, dst, snd.at[i, r], rcv.at[i, r], device_id=peer, device_id_type=MESH)
        c.start()
        return c, pltpu.make_async_remote_copy(land, land, snd.at[i, r], rcv.at[i, r], device_id=peer, device_id_type=MESH)

    pend = {}
    own, oth = m.own, m.oth
    if ring:
        theirs = m.wall.at[rg.me, :, THEIRS:QKV]
        pend[7, 1] = swap(7, 1, m.outw, theirs, theirs)
    pend[7, 0] = swap(7, 0, m.par.at[:, own], m.par.at[:, own], m.par.at[:, oth])
    for i in range(2):
        acts[i].wait()
        pend[6, i] = swap(6, i, m.act.at[i, :, :, own], m.act.at[i, :, :, own], m.act.at[i, :, :, oth])
    def gather(*items):
        if ring:
            for i, s in items:
                rg.gather(i, s)

    def scatter(*items):
        if ring:
            for i, s in items:
                rg.scatter(i, s)

    m.turn_frames()
    if ring:
        G, S = rg.gather, rg.scatter
        for s in range(1, 5):
            for q in range(4):
                G(q, s)
            if s == 3:
                for c in loads:
                    c.wait()
                pend[7, 1][1].wait_recv()
                G(4, 0)
        gather((4, 1), (5, 0), (6, 0))
        for q in range(4):
            rg.gathered(q)
    else:
        for c in loads:
            c.wait()
    m.conv_forward()
    gather((4, 2), (5, 1))
    for r in range(R):
        m.conv_finish(r)
        pend[0, r] = swap(0, r, m.gc.at[r, :, own], m.gc.at[r, :, own], m.gc.at[r, :, oth])
    gather((6, 1))
    pend[7, 0][1].wait_recv()
    pend[6, 0][1].wait_recv()
    pend[0, 0][1].wait_recv()
    m.norm_first(0)
    gather((4, 3))
    pend[0, 1][1].wait_recv()
    m.norm_first(1)
    gather((5, 2), (6, 2), (4, 4))
    if ring:
        rg.gathered(4)
    for r in range(R):
        m.project(r)
        m.attend(r)
        pend[1, r] = swap(1, r, m.ctx.at[r], m.a_peer.at[r, :, 0:H], m.a_peer.at[r, :, 0:H])
        m.add_attended(r, m.ctx[r], OUT)
        gather((5 + r, 3))
    gather((5, 4))
    if ring:
        rg.gathered(5)
    for r in range(R):
        pend[1, r][1].wait_recv()
        m.add_attended(r, m.a_peer[r, :, 0:H], THEIRS)
        pend[0, r][0].wait_send()
        m.norm_second(r)
        m.feed_up(r)
        if ring and r == 0:
            rg.gather(6, 4)
            rg.gathered(6)
        for n in range(2):
            half = slice(n * H, (n + 1) * H)
            m.feed_down(r, n)
            pend[(2, 8)[n], r] = swap((2, 8)[n], r, m.b_own.at[r, :, half], m.b_peer.at[r, :, half], m.b_peer.at[r, :, half])
    pend[6, 1][1].wait_recv()
    for r in range(R):
        pend[2, r][1].wait_recv()
        pend[8, r][1].wait_recv()
        m.norm_third(r)
        m.feed_backward(r)
        if r == 1:
            m.weight_grad(m.gdl, m.hid, 4, DOWN)
            if ring:
                rg.scatter_begin(6)
        pend[1, r][0].wait_send()
        m.feed_back_up(r)
        pend[3, r] = swap(3, r, m.a_own.at[r], m.a_peer.at[r], m.a_peer.at[r])
    done = [pltpu.make_async_copy(m.mixed, m.mixed_hbm, loc.at[0])]
    done[0].start()
    scatter((6, 0))
    m.weight_grad(m.slow, m.dg, 4, UP)
    if ring:
        rg.scatter_begin(5)
    else:
        gb = pltpu.make_async_copy(m.wall.at[:, :, UP:ALL], m.gb_hbm, loc.at[4])
        gb.start()
    for r in range(R):
        pend[3, r][1].wait_recv()
        m.norm_second_back(r)
        if r == 0:
            scatter((5, 0))
        m.attend_back(r)
        scatter(((6, 1), (5, 2))[r])
        pend[2, r][0].wait_send()
        pend[8, r][0].wait_send()

        def send(r=r):
            pend[4, r] = swap(4, r, m.b_own.at[r, :, 0:H], m.b_peer.at[r, :, 0:H], m.b_peer.at[r, :, 0:H])

        m.project_back(r, send)
        pend[5, r] = swap(5, r, m.st_own.at[r], m.st_peer.at[r], m.st_peer.at[r])
        if r == 0:
            scatter((5, 1), (6, 2))
    m.weight_grad(m.gal, m.ctx, 1, OUT)
    m.weight_grad(m.flow, m.gst, 3, QKV)
    if ring:
        rg.scatter_begin(4)
        rg.scatter(6, 3)
    else:
        ga = pltpu.make_async_copy(m.wall.at[:, :, QKV:UP], m.ga_hbm, loc.at[3])
        ga.start()
    for r in range(R):
        pend[5, r][1].wait_recv()
        pend[4, r][1].wait_recv()
        m.norm_first_back(r)
        if r == 0:
            scatter((5, 3), (4, 0))
    if ring:
        m.pall[pl.ds(rg.me, 1), 0:11, :] = m.psum[0:11, own][None]
        m.pall[pl.ds(rg.me, 1), 11:12, :] = jnp.zeros((1, 1, H), F32)
        m.pall[pl.ds(rg.me, 1), 12:16, :] = m.pub[...][None]
        G(7, 0)

        def grads(q, c):
            m.conv_weight_grad(2 * q)
            rg.scatter_begin(q, True)

            @pl.when(q > 0)
            def _():
                S(q - 1, 0, True)

            @pl.when(q == 2)
            def _():
                S(4, 1)
            return c

        def hop(j, first=0, last=4):
            def step(q, c):
                S(q, j, True)
                return c
            lax.fori_loop(first, last, step, 0)

        tiles(grads, 4)
        S(3, 0, True)
        G(7, 1)
        hop(1, 0, 2)
        m.conv_input_grad(0)
        hop(1, 2, 4)
        scatter((4, 2))
        G(7, 2)
        hop(2, 0, 2)
        m.conv_input_grad(4)
        hop(2, 2, 4)
        scatter((4, 3))
        G(7, 3)
        m.add_input_grad()
        done.append(pltpu.make_async_copy(m.gf, m.gf_hbm, loc.at[1]))
        done[1].start()
        hop(3)
        scatter((6, 4), (5, 4), (4, 4))
        G(7, 4)
        hop(4)
        rg.gathered(7)
        tot = jnp.sum(m.pall[...], axis=0)
        m.ggains[...] = tot[0:3]
        m.gbiases[...] = tot[3:11]
        for k in range(4):
            m.gupb[k * H:(k + 1) * H] = tot[12 + k]
        for i in range(4, 7):
            rg.scattered(i)
        for q in range(4):
            rg.scattered(q, True)
    else:
        for g in range(0, 8, 2):
            m.conv_weight_grad(g)
            if g % 4 == 2:
                m.conv_input_grad(g - 2)
        m.add_input_grad()
        done.append(pltpu.make_async_copy(m.gf, m.gf_hbm, loc.at[1]))
        done[1].start()
        gc = pltpu.make_async_copy(m.big, m.gconv_hbm, loc.at[2])
        gc.start()
        m.pout[0:11, :] = m.psum[0:11, own]
        m.pout[11:12, :] = jnp.zeros((1, H), F32)
        m.pout[12:16, :] = m.pub[...]
        for c in (ga, gb, gc):
            c.wait()
    if ring:
        pend[7, 1][0].wait_send()
    for c in done:
        c.wait()
    for i, r in ((3, 0), (3, 1), (4, 0), (4, 1), (5, 0), (5, 1), (6, 0), (6, 1), (7, 0)):
        pend[i, r][0].wait_send()


def layer(ring, *args):
    vm, hb = pl.BlockSpec(memory_space=pltpu.VMEM), pl.BlockSpec(memory_space=pl.ANY)
    S = jax.ShapeDtypeStruct
    outs = [S((R, T, H), BF16), S((R, T, H), F32)]
    dma = pltpu.SemaphoreType.DMA
    scratch = dict(SCRATCH)
    if ring:
        scratch.update(RING_SCRATCH)
        outs += [S((H, H), F32), S((3, 48, H), F32), S((48, H), F32), S((48, FF), F32), S((48, FF), F32), S((FF,), F32), S((3, H), F32), S((8, H), F32)]
        in_specs, out_specs = [hb] * 2 + [vm] * 5 + [hb] * 5, [hb] * 2 + [vm] * 8
        sems = [dma((9,)), dma((9, R)), dma((9, R))] + [dma((8, w)) for w in (4, 4, 3, 3, 8, 8)] + [dma((7, w)) for w in (4, 4, 3, 3, 8, 8)]
    else:
        outs += [S((16, H, H), BF16), S((16, 48, UP - QKV), BF16), S((16, 48, ALL - UP), BF16), S((16, H), F32)]
        in_specs, out_specs = [hb] * 2 + [vm] * 5 + [hb] * 3, [hb] * 5 + [vm]
        sems = [dma((5,)), dma((9, R)), dma((9, R))]
    return pl.pallas_call(
        functools.partial(layer_kernel, ring),
        out_shape=outs,
        in_specs=in_specs,
        out_specs=out_specs,
        scratch_shapes=[pltpu.VMEM(s, d) for s, d in scratch.values()] + sems,
        compiler_params=pltpu.CompilerParams(collective_id=0, has_side_effects=True, vmem_limit_bytes=63 << 20),
        name="layer",
    )(*args)


def pass_on(*arrays):
    count = len(arrays)

    def kernel(*refs):
        ins, outs, held, sems = refs[:count], refs[count:2 * count], refs[2 * count:3 * count], refs[3 * count + 1]
        turned = refs[3 * count]
        loads = [pltpu.make_async_copy(ins[i], held[i], sems.at[0, i]) for i in range(count)]
        stores = [pltpu.make_async_copy(turned if i == 2 else held[i], outs[i], sems.at[1, i]) for i in range(count)]
        for c in loads:
            c.start()
        for i in range(count):
            if i != 2:
                loads[i].wait()
                stores[i].start()
        loads[2].wait()
        swap_blocks(held[2][...], turned)
        stores[2].start()
        for c in stores:
            c.wait()

    hb = pl.BlockSpec(memory_space=pl.ANY)
    return pl.pallas_call(
        kernel,
        out_shape=[jax.ShapeDtypeStruct(a.shape, a.dtype) for a in arrays],
        in_specs=[hb] * count,
        out_specs=[hb] * count,
        scratch_shapes=[pltpu.VMEM(a.shape, a.dtype) for a in arrays] + [pltpu.VMEM((H, H), F32), pltpu.SemaphoreType.DMA((2, count))],
        name="pass_on",
    )(*arrays)


def taps_in(weight):
    blocks = weight.reshape(-1, 8, 48, 8, 48)
    return blocks.transpose(0, 3, 2, 1, 4).reshape(-1, 384, 384)


def taps_out(grad):
    blocks = grad.reshape(-1, 8, 48, 8, 48)
    return blocks.transpose(0, 3, 2, 1, 4).reshape(-1, 384)


def body(frames, segment_ids, live, conv_weight, qkv_weight, out_weight, up_weight, down_weight,
         up_bias, gains, biases, out_grad):
    common = (frames, out_grad, segment_ids, live, up_bias, gains, biases)
    if conv_weight.shape[0] == 384 and qkv_weight.shape[0] == 48:
        mixed, grad_in, g_conv, g_qkv, g_out, g_up, g_down, g_upb, g_gains, g_biases = pass_on(
            *layer(True, *common, conv_weight, qkv_weight.transpose(1, 0, 2), out_weight.T, up_weight, down_weight.T)
        )
        return (mixed, grad_in, g_conv, g_qkv.transpose(1, 0, 2), g_out.T, g_up, g_down.T, g_upb, g_gains, g_biases)
    theirs = lax.ppermute(out_weight.T, "mp", [(0, 1), (1, 0)])
    wa = jnp.concatenate([theirs, qkv_weight.reshape(-1, 3 * H), out_weight.T], axis=1)
    wb = jnp.concatenate([up_weight, down_weight.T], axis=1)
    convw = taps_in(lax.all_gather(conv_weight, "dp", axis=0, tiled=True))
    wa, wb = (lax.all_gather(w, "dp", axis=0, tiled=True).reshape(16, 48, -1) for w in (wa, wb))
    mixed, grad_in, g_conv, g_a, g_b, sums = layer(False, *common, convw, wa, wb)
    g_conv, g_a, g_b = (
        lax.psum_scatter(g, "dp", scatter_dimension=0, tiled=True).astype(F32)
        for g in (taps_out(g_conv), g_a.reshape(D, -1), g_b.reshape(D, -1))
    )
    sums = lax.psum(sums, "dp")
    return (
        mixed,
        grad_in,
        g_conv,
        g_a[:, : 3 * H].reshape(-1, 3, H),
        g_a[:, 3 * H :].T,
        g_b[:, :FF],
        g_b[:, FF:].T,
        sums[12:16].reshape(FF),
        sums[0:3],
        sums[3:11],
    )


def solution(mesh):
    placed = (
        P("dp", None, "mp"),
        P("dp", None),
        P("dp", None),
        P("dp", "mp"),
        P("dp", None, "mp"),
        P("mp", "dp"),
        P("dp", "mp"),
        P("mp", "dp"),
        P("mp"),
        P(None, "mp"),
        P(None, "mp"),
        P("dp", None, "mp"),
    )
    return jax.shard_map(
        body,
        mesh=mesh,
        in_specs=placed,
        out_specs=(
            P("dp", None, "mp"),
            P("dp", None, "mp"),
            P("dp", "mp"),
            P("dp", None, "mp"),
            P("mp", "dp"),
            P("dp", "mp"),
            P("mp", "dp"),
            P("mp"),
            P(None, "mp"),
            P(None, "mp"),
        ),
        check_vma=False,
    )
```
